32 devices in a mesh: section: 2 (over core), dp: 16 (over z, y, x).
Axes of the slice: x: 2, y: 2, z: 4, core: 2. Of those that a mesh axis runs over, the one named last changes fastest.
Arguments:
- inputs: bfloat16 [2, 16, 256, 1024], P(None, 'dp'), may hold values from -6 to 6
- lengths: int32 [2, 16], P(None, 'dp'), may hold values from 1 to 256, 2560 in all within a row
- out_grad: bfloat16 [2, 16, 256, 1024], P(None, 'dp'), may hold values from -6 to 6
- attn_gain: bfloat16 [2, 1024], P('section', 'dp'), may hold values from 0.5 to 1.5
- q_weight: bfloat16 [2, 1024, 512], P('section', 'dp'), may hold values from -1 to 1, as said below
- k_weight: bfloat16 [2, 1024, 512], P('section', 'dp'), may hold values from -1 to 1, as said below
- v_weight: bfloat16 [2, 1024, 1024], P('section', 'dp'), may hold values from -0.1875 to 0.1875
- rank_down: bfloat16 [2, 1024, 16], P('section', 'dp'), may hold values from -0.1875 to 0.1875
- rank_up: bfloat16 [2, 16, 512], P('section', None, 'dp'), may hold values from -1.5 to 1.5
- rank_bias: bfloat16 [2, 512], P('section', 'dp'), may hold values from -1 to 4
- gate_weight: bfloat16 [2, 1024, 1024], P('section', 'dp'), may hold values from -0.1875 to 0.1875
- group_gain: bfloat16 [2, 256], P('section', 'dp'), may hold values from 0.5 to 1.5
- out_weight: bfloat16 [2, 1024, 1024], P('section', 'dp'), may hold values from -0.25 to 0.25
- mlp_gain: bfloat16 [2, 1024], P('section', 'dp'), may hold values from 0.5 to 1.5
- ffn_gate: bfloat16 [2, 1024, 2816], P('section', 'dp'), may hold values from -0.1875 to 0.1875
- ffn_up: bfloat16 [2, 1024, 2816], P('section', 'dp'), may hold values from -0.1875 to 0.1875
- ffn_down: bfloat16 [2, 2816, 1024], P('section', 'dp'), may hold values from -0.15625 to 0.15625
Outputs:
- layer_outputs: bfloat16 [2, 2, 16, 256, 1024], P('section', None, 'dp')
- input_grads: float32 [2, 2, 16, 256, 1024], P('section', None, 'dp')
- grad_attn_gain: float32 [2, 1024], P('section', 'dp')
- grad_q_weight: float32 [2, 1024, 512], P('section', 'dp')
- grad_k_weight: float32 [2, 1024, 512], P('section', 'dp')
- grad_v_weight: float32 [2, 1024, 1024], P('section', 'dp')
- grad_rank_down: float32 [2, 1024, 16], P('section', 'dp')
- grad_rank_up: float32 [2, 16, 512], P('section', None, 'dp')
- grad_rank_bias: float32 [2, 512], P('section', 'dp')
- grad_gate_weight: float32 [2, 1024, 1024], P('section', 'dp')
- grad_group_gain: float32 [2, 256], P('section', 'dp')
- grad_out_weight: float32 [2, 1024, 1024], P('section', 'dp')
- grad_mlp_gain: float32 [2, 1024], P('section', 'dp')
- grad_ffn_gate: float32 [2, 1024, 2816], P('section', 'dp')
- grad_ffn_up: float32 [2, 1024, 2816], P('section', 'dp')
- grad_ffn_down: float32 [2, 2816, 1024], P('section', 'dp')
The draws below stay inside these ranges and needn't reach their ends.
Inputs may be any that keep to these rules, and one draw needn't show every extreme that they name: `lengths`: each row's valid tokens stand at its first positions; the rest of the row is padding. `q_weight`: entries of deviation about 1024^-0.5. `k_weight`: entries of deviation about 1024^-0.5.
All inputs are finite; a program needn't handle non-finite values. No bound on the sum of `lengths` on one device may be relied on, other than what follows from the above.
Results may differ from the reference program's by a relative error of at most 0.025.
Values may be sent and summed in bfloat16 or wider, within the bound.
No kernel may reach another device: no remote copies, remote signals or barrier semaphores. Data moves between devices by JAX's collectives and lax.ppermute only.
A program may use at most 320 MiB of HBM per device.

```python
import math
from functools import partial
import jax
import jax.numpy as jnp
import numpy as np
from jax import lax

D = 1024
VH = 256
FF = 2816
RANK = 16
SPAN = 64
SEQ = 256
MICRO = 2
ROWS = 16
KEYS = 512
VALS = 1024


def shared_projection(key):
    return jax.random.normal(key, (2, D, KEYS), jnp.float32)


def mixed_projection(common, key):
    own = jax.random.normal(key, (2, D, KEYS), jnp.float32)
    limit = 6.0 * D ** (-0.5)
    return jnp.clip((0.8 * common + 0.6 * own) * D ** (-0.5), -limit, limit).astype(jnp.bfloat16)


def draw_q_weight(key, part):
    common = shared_projection(key)
    key = jax.random.fold_in(key, 11)
    return mixed_projection(common, key)


def draw_k_weight(key, part):
    common = shared_projection(key)
    key = jax.random.fold_in(key, 12)
    return mixed_projection(common, key)


def levels(key, dims, shards, least, top_value):
    def one(dim, parts):
        heights = jax.random.uniform(jax.random.fold_in(jax.random.fold_in(key, 6), dim), (parts,), jnp.float32, least / len(shards), top_value / len(shards))
        return jnp.repeat(jnp.exp(heights), dims[dim] // parts).reshape((-1,) + (1,) * (len(dims) - dim - 1))

    factor_of = one(*shards[0])
    for cut in shards[1:]:
        factor_of = factor_of * one(*cut)
    return factor_of


def split_up(number_of, total, bound, lean):
    weights = [(1 << 20) // math.isqrt(grade ** lean) + 1 for grade in range(2, number_of + 1)]
    rest, counts = total - bound - (number_of - 1), [1] * (number_of - 1)
    while rest > 0:
        movable = [i for i in range(number_of - 1) if counts[i] < bound]
        whole, remaining = sum([weights[i] for i in movable]), rest
        for i in movable:
            more = min(bound - counts[i], max(1, remaining * weights[i] // whole), rest)
            counts[i] = counts[i] + more
            rest = rest - more
    return np.array([bound] + counts)


def uneven_parts(rng, number_of, total, reach, lean):
    if number_of == 2:
        one = jax.random.randint(rng, (), max(1, total - reach), min(reach, total - 1) + 1)
        return jnp.stack([one, total - one])
    tallies = jnp.asarray(split_up(number_of, total, reach, lean), jnp.int32)
    pairs = (number_of - 1) // 2
    giver, sink = tallies[1:1 + 2 * pairs:2], tallies[2:2 + 2 * pairs:2]
    margin = jnp.minimum(giver - 1, reach - sink)
    passed = jax.random.randint(jax.random.fold_in(rng, 1), (pairs,), 0, 1 << 20) % (margin + 1)
    tallies = tallies.at[1:1 + 2 * pairs:2].set(giver - passed).at[2:2 + 2 * pairs:2].set(sink + passed)
    return tallies[jax.random.permutation(jax.random.fold_in(rng, 2), number_of)]


def noise(stream_key, dims, scale, most, shards=(), kind=jnp.bfloat16):
    array = scale * jax.random.normal(stream_key, dims, jnp.float32)
    if shards:
        array = array * levels(stream_key, dims, shards, -0.22, 0.18)
    return jnp.clip(array, -most, most).astype(kind)


def setup_inputs(seed: int = 0) -> dict:
    arg_keys = jax.random.split(jax.random.key(seed), 18)
    inputs = noise(arg_keys[0], (MICRO, ROWS, SEQ, D), 1.0, 6.0, ((1, 16),))
    lengths = jax.vmap(lambda own: uneven_parts(own, ROWS, ROWS * SEQ * 5 // 8, SEQ, 2))(jax.random.split(arg_keys[1], MICRO)).reshape((MICRO, ROWS)).astype(jnp.int32)
    out_grad = noise(arg_keys[2], (MICRO, ROWS, SEQ, D), 1.0, 6.0, ((1, 16),))
    attn_gain = jnp.clip(1.0 + 0.1 * jax.random.normal(arg_keys[3], (2, D), jnp.float32), 0.5, 1.5).astype(jnp.bfloat16)
    q_weight = draw_q_weight(jax.random.fold_in(arg_keys[17], 71), 0)
    k_weight = draw_k_weight(jax.random.fold_in(arg_keys[17], 71), 0)
    v_weight = noise(arg_keys[6], (2, D, VALS), D ** -0.5, 0.1875, ((0, 2), (1, 16)))
    rank_down = noise(arg_keys[7], (2, D, RANK), D ** -0.5, 0.1875, ((0, 2), (1, 16)))
    rank_up = noise(arg_keys[8], (2, RANK, KEYS), RANK ** -0.5, 1.5, ((0, 2), (2, 16)))
    rank_bias = jnp.clip(-1.0 + 5.0 * jax.random.uniform(arg_keys[9], (2, KEYS), jnp.float32) ** levels(arg_keys[9], (2, KEYS), ((0, 2), (1, 16)), -0.2, 0.2), -1.0, 4.0).astype(jnp.bfloat16)
    gate_weight = noise(arg_keys[10], (2, D, VALS), D ** -0.5, 0.1875, ((0, 2), (1, 16)))
    group_gain = jnp.clip(1.0 + 0.1 * jax.random.normal(arg_keys[11], (2, VH), jnp.float32), 0.5, 1.5).astype(jnp.bfloat16)
    out_weight = noise(arg_keys[12], (2, VALS, D), (VALS // 2) ** -0.5, 0.25, ((0, 2), (1, 16)))
    mlp_gain = jnp.clip(1.0 + 0.1 * jax.random.normal(arg_keys[13], (2, D), jnp.float32), 0.5, 1.5).astype(jnp.bfloat16)
    ffn_gate = noise(arg_keys[14], (2, D, FF), D ** -0.5, 0.1875, ((0, 2), (1, 16)))
    ffn_up = noise(arg_keys[15], (2, D, FF), D ** -0.5, 0.1875, ((0, 2), (1, 16)))
    ffn_down = noise(arg_keys[16], (2, FF, D), (FF // 2) ** -0.5, 0.15625, ((0, 2), (1, 16)))
    return dict(inputs=inputs, lengths=lengths, out_grad=out_grad, attn_gain=attn_gain, q_weight=q_weight, k_weight=k_weight, v_weight=v_weight, rank_down=rank_down, rank_up=rank_up, rank_bias=rank_bias, gate_weight=gate_weight, group_gain=group_gain, out_weight=out_weight, mlp_gain=mlp_gain, ffn_gate=ffn_gate, ffn_up=ffn_up, ffn_down=ffn_down)


highest = lax.Precision.HIGHEST
gate_scale = 16.0

@jax.custom_vjp
def low(v):
    return lax.optimization_barrier(v.astype(jnp.bfloat16)).astype(jnp.float32)

@jax.custom_vjp
def low_back(v):
    return v

def low_keep(v):
    return (low(v), None)

def low_pass(kept, grad):
    return (grad,)

def back_keep(v):
    return (v, None)

def back_low(kept, grad):
    return (low(grad),)
low.defvjp(low_keep, low_pass)
low_back.defvjp(back_keep, back_low)

def rounded(value):
    return low_back(low(value))

def matmul(left, right):
    return jnp.matmul(left, right, precision=highest)

def rms_norm(value, gain, eps):
    return value * lax.rsqrt(lax.optimization_barrier(jnp.mean(value * value, axis=-1, keepdims=True)) + eps) * gain

def carry_step(carried, pieces):
    decays, update = pieces
    return (decays[..., None] * carried + update, carried)

def linear_mixer(normed, params):
    row_count, length, _ = normed.shape
    val_head = params[8].shape[0]
    head_count = params[3].shape[1] // val_head
    key_head = params[1].shape[1] // head_count
    blocks = length // SPAN
    queries = rounded(matmul(normed, params[1])).reshape(row_count, blocks, SPAN, head_count, key_head)
    key_proj = rounded(matmul(normed, params[2])).reshape(row_count, blocks, SPAN, head_count, key_head)
    values = rounded(matmul(normed, params[3])).reshape(row_count, blocks, SPAN, head_count, val_head)
    logits = matmul(matmul(normed, params[4]), params[5]) + params[6]
    log_decay = (jax.nn.log_sigmoid(logits) / gate_scale).reshape(row_count, blocks, SPAN, head_count, key_head)
    within = jnp.cumsum(log_decay, axis=2)
    span_end = within[:, :, -1:]
    scaled_q = queries * key_head ** (-0.5) * jnp.exp(within)
    scaled_k = key_proj * jnp.exp(-within)
    carried_k = key_proj * jnp.exp(span_end - within)
    scores = jnp.einsum('rnihc,rnjhc->rnhij', scaled_q, scaled_k, precision=highest)
    place = jnp.arange(SPAN).astype(jnp.int32)
    causal = place[:, None] >= place[None, :]
    scores = jnp.where(causal, scores, jnp.zeros_like(scores))
    local_out = jnp.einsum('rnhij,rnjhv->rnihv', scores, values, precision=highest)
    updates = jnp.einsum('rnjhc,rnjhv->nrhcv', carried_k, values, precision=highest)
    decays = jnp.exp(jnp.moveaxis(span_end[:, :, 0], 1, 0))
    initial = jnp.zeros((row_count, head_count, key_head, val_head), updates.dtype)
    _, states = lax.scan(jax.checkpoint(carry_step), initial, (decays, updates))
    carried_out = jnp.einsum('rnihc,nrhcv->rnihv', scaled_q, states, precision=highest)
    mixed_out = (local_out + carried_out).reshape(row_count, length, head_count, val_head)
    mixed_out = rms_norm(mixed_out, params[8], 1e-05)
    gate_pre = matmul(normed, params[7]).reshape(row_count, length, head_count, val_head)
    gated_out = rounded((mixed_out * jax.nn.silu(gate_pre)).reshape(row_count, length, head_count * val_head))
    return matmul(gated_out, params[9])

def block_forward(inputs, params, token_mask):
    normed = rounded(rms_norm(inputs, params[0], 1e-06))
    hidden = inputs + linear_mixer(normed, params)
    second = rounded(rms_norm(hidden, params[10], 1e-06))
    activated = rounded(jax.nn.silu(matmul(second, params[11])) * matmul(second, params[12]))
    return (hidden + matmul(activated, params[13])) * token_mask

def two_layers(inputs, shift, first_params, second_params, token_mask):
    middle = rounded(block_forward(inputs, first_params, token_mask)) + shift
    return (block_forward(middle, second_params, token_mask), middle)

def reference(inputs, lengths, out_grad, attn_gain, q_weight, k_weight, v_weight, rank_down, rank_up, rank_bias, gate_weight, group_gain, out_weight, mlp_gain, ffn_gate, ffn_up, ffn_down):
    weights = (attn_gain, q_weight, k_weight, v_weight, rank_down, rank_up, rank_bias, gate_weight, group_gain, out_weight, mlp_gain, ffn_gate, ffn_up, ffn_down)
    first_params = tuple((w[0].astype(jnp.float32) for w in weights))
    second_params = tuple((w[1].astype(jnp.float32) for w in weights))
    groups = MICRO * ROWS // 8
    rows_all = inputs.astype(jnp.float32).reshape(groups, 8, SEQ, D)
    lens_all = lengths.astype(jnp.int32).reshape(groups, 8)
    cot_all = out_grad.astype(jnp.float32).reshape(groups, 8, SEQ, D)
    spots = jnp.arange(SEQ).astype(jnp.int32)

    def group_step(totals, pieces):
        rows_in, lens_row, cotangent = pieces
        token_mask = (spots[None, :] < lens_row[:, None]).astype(rows_in.dtype)[..., None]
        zero_shift = jnp.zeros_like(rows_in)
        forward_fn = partial(two_layers, token_mask=token_mask)
        final_out, pullback, middle = jax.vjp(forward_fn, rows_in, zero_shift, first_params, second_params, has_aux=True)
        grad_input, grad_middle, grad_first, grad_second = pullback(cotangent)
        totals = jax.tree.map(jnp.add, totals, (grad_first, grad_second))
        return (totals, (middle.astype(jnp.bfloat16), final_out.astype(jnp.bfloat16), grad_input, grad_middle))
    start = (jax.tree.map(jnp.zeros_like, first_params), jax.tree.map(jnp.zeros_like, second_params))
    totals, stacked = lax.scan(group_step, start, (rows_all, lens_all, cot_all))
    middle_all, final_all, grad_in_all, grad_mid_all = stacked
    shape_out = (MICRO, ROWS, SEQ, D)
    layer_outputs = jnp.stack([middle_all.reshape(shape_out), final_all.reshape(shape_out)])
    input_grads = jnp.stack([grad_in_all.reshape(shape_out), grad_mid_all.reshape(shape_out)])
    grads = [jnp.stack([totals[0][index], totals[1][index]]) for index in range(14)]
    return (layer_outputs, input_grads, grads[0], grads[1], grads[2], grads[3], grads[4], grads[5], grads[6], grads[7], grads[8], grads[9], grads[10], grads[11], grads[12], grads[13])
```

```python
import jax
import jax.numpy as jnp
from jax import lax
from jax.sharding import PartitionSpec as P

SPAN = 64
BF = jnp.bfloat16
F32 = jnp.float32


class Grid:
    def __init__(self, size):
        self.fast = size == 16
        self.size = size

        def pairs(dz, dy, dx):
            return [
                (z * 4 + y * 2 + x, ((z + dz) % 4) * 4 + (y ^ dy) * 2 + (x ^ dx))
                for z in range(4)
                for y in range(2)
                for x in range(2)
            ]

        if self.fast:
            self.px = lambda v: lax.ppermute(v, "dp", pairs(0, 0, 1))
            self.py = lambda v: lax.ppermute(v, "dp", pairs(0, 1, 0))
            self.pz = lambda v: lax.ppermute(v, "dp", pairs(1, 0, 0))

    def place(self):
        i = lax.axis_index("dp")
        return i // 4, (i // 2) % 2, i % 2

    def split(self, v):
        h = (v.shape[-1] // 2 + 127) // 128 * 128
        return v[..., :h], v[..., h:]

    def xy_gather(self, blk):
        X = self.px(blk)
        Y = self.py(blk)
        D1 = self.py(self.split(X)[0])
        D2 = self.px(self.split(Y)[1])
        return (0, 0, blk), (0, 1, X), (1, 0, Y), (1, 1, jnp.concatenate([D1, D2], -1))

    def gather_z_first(self, shard):
        if not self.fast:
            return lax.all_gather(shard, "dp", axis=0, tiled=True)
        z, y, x = self.place()
        R, C = shard.shape
        out = jnp.zeros((4, 2, 2, R, C), shard.dtype)
        cur = shard
        for i in range(4):
            for yy, xx, p in self.xy_gather(cur):
                out = lax.dynamic_update_slice(
                    out, p[None, None, None], ((z - i) % 4, y ^ yy, x ^ xx, 0, 0)
                )
            if i < 3:
                cur = self.pz(cur)
        return out.reshape(16 * R, C)

    def gather_z_last(self, shard):
        if not self.fast:
            return lax.all_gather(shard, "dp", axis=0, tiled=True)
        z, y, x = self.place()
        R, C = shard.shape
        cur = jnp.zeros((2, 2, R, C), shard.dtype)
        for yy, xx, p in self.xy_gather(shard):
            cur = lax.dynamic_update_slice(cur, p[None, None], (y ^ yy, x ^ xx, 0, 0))
        out = jnp.zeros((4, 2, 2, R, C), shard.dtype)
        for i in range(4):
            out = lax.dynamic_update_slice(out, cur[None], ((z - i) % 4, 0, 0, 0, 0))
            if i < 3:
                cur = self.pz(cur)
        return out.reshape(16 * R, C)

    def relative(self, v, axis):
        if not self.fast:
            return v
        z, _, _ = self.place()
        n = v.shape[axis] // 4
        return jnp.concatenate(
            [lax.dynamic_slice_in_dim(v, ((z - 1 - i) % 4) * n, n, axis) for i in range(4)], axis
        )

    def add(self, a, b):
        return (a.astype(F32) + b.astype(F32)).astype(a.dtype)

    def xy_reduce(self, G):
        _, y, x = self.place()
        n, _, _, R, C = G.shape

        def pick(yy, xx):
            return lax.dynamic_slice(G, (0, y ^ yy, x ^ xx, 0, 0), (n, 1, 1, R, C)).reshape(n, R, C)

        d1, d2 = self.split(pick(1, 1))
        r1 = self.px(d1)
        r2 = self.py(d2)
        y1, y2 = self.split(pick(1, 0))
        x1, x2 = self.split(pick(0, 1))
        a = self.py(jnp.concatenate([self.add(y1, r1), y2], -1))
        b = self.px(jnp.concatenate([x1, self.add(x2, r2)], -1))
        return (pick(0, 0).astype(F32) + a.astype(F32) + b.astype(F32)).astype(G.dtype)

    def z_reduce(self, parts):
        v = parts[0]
        for i in range(1, 4):
            v = self.add(self.pz(v), parts[i])
        return v

    def reduce_z_last(self, G):
        if not self.fast:
            return lax.psum_scatter(G, "dp", scatter_dimension=0, tiled=True)
        R, C = G.shape[0] // 16, G.shape[1]
        G = G.reshape(4, 2, 2, R, C)
        return self.z_reduce([self.xy_reduce(G[i : i + 1])[0] for i in range(4)])

    def reduce_z_first(self, G):
        if not self.fast:
            return lax.psum_scatter(G, "dp", scatter_dimension=0, tiled=True)
        R, C = G.shape[0] // 16, G.shape[1]
        G = G.reshape(4, 2, 2, R, C)
        return self.xy_reduce(self.z_reduce([G[i] for i in range(4)])[None])[0]


def over_core(v):
    return lax.ppermute(v, "section", [(0, 1), (1, 0)])


def core_sum(v):
    v = v.astype(BF)
    return v.astype(F32) + over_core(v).astype(F32)


def mm(a, b):
    return lax.dot_general(a, b, (((1,), (0,)), ((), ())), preferred_element_type=F32)


def mm_nt(a, b):
    return lax.dot_general(a, b, (((1,), (1,)), ((), ())), preferred_element_type=F32)


def mm_tn(a, b):
    return lax.dot_general(a, b, (((0,), (0,)), ((), ())), preferred_element_type=F32)


def ein(spec, a, b):
    return jnp.einsum(spec, a.astype(BF), b.astype(BF), preferred_element_type=F32)


def mixer(q, k, v, logits, g, gain, rows):
    heads = v.shape[1] // gain.shape[0]
    blocks = q.shape[0] // rows // SPAN

    def cut(a):
        return a.astype(F32).reshape(rows, blocks, SPAN, heads, a.shape[1] // heads)

    q, k, v = cut(q), cut(k), cut(v)
    b = jnp.cumsum(cut(jax.nn.log_sigmoid(logits) / 16.0), axis=2)
    last = b[:, :, -1:]
    qs = q * q.shape[-1] ** (-0.5) * jnp.exp(b)
    ks = k * jnp.exp(-b)
    kc = k * jnp.exp(last - b)
    sc = ein("rnihc,rnjhc->rnhij", qs, ks)
    i = jnp.arange(SPAN)
    sc = jnp.where(i[:, None] >= i[None, :], sc, 0.0)
    out = ein("rnhij,rnjhv->rnihv", sc, v)
    up = ein("rnjhc,rnjhv->rnhcv", kc, v)
    dec = jnp.exp(last[:, :, 0])[..., None]
    S = jnp.zeros_like(up[:, 0])
    states = []
    for n in range(blocks):
        states.append(S)
        S = dec[:, n] * S + up[:, n]
    out = out + ein("rnihc,rnhcv->rnihv", qs, jnp.stack(states, 1))
    out = out * lax.rsqrt(jnp.mean(out * out, axis=-1, keepdims=True) + 1e-5) * gain
    return (out * jax.nn.silu(cut(g))).reshape(g.shape)


def norm_back(dn, x, r, gain):
    t = dn * gain
    dx = t * r - x * (r * r * r * jnp.mean(t * x, axis=-1, keepdims=True))
    return dx, jnp.sum(dn * x * r, axis=0)


def layer_forward(x, w, mask, rows):
    K = w["ru"].shape[1]
    V = w["WO"].shape[0]
    r1 = lax.rsqrt(jnp.mean(x * x, axis=-1, keepdims=True) + 1e-6)
    n = (x * r1 * w["ag"]).astype(BF)
    pre = mm(n, w["WA"])
    q, k = pre[:, :K].astype(BF), pre[:, K : 2 * K].astype(BF)
    v, g = pre[:, 2 * K : 2 * K + V].astype(BF), pre[:, 2 * K + V :]
    low = mm(n, w["rd"])
    logits = jnp.matmul(low, w["ru"], precision=lax.Precision.HIGHEST) + w["rb"]
    gated, mix_back = jax.vjp(lambda *a: mixer(*a, rows), q, k, v, logits, g, w["gg"])
    gated = gated.astype(BF)
    hidden = x + core_sum(mm(gated, w["WO"]))
    r2 = lax.rsqrt(jnp.mean(hidden * hidden, axis=-1, keepdims=True) + 1e-6)
    second = (hidden * r2 * w["mg"]).astype(BF)
    gu = mm(second, w["WF"])
    F = gu.shape[1] // 2
    act = (jax.nn.silu(gu[:, :F]) * gu[:, F:]).astype(BF)
    y = (hidden + core_sum(mm(act, w["WD"]))) * mask
    saved = (x, r1, n, low, logits, mix_back, gated, hidden, r2, second, gu, act)
    return y, saved


def layer_backward(dy, w, saved, grid):
    x, r1, n, low, logits, mix_back, gated, hidden, r2, second, gu, act = saved
    s = lax.axis_index("section")
    F = gu.shape[1] // 2
    da = mm_nt(dy, w["WD"]).astype(BF).astype(F32)
    gD = back_rows(mm_tn(act, dy).astype(BF), s)
    gate, up = gu[:, :F], gu[:, F:]
    sig = jax.nn.sigmoid(gate)
    dgu = jnp.concatenate([da * up * (sig * (1.0 + gate * (1.0 - sig))), da * (gate * sig)], 1).astype(BF)
    gF = mm_tn(grid.relative(second, 1), dgu).astype(BF)
    dsec = core_sum(mm_nt(dgu, w["WF"])).astype(BF).astype(F32)
    back, d_mg = norm_back(dsec, hidden, r2, w["mg"])
    dhid = dy.astype(F32) + back
    dhid_low = dhid.astype(BF)
    dgated = mm_nt(dhid_low, w["WO"]).astype(BF).astype(F32)
    gO = back_rows(mm_tn(gated, dhid_low).astype(BF), s)
    dq, dk, dv, dlogits, dg, d_gg = mix_back(dgated)
    dpre = jnp.concatenate([dq, dk, dv, dg.astype(BF)], 1)
    dlow = jnp.matmul(dlogits, w["ru"].T, precision=lax.Precision.HIGHEST)
    d_ru = mm_tn(low, dlogits)
    d_rb = jnp.sum(dlogits, axis=0)
    gA = mm_tn(grid.relative(n, 1), dpre).astype(BF)
    dn = mm_nt(dpre, w["WA"]) + mm_nt(dlow.astype(BF), w["rd"])
    dn = core_sum(dn).astype(BF).astype(F32)
    dlow = core_sum(dlow)
    d_rd = mm_tn(n, dlow.astype(BF))
    back, d_ag = norm_back(dn, x, r1, w["ag"])
    dx = dhid + back
    small = (d_ag, d_rd, d_ru, d_rb, d_gg, d_mg)
    gD = grid.relative(gD, 0)
    gAO = jnp.concatenate([gA, grid.relative(gO, 0)], 1)
    return dx, gD, gF, gAO, small


def halves(v, s):
    h = v.shape[1] // 2
    first = s == 0
    return jnp.where(first, v[:, :h], v[:, h:]), jnp.where(first, v[:, h:], v[:, :h])


def in_rows(w, s):
    h = w.shape[0] // 2
    keep = lax.dynamic_slice_in_dim(w, s * h, h, 0)
    got = over_core(lax.dynamic_slice_in_dim(w, (1 - s) * h, h, 0))
    return jnp.where(s == 0, jnp.concatenate([keep, got], 1), jnp.concatenate([got, keep], 1))


def back_rows(w, s):
    keep, give = halves(w, s)
    got = over_core(give)
    return jnp.where(s == 0, jnp.concatenate([keep, got], 0), jnp.concatenate([got, keep], 0))


def body(
    inputs,
    lengths,
    out_grad,
    attn_gain,
    q_weight,
    k_weight,
    v_weight,
    rank_down,
    rank_up,
    rank_bias,
    gate_weight,
    group_gain,
    out_weight,
    mlp_gain,
    ffn_gate,
    ffn_up,
    ffn_down,
):
    size = lax.axis_size("dp")
    grid = Grid(size)
    s = lax.axis_index("section")
    first = s == 0
    shape = inputs.shape
    rows = shape[0] * shape[1]
    length, width = shape[2], shape[3]
    tokens = rows * length
    R = q_weight.shape[1]

    wide = [q_weight[0], k_weight[0], v_weight[0], gate_weight[0], ffn_gate[0], ffn_up[0], out_weight[0]]
    both = [halves(v, s) for v in wide]
    keep = jnp.concatenate([p[0] for p in both], 1)
    give = jnp.concatenate([p[1] for p in both], 1)
    smalls = [attn_gain[0], rank_down[0], rank_up[0], rank_bias[0], group_gain[0], mlp_gain[0]]
    sizes = [v.size for v in smalls]
    small = jnp.concatenate([v.reshape(-1) for v in smalls])
    small = jnp.pad(small, (0, R * 64 - small.size)).reshape(R // 2, 128)
    keep_d, give_d = halves(ffn_down[0], s)
    got, got_d, got_small = over_core(give), over_core(give_d), over_core(small)
    shard0, shard1 = jnp.where(first, keep, got), jnp.where(first, got, keep)
    down0, down1 = jnp.where(first, keep_d, got_d), jnp.where(first, got_d, keep_d)
    both_small = jnp.where(
        first, jnp.concatenate([small, got_small], 0), jnp.concatenate([got_small, small], 0)
    )
    shard0 = jnp.concatenate([shard0, both_small], 1)

    K, V, F = q_weight.shape[2] // 2, v_weight.shape[2] // 2, ffn_gate.shape[2] // 2
    A = 2 * K + 2 * V
    wide0, col0 = grid.gather_z_first(shard0), grid.gather_z_last(down0)
    wide1, col1 = grid.gather_z_first(shard1), grid.gather_z_last(down1)

    table = wide0[:, A + 2 * F + width // 2 :].reshape(size, 2, R * 64)

    def unpack(layer):
        t = table[:, layer].astype(F32)
        parts = []
        at = 0
        for n in sizes:
            parts.append(t[:, at : at + n])
            at += n
        ag, rd, ru, rb, gg, mg = parts
        ru = jnp.moveaxis(ru.reshape(size, rank_up.shape[1], -1), 0, 1).reshape(rank_up.shape[1], -1)
        return dict(
            ag=ag.reshape(1, -1),
            rd=rd.reshape(width, -1).astype(BF),
            ru=lax.dynamic_slice_in_dim(ru, s * K, K, 1),
            rb=lax.dynamic_slice_in_dim(rb.reshape(1, -1), s * K, K, 1),
            gg=gg.reshape(-1),
            mg=mg.reshape(1, -1),
        )

    def weights(w, col, layer):
        return dict(
            unpack(layer),
            WA=w[:, :A],
            WF=w[:, A : A + 2 * F],
            WO=in_rows(w[:, A + 2 * F : A + 2 * F + width // 2], s),
            WD=in_rows(col, s),
        )

    w0, w1 = weights(wide0, col0, 0), weights(wide1, col1, 1)

    spots = jnp.arange(length)
    mask = (spots[None, :] < lengths.reshape(rows, 1)).astype(F32).reshape(tokens, 1)
    x0 = inputs.reshape(tokens, width).astype(F32)
    y0, saved0 = layer_forward(x0, w0, mask, rows)
    x1 = y0.astype(BF)
    y1, saved1 = layer_forward(x1.astype(F32), w1, mask, rows)
    layer_out = jnp.where(first, x1, y1.astype(BF)).reshape((1,) + shape)

    low_mask = mask.astype(BF)
    dx1, gD1, gF1, gAO1, small1 = layer_backward(
        out_grad.reshape(tokens, width) * low_mask, w1, saved1, grid
    )
    rD1 = grid.reduce_z_first(gD1)
    rF1 = grid.reduce_z_last(gF1)
    rAO1 = grid.reduce_z_last(gAO1)
    dx0, gD0, gF0, gAO0, small0 = layer_backward(dx1.astype(BF) * low_mask, w0, saved0, grid)
    input_out = jnp.where(first, dx0, dx1).reshape((1,) + shape)
    rD0 = grid.reduce_z_first(gD0)
    rF0 = grid.reduce_z_last(gF0)

    def flat(pair):
        return jnp.concatenate([pair[2].reshape(-1), pair[3], pair[4]])

    mine = [jnp.where(first, a, b) for a, b in zip(small0, small1)]
    other = over_core(jnp.where(first, flat(small1), flat(small0)))
    n_ru = mine[2].size
    other_ru, other_rb, other_gg = (
        other[:n_ru].reshape(mine[2].shape),
        other[n_ru : n_ru + K],
        other[n_ru + K :],
    )
    full_ru = jnp.where(
        first, jnp.concatenate([mine[2], other_ru], 1), jnp.concatenate([other_ru, mine[2]], 1)
    )
    full_rb = jnp.where(first, jnp.concatenate([mine[3], other_rb]), jnp.concatenate([other_rb, mine[3]]))
    full_gg = mine[4] + other_gg
    pieces = [
        mine[0].reshape(size, -1),
        mine[1].reshape(size, -1),
        jnp.moveaxis(full_ru.reshape(full_ru.shape[0], size, -1), 1, 0).reshape(size, -1),
        full_rb.reshape(size, -1),
        full_gg.reshape(size, -1),
        mine[5].reshape(size, -1),
    ]
    packed = jnp.concatenate(pieces, 1).astype(BF)
    packed = jnp.pad(packed, ((0, 0), (0, R * 128 - packed.shape[1]))).reshape(size * R, 128)
    rAO0 = grid.reduce_z_last(jnp.concatenate([gAO0, grid.relative(packed, 0)], 1))
    small_out = rAO0[:, A + width // 2 :].reshape(-1)
    rAO0 = rAO0[:, : A + width // 2]

    def join(a, b):
        got = over_core(jnp.where(first, b, a))
        keep = jnp.where(first, a, b)
        return jnp.where(first, keep, got), jnp.where(first, got, keep)

    AOs = join(rAO0, rAO1)
    Fs = join(rF0, rF1)
    Ds = join(rD0, rD1)

    def cols(pair, lo, hi):
        return jnp.concatenate([p[:, lo:hi] for p in pair], 1).astype(F32)[None]

    out_small = []
    at = 0
    for v in smalls:
        out_small.append(small_out[at : at + v.size].reshape(v.shape).astype(F32)[None])
        at += v.size
    return (
        layer_out,
        input_out,
        out_small[0],
        cols(AOs, 0, K),
        cols(AOs, K, 2 * K),
        cols(AOs, 2 * K, 2 * K + V),
        out_small[1],
        out_small[2],
        out_small[3],
        cols(AOs, 2 * K + V, A),
        out_small[4],
        cols(AOs, A, A + width // 2),
        out_small[5],
        cols(Fs, 0, F),
        cols(Fs, F, 2 * F),
        cols(Ds, 0, width // 2),
    )


def solution(mesh):
    rows3 = P("section", "dp", None)
    one = P("section", "dp")
    return jax.shard_map(
        body,
        mesh=mesh,
        in_specs=(
            P(None, "dp", None, None),
            P(None, "dp"),
            P(None, "dp", None, None),
            one,
            rows3,
            rows3,
            rows3,
            rows3,
            P("section", None, "dp"),
            one,
            rows3,
            one,
            rows3,
            one,
            rows3,
            rows3,
            rows3,
        ),
        out_specs=(
            P("section", None, "dp", None, None),
            P("section", None, "dp", None, None),
            one,
            rows3,
            rows3,
            rows3,
            rows3,
            P("section", None, "dp"),
            one,
            rows3,
            one,
            rows3,
            one,
            rows3,
            rows3,
            rows3,
        ),
        check_vma=False,
    )
```

```python
from functools import partial

import jax
import jax.numpy as jnp
from jax import lax
from jax.experimental import pallas as pl
from jax.experimental.pallas import tpu as pltpu
from jax.sharding import PartitionSpec as P

SPAN = 64
BF = jnp.bfloat16
F32 = jnp.float32
PARAMS = pltpu.CompilerParams(vmem_limit_bytes=40 << 20)
FULL = pltpu.CompilerParams(vmem_limit_bytes=60 << 20)
COST = pl.CostEstimate(flops=0, bytes_accessed=0, transcendentals=0)


def mm(a, b):
    return lax.dot_general(
        a.astype(BF), b.astype(BF), (((1,), (0,)), ((), ())), preferred_element_type=F32
    )


def mm_nt(a, b):
    return lax.dot_general(
        a.astype(BF), b.astype(BF), (((1,), (1,)), ((), ())), preferred_element_type=F32
    )


def mm_tn(a, b):
    return lax.dot_general(
        a.astype(BF), b.astype(BF), (((0,), (0,)), ((), ())), preferred_element_type=F32
    )


def after(value, *tokens):
    return lax.optimization_barrier((value,) + tokens)[0]


def copy_call(kernel, at, ins, in_specs, outs, out_specs, grid, params=None):
    return pl.pallas_call(
        kernel,
        grid_spec=pltpu.PrefetchScalarGridSpec(
            num_scalar_prefetch=1, grid=grid, in_specs=in_specs, out_specs=out_specs
        ),
        out_shape=[jax.ShapeDtypeStruct(o, BF) for o in outs],
        compiler_params=params or PARAMS,
        cost_estimate=COST,
    )(at, *ins)


def table_block(s, rd, ag, mg, rb, gg, ru):
    R, rank = rd.shape

    def one_hot(n, at):
        i = lax.broadcasted_iota(jnp.int32, (n, 128), 0)
        return jnp.where(i + at + 64 * s == lax.broadcasted_iota(jnp.int32, (n, 128), 1), 1.0, 0.0)

    def upright(row):
        n = row.shape[1]
        i = lax.broadcasted_iota(jnp.int32, (R, n), 0)
        return mm_nt(jnp.where(i == lax.broadcasted_iota(jnp.int32, (R, n), 1), 1.0, 0.0), row)

    out = mm(rd, one_hot(rank, 0)) + mm(upright(ru), one_hot(rank, rank + 4))
    for k, row in enumerate((ag, mg, rb, gg)):
        out = out + mm(upright(jnp.broadcast_to(row, (8, row.shape[1]))), one_hot(8, rank + k)[0:1] * (
            lax.broadcasted_iota(jnp.int32, (8, 1), 0) == 0
        ).astype(F32))
    return out.astype(BF)


def cut_kernel(groups, at_ref, *refs):
    n = sum(len(g) for g in groups)
    ins, smalls, outs = refs[:n], refs[n : n + 6], refs[n + 6 :]
    s = at_ref[3]
    k = 0
    for g, _ in enumerate(groups):
        to = 0
        for _ in groups[g]:
            h = ins[k].shape[2] // 2
            for o, half in ((2 * g, s), (2 * g + 1, 1 - s)):
                outs[o][:, to : to + h] = ins[k][0, :, pl.ds(pl.multiple_of(half * h, h), h)]
            to += h
            k += 1
        if g == 0:
            rd, ag, mg, rb, gg, ru = smalls
            table = table_block(s, rd[0], ag[...], mg[...], rb[...], gg[...], ru[0])
            outs[0][:, to:] = table
            outs[1][:, to:] = table


def cut_columns(groups, smalls, at):
    ins = [v for g in groups for v in g] + list(smalls)
    in_specs = [pl.BlockSpec(v.shape, lambda i, a, d=v.ndim: (0,) * d) for v in ins]
    outs = []
    for g, arrays in enumerate(groups):
        C = sum(v.shape[2] for v in arrays) // 2 + (128 if g == 0 else 0)
        outs += [(arrays[0].shape[1], C)] * 2
    out_specs = [pl.BlockSpec(o, lambda i, a: (0, 0)) for o in outs]
    out = copy_call(partial(cut_kernel, groups), at, ins, in_specs, outs, out_specs, (1,), FULL)
    return [(out[2 * g], out[2 * g + 1]) for g in range(len(groups))]


def join_kernel(at_ref, keep_ref, got_ref, out_ref):
    W = keep_ref.shape[1]
    s = at_ref[3]
    out_ref[:, pl.ds(pl.multiple_of(s * W, W), W)] = keep_ref[...]
    out_ref[:, pl.ds(pl.multiple_of((1 - s) * W, W), W)] = got_ref[...]


def join_columns(keep, got, at):
    H, W = keep.shape
    n = H // 4
    spec = pl.BlockSpec((n, W), lambda i, a: (i, 0))
    out = pl.BlockSpec((n, 2 * W), lambda i, a: (i, 0))
    return copy_call(join_kernel, at, [keep, got], [spec, spec], [(H, 2 * W)], [out], (4,))[0]


def pairs(dz, dy, dx):
    return [
        (z * 4 + y * 2 + x, ((z + dz) % 4) * 4 + (y ^ dy) * 2 + (x ^ dx))
        for z in range(4)
        for y in range(2)
        for x in range(2)
    ]


class Link:
    def __init__(self, step, depth=1):
        self.pairs = pairs(*step)
        self.depth = depth
        self.sent = []

    def __call__(self, v, step=None):
        if len(self.sent) >= self.depth:
            v = after(v, self.sent[-self.depth])
        self.sent.append(lax.ppermute(v, "dp", pairs(*step) if step else self.pairs))
        return self.sent[-1]


def over_core(v):
    return lax.ppermute(v, "section", [(0, 1), (1, 0)])


def core_sum(v):
    v = v.astype(BF)
    return v.astype(F32) + over_core(v).astype(F32)


def add(a, b):
    return (a.astype(F32) + b.astype(F32)).astype(BF)


def ring(pz, v):
    slabs = [v]
    for _ in range(3):
        slabs.append(pz(slabs[-1]))
    return slabs


BLOCKS = ((0, 0), (0, 1), (1, 0), (1, 1))


class Idle:
    def __getattr__(self, name):
        return lambda: None


class GatherWide:
    def __init__(self, links, shard, half):
        self.px, self.py, self.pz = links
        self.slabs, self.half = [shard], half

    def ring(self):
        self.slabs.append(self.pz(self.slabs[-1]))

    def first(self):
        h = self.half
        self.a = jnp.stack([v[:, :h] for v in self.slabs])
        self.b = jnp.stack([v[:, h:] for v in self.slabs])
        self.X1, self.Y2 = self.px(self.a), self.py(self.b)

    def second(self):
        self.X2, self.Y1 = self.px(self.b), self.py(self.a)

    def third(self):
        self.D2, self.D1 = self.px(self.Y2), self.py(self.X1)

    def parts(self):
        return [self.a, self.X1, self.Y1, self.D1], [self.b, self.X2, self.Y2, self.D2]


def plane_of(j, a):
    return (2 * a[3] + j) % 4


def slab_of(j, a):
    return (a[0] + 4 - plane_of(j, a)) % 4


def place_kernel(columns, split, n_out, at_ref, *refs):
    ins, outs = refs[:-n_out], refs[-n_out:]
    j = pl.program_id(0)
    y, x = at_ref[1], at_ref[2]

    def write(h, lo, hi, o, to):
        for b, (yy, xx) in enumerate(BLOCKS):
            outs[o][0, y ^ yy, x ^ xx, :, to : to + hi - lo] = ins[4 * h + b][0, :, lo:hi]

    for h, half in enumerate(columns):
        for lo, hi, o, to in half:
            if o == split:
                pl.when(j < 2)(partial(write, h, lo, hi, o, to))
                pl.when(j >= 2)(partial(write, h, lo, hi, o + 1, to))
            else:
                write(h, lo, hi, o, to)


def place_blocks(halves_, columns, at, split=None):
    _, R, _ = halves_[0][0].shape
    width = {}
    for half in columns:
        for lo, hi, o, to in half:
            width[o] = max(width.get(o, 0), to + hi - lo)
    if split is not None:
        width[split + 1] = width[split]
    shapes, specs = [], []
    for o in sorted(width):
        block = (1, 2, 2, R, width[o])
        if split is not None and o == split:
            shapes.append((2,) + block[1:])
            specs.append(pl.BlockSpec(block, lambda j, a: (jnp.minimum(j, 1), 0, 0, 0, 0)))
        elif split is not None and o == split + 1:
            shapes.append((2,) + block[1:])
            specs.append(pl.BlockSpec(block, lambda j, a: (jnp.maximum(j, 2) - 2, 0, 0, 0, 0)))
        else:
            shapes.append((4,) + block[1:])
            specs.append(pl.BlockSpec(block, lambda j, a: (plane_of(j, a), 0, 0, 0, 0)))
    ins = list(halves_[0]) + list(halves_[1])
    in_specs = [pl.BlockSpec((1,) + v.shape[1:], lambda j, a: (slab_of(j, a), 0, 0)) for v in ins]
    return copy_call(
        partial(place_kernel, columns, split, len(shapes)), at, ins, in_specs, shapes, specs, (4,)
    )


class GatherDown:
    def __init__(self, links, shard, at):
        self.px, self.py, self.pz = links
        self.shard, self.at = shard, at

    def sides(self):
        self.X, self.Y = self.px(self.shard), self.py(self.shard)

    def diag(self):
        R, C = self.shard.shape
        h = C // 2
        y, x = self.at[1], self.at[2]
        D2, D1 = self.px(self.Y[:, h:]), self.py(self.X[:, :h])
        out = jnp.zeros((2, 2, R, C), BF)
        for b, p, c in ((0, self.shard, 0), (1, self.X, 0), (2, self.Y, 0), (3, D1, 0), (3, D2, h)):
            yy, xx = BLOCKS[b]
            out = lax.dynamic_update_slice(out, p[None, None], (y ^ yy, x ^ xx, 0, c))
        self.slabs = [out.reshape(4 * R, C)]

    def ring(self):
        self.slabs.append(self.pz(self.slabs[-1]))


def split_kernel(at_ref, *refs):
    ins, keep, give = refs[:4], refs[4], refs[5]
    j = pl.program_id(0)
    slab = slab_of(j, at_ref)
    for i in range(4):

        @pl.when((slab == i) & (j < 2))
        def _(i=i):
            keep[0] = ins[i][...]

        @pl.when((slab == i) & (j >= 2))
        def _(i=i):
            give[0] = ins[i][...]


def split_planes(slabs, at):
    n, C = slabs[0].shape
    specs = [
        pl.BlockSpec((1, n, C), lambda j, a: (jnp.minimum(j, 1), 0, 0)),
        pl.BlockSpec((1, n, C), lambda j, a: (jnp.maximum(j, 2) - 2, 0, 0)),
    ]
    whole = pl.BlockSpec((n, C), lambda j, a: (0, 0))
    out = copy_call(split_kernel, at, slabs, [whole] * 4, [(2, n, C)] * 2, specs, (4,))
    return out[0].reshape(2 * n, C), out[1].reshape(2 * n, C)


def grad_kernel(half, R, at_ref, lhs_ref, rhs_ref, *refs):
    acc = refs[-1]
    extras, outs = refs[:-9], refs[-9:-1]
    C = rhs_ref.shape[1]
    acc[:, :C] = mm_tn(lhs_ref[...], rhs_ref[...])
    i = pl.program_id(0)
    z, y, x, s = at_ref[0], at_ref[1], at_ref[2], at_ref[3]
    if extras:
        d = (z + 3 - i) % 4
        keep, got = extras[0][...].astype(F32), extras[1][...].astype(F32)
        W = keep.shape[1]
        acc[:, C : C + W] = jnp.where((d // 2) == s, keep, got)
        if len(extras) > 2:
            acc[:, C + W :] = extras[2][...].astype(F32)
    for b, (yy, xx) in enumerate(BLOCKS):
        rows = pl.ds(pl.multiple_of(((y ^ yy) * 2 + (x ^ xx)) * R, R), R)
        outs[2 * b][0] = acc[rows, :half].astype(BF)
        outs[2 * b + 1][0] = acc[rows, half:].astype(BF)


def grad_blocks(lhs, rhs, half, at, extras=()):
    tokens, D = lhs.shape
    C = rhs.shape[1]
    E = sum(e.shape[1] for e in extras[:1] + extras[2:])
    n = D // 4
    R = n // 4

    def plane(i, a):
        return (a[0] + 3 - i) % 4

    in_specs = [
        pl.BlockSpec((tokens, n), lambda i, a: (0, plane(i, a))),
        pl.BlockSpec((tokens, C), lambda i, a: (0, 0)),
    ]
    for k, e in enumerate(extras):
        if k < 2:
            in_specs.append(pl.BlockSpec((n, e.shape[1]), lambda i, a: (plane(i, a) % 2, 0)))
        else:
            in_specs.append(pl.BlockSpec((n, e.shape[1]), lambda i, a: (plane(i, a), 0)))
    widths = (half, C + E - half)
    return pl.pallas_call(
        partial(grad_kernel, half, R),
        grid_spec=pltpu.PrefetchScalarGridSpec(
            num_scalar_prefetch=1,
            grid=(4,),
            in_specs=in_specs,
            out_specs=[pl.BlockSpec((1, R, widths[k % 2]), lambda i, a: (i, 0, 0)) for k in range(8)],
            scratch_shapes=[pltpu.VMEM((n, C + E), F32)],
        ),
        out_shape=[jax.ShapeDtypeStruct((4, R, widths[k % 2]), BF) for k in range(8)],
        compiler_params=PARAMS,
        cost_estimate=COST,
    )(at, lhs, rhs, *extras)


def slab_kernel(o1, o2, x1, x2, y1, y2, out):
    h = o1.shape[2]
    out[0, :, :h] = (o1[0].astype(F32) + x1[0].astype(F32) + y1[0].astype(F32)).astype(BF)
    out[0, :, h:] = (o2[0].astype(F32) + x2[0].astype(F32) + y2[0].astype(F32)).astype(BF)


def slabs_kernel(n, *refs):
    ins, outs = refs[:-4], refs[-4:]
    i = pl.program_id(0)
    for k in range(4):

        @pl.when(i == k)
        def _(k=k):
            to = 0
            for p in range(0, len(ins), n):
                w = ins[p].shape[2]
                total = ins[p][0].astype(F32)
                for v in ins[p + 1 : p + n]:
                    total = total + v[0].astype(F32)
                outs[k][:, to : to + w] = total.astype(BF)
                to += w


def sum_slabs(*groups):
    n = len(groups[0])
    ins = [v for g in groups for v in g]
    R = ins[0].shape[1]
    C = sum(g[0].shape[2] for g in groups)
    return pl.pallas_call(
        partial(slabs_kernel, n),
        grid=(4,),
        in_specs=[pl.BlockSpec((1,) + v.shape[1:], lambda i: (i, 0, 0)) for v in ins],
        out_specs=[pl.BlockSpec((R, C), lambda i: (0, 0))] * 4,
        out_shape=[jax.ShapeDtypeStruct((R, C), BF)] * 4,
        compiler_params=PARAMS,
    )(*ins)


def total(*parts):
    t = parts[0].astype(F32)
    for v in parts[1:]:
        t = t + v.astype(F32)
    return t.astype(BF)


class ReduceWide:
    def __init__(self, links, blocks):
        self.px, self.py, self.pz = links
        self.o1, self.o2, self.X1, self.X2, self.Y1, self.Y2, self.D1, self.D2 = blocks

    def diag(self):
        self.r1, self.r2 = self.px(self.D1), self.py(self.D2)

    def sides(self):
        self.a1, self.b2 = self.px(self.X1), self.py(self.Y2)

    def rest(self):
        self.a2, self.b1 = self.px(add(self.X2, self.r2)), self.py(add(self.Y1, self.r1))

    def ring(self):
        if not hasattr(self, "slabs"):
            _, R, h = self.o1.shape
            C = h + self.o2.shape[2]
            spec1 = pl.BlockSpec((1, R, h), lambda i: (i, 0, 0))
            spec2 = pl.BlockSpec((1, R, C - h), lambda i: (i, 0, 0))
            self.slabs = pl.pallas_call(
                slab_kernel,
                grid=(4,),
                in_specs=[spec1, spec2] * 3,
                out_specs=pl.BlockSpec((1, R, C), lambda i: (i, 0, 0)),
                out_shape=jax.ShapeDtypeStruct((4, R, C), BF),
            )(self.o1, self.o2, self.a1, self.a2, self.b1, self.b2)
            self.sum, self.at = self.slabs[0], 0
        self.at += 1
        self.sum = add(self.pz(self.sum), self.slabs[self.at])

    def along(self):
        a, b, c, d = sum_slabs((self.o1, self.a1, self.b1), (self.o2, self.a2, self.b2))
        self.sum = total(d, *[self.pz(v, (up, 0, 0)) for v, up in ((a, 3), (b, 2), (c, 1))])


class ReduceDown:
    def __init__(self, links, keep, got, at):
        self.px, self.py, self.pz = links
        self.keep, self.got, self.at, self.step = keep, got, at, 0

    def plane(self):
        n = self.keep.shape[0] // 2
        d = (self.at[0] + 3 - self.step) % 4
        self.step += 1
        a = lax.dynamic_slice_in_dim(self.keep, (d % 2) * n, n, 0)
        b = lax.dynamic_slice_in_dim(self.got, (d % 2) * n, n, 0)
        return jnp.where((d // 2) == self.at[3], a, b)

    def ring(self):
        if self.step == 0:
            self.sum = self.plane()
        self.sum = add(self.pz(self.sum), self.plane())

    def pick(self, b, lo, hi):
        yy, xx = BLOCKS[b]
        R = self.sum.shape[0] // 4
        v = self.sum.reshape(2, 2, R, -1)
        y, x = self.at[1], self.at[2]
        return lax.dynamic_slice(v, (y ^ yy, x ^ xx, 0, lo), (1, 1, R, hi - lo)).reshape(R, hi - lo)

    def diag(self):
        C = self.sum.shape[1]
        h = C // 2
        self.r1, self.r2 = self.px(self.pick(3, 0, h)), self.py(self.pick(3, h, C))

    def sides(self):
        C = self.sum.shape[1]
        h = C // 2
        self.a1, self.b2 = self.px(self.pick(1, 0, h)), self.py(self.pick(2, h, C))

    def rest(self):
        C = self.sum.shape[1]
        h = C // 2
        a2 = self.px(add(self.pick(1, h, C), self.r2))
        b1 = self.py(add(self.pick(2, 0, h), self.r1))
        first = add(add(self.pick(0, 0, h), self.a1), b1)
        second = add(add(self.pick(0, h, C), a2), self.b2)
        self.sum = jnp.concatenate([first, second], 1)


def finish_kernel(widths, at_ref, keep_ref, got_ref, *outs):
    s = at_ref[3]
    to = 0
    for w, out in zip(widths, outs):
        out[0, :, pl.ds(pl.multiple_of(s * w, w), w)] = keep_ref[:, to : to + w].astype(F32)
        out[0, :, pl.ds(pl.multiple_of((1 - s) * w, w), w)] = got_ref[:, to : to + w].astype(F32)
        to += w


def finish(keep, got, widths, at):
    R = keep.shape[0]
    return pl.pallas_call(
        partial(finish_kernel, widths),
        grid_spec=pltpu.PrefetchScalarGridSpec(
            num_scalar_prefetch=1,
            grid=(1,),
            in_specs=[pl.BlockSpec(keep.shape, lambda i, a: (0, 0))] * 2,
            out_specs=[pl.BlockSpec((1, R, 2 * w), lambda i, a: (0, 0, 0)) for w in widths],
        ),
        out_shape=[jax.ShapeDtypeStruct((1, R, 2 * w), F32) for w in widths],
        compiler_params=PARAMS,
    )(at, keep, got)


def causal(length):
    i = lax.broadcasted_iota(jnp.int32, (length, length), 0)
    j = lax.broadcasted_iota(jnp.int32, (length, length), 1)
    return (i >= j) & (i // SPAN == j // SPAN)

def head_state(pre, logits, h, K, V, heads, keep):
    kh, vh = K // heads, V // heads
    length = pre.shape[0]
    q = pre[:, h * kh : (h + 1) * kh].astype(F32)
    k = pre[:, K + h * kh : K + (h + 1) * kh].astype(F32)
    v = pre[:, 2 * K + h * vh : 2 * K + (h + 1) * vh]
    x = logits[:, h * kh : (h + 1) * kh]
    a = (jnp.minimum(x, 0.0) - jnp.log1p(jnp.exp(-jnp.abs(x)))) * (1.0 / 16.0)
    tri = jnp.where(keep, 1.0, 0.0)
    b = lax.dot_general(tri, a, (((1,), (0,)), ((), ())), precision=lax.Precision.HIGHEST, preferred_element_type=F32)
    n = length // SPAN
    lasts = [b[(i + 1) * SPAN - 1 : (i + 1) * SPAN] for i in range(n)]
    last = jnp.concatenate([jnp.broadcast_to(t, (SPAN, kh)) for t in lasts], 0)
    eb = jnp.exp(b)
    enb = jnp.exp(-b)
    elb = jnp.exp(last - b)
    qs = q * (kh ** -0.5) * eb
    ks = k * enb
    kc = k * elb
    qs_l, ks_l, kc_l = qs.astype(BF), ks.astype(BF), kc.astype(BF)
    sc = jnp.where(keep, mm_nt(qs_l, ks_l), 0.0).astype(BF)
    local = mm(sc, v)
    states, decs, outs = [], [], []
    S = jnp.zeros((vh, kh), F32)
    for i in range(n):
        at = slice(i * SPAN, (i + 1) * SPAN)
        states.append(S)
        decs.append(jnp.exp(lasts[i]))
        o = local[at]
        if i:
            o = o + mm_nt(qs_l[at], S)
        outs.append(o)
        if i < n - 1:
            S = S * decs[i] + mm_tn(v[at], kc_l[at])
    return dict(q=q, k=k, v=v, x=x, eb=eb, enb=enb, elb=elb, qs=qs, ks=ks, kc=kc, qs_l=qs_l, ks_l=ks_l,
                kc_l=kc_l, sc=sc, states=states, decs=decs, out=jnp.concatenate(outs, 0))

def mixer_fwd_kernel(K, V, heads, pre_ref, logits_ref, gain_ref, out_ref):
    pre, logits, gain = pre_ref[...], logits_ref[...], gain_ref[...]
    keep = causal(pre.shape[0])
    vh = V // heads
    for h in range(heads):
        o = head_state(pre, logits, h, K, V, heads, keep)["out"]
        g = pre[:, 2 * K + V + h * vh : 2 * K + V + (h + 1) * vh].astype(F32)
        o = o * lax.rsqrt(jnp.mean(o * o, axis=-1, keepdims=True) + 1e-5) * gain
        out_ref[:, h * vh : (h + 1) * vh] = (o * (g * jax.nn.sigmoid(g))).astype(BF)

def mixer_bwd_kernel(K, V, heads, pre_ref, logits_ref, gain_ref, dg_ref, dpre_ref, dlog_ref, dgain_ref):
    pre, logits, gain = pre_ref[...], logits_ref[...], gain_ref[...]
    keep = causal(pre.shape[0])
    length = pre.shape[0]
    kh, vh = K // heads, V // heads
    n = length // SPAN
    dgain = jnp.zeros((1, vh), F32)
    for h in range(heads):
        st = head_state(pre, logits, h, K, V, heads, keep)
        out, v = st["out"], st["v"]
        g = pre[:, 2 * K + V + h * vh : 2 * K + V + (h + 1) * vh].astype(F32)
        dgated = dg_ref[:, h * vh : (h + 1) * vh].astype(F32)
        r = lax.rsqrt(jnp.mean(out * out, axis=-1, keepdims=True) + 1e-5)
        sg = jax.nn.sigmoid(g)
        on = out * r
        dgate = dgated * (on * gain) * (sg * (1.0 + g * (1.0 - sg)))
        dm = dgated * (g * sg)
        dgain = dgain + jnp.sum(dm * on, axis=0, keepdims=True)
        t = dm * gain
        dO = (t * r - on * (r * r * jnp.mean(t * out, axis=-1, keepdims=True))).astype(BF)
        dsc = jnp.where(keep, mm_nt(dO, v), 0.0).astype(BF)
        dv = mm_tn(st["sc"], dO)
        dqs = mm(dsc, st["ks_l"])
        dks = mm_tn(dsc, st["qs_l"])
        dqs_c, dkc, dv_c, dlast = [None] * n, [None] * n, [None] * n, [None] * n
        T = None
        for i in range(n - 1, -1, -1):
            at = slice(i * SPAN, (i + 1) * SPAN)
            if i:
                dqs_c[i] = mm(dO[at], st["states"][i])
            else:
                dqs_c[i] = jnp.zeros((SPAN, kh), F32)
            if T is None:
                dkc[i] = jnp.zeros((SPAN, kh), F32)
                dv_c[i] = jnp.zeros((SPAN, vh), F32)
                dlast[i] = jnp.zeros((SPAN, kh), F32)
            else:
                T_l = T.astype(BF)
                dkc[i] = mm(v[at], T_l)
                dv_c[i] = mm_nt(st["kc_l"][at], T_l)
                dl = jnp.sum(dkc[i] * st["kc"][at], axis=0, keepdims=True)
                if i:
                    dl = dl + jnp.sum(T * st["states"][i], axis=0, keepdims=True) * st["decs"][i]
                dlast[i] = jnp.broadcast_to(dl, (SPAN, kh))
            if i:
                new = mm_tn(dO[at], st["qs_l"][at])
                T = new if T is None else T * st["decs"][i] + new
        dqs = dqs + jnp.concatenate(dqs_c, 0)
        dkc = jnp.concatenate(dkc, 0)
        dv = dv + jnp.concatenate(dv_c, 0)
        db = dqs * st["qs"] - dks * st["ks"] - dkc * st["kc"]
        tri = jnp.where(keep, 1.0, 0.0)
        da = lax.dot_general(tri, db, (((0,), (0,)), ((), ())), precision=lax.Precision.HIGHEST, preferred_element_type=F32)
        da = da + jnp.concatenate(dlast, 0)
        x = st["x"]
        dlog_ref[:, h * kh : (h + 1) * kh] = da * (1.0 / 16.0) * (1.0 - jax.nn.sigmoid(x))
        dpre_ref[:, h * kh : (h + 1) * kh] = (dqs * (kh ** -0.5) * st["eb"]).astype(BF)
        dpre_ref[:, K + h * kh : K + (h + 1) * kh] = (dks * st["enb"] + dkc * st["elb"]).astype(BF)
        dpre_ref[:, 2 * K + h * vh : 2 * K + (h + 1) * vh] = dv.astype(BF)
        dpre_ref[:, 2 * K + V + h * vh : 2 * K + V + (h + 1) * vh] = dgate.astype(BF)
    @pl.when(pl.program_id(0) == 0)
    def _():
        dgain_ref[...] = jnp.zeros_like(dgain_ref)
    dgain_ref[...] += dgain

def row_spec(length, cols):
    return pl.BlockSpec((length, cols), lambda r: (r, 0))
def mixer_fwd(pre, logits, gain, rows, V):
    tokens, K = logits.shape
    length = tokens // rows
    heads = V // gain.shape[1]
    return pl.pallas_call(
        partial(mixer_fwd_kernel, K, V, heads),
        grid=(rows,),
        in_specs=[row_spec(length, pre.shape[1]), row_spec(length, K), pl.BlockSpec(gain.shape, lambda r: (0, 0))],
        out_specs=row_spec(length, V),
        out_shape=jax.ShapeDtypeStruct((tokens, V), BF),
        compiler_params=PARAMS,
        cost_estimate=COST,
    )(pre, logits, gain)
def mixer_bwd(pre, logits, gain, dgated, rows):
    tokens, K = logits.shape
    V = dgated.shape[1]
    length = tokens // rows
    heads = V // gain.shape[1]
    return pl.pallas_call(
        partial(mixer_bwd_kernel, K, V, heads),
        grid=(rows,),
        in_specs=[row_spec(length, pre.shape[1]), row_spec(length, K), pl.BlockSpec(gain.shape, lambda r: (0, 0)), row_spec(length, V)],
        out_specs=[row_spec(length, pre.shape[1]), row_spec(length, K), pl.BlockSpec(gain.shape, lambda r: (0, 0))],
        out_shape=[jax.ShapeDtypeStruct(pre.shape, BF), jax.ShapeDtypeStruct(logits.shape, F32), jax.ShapeDtypeStruct(gain.shape, F32)],
        compiler_params=PARAMS,
        cost_estimate=COST,
    )(pre, logits, gain, dgated)


def norm_back(dn, x, r, gain):
    t = dn * gain
    dx = t * r - x * (r * r * r * jnp.mean(t * x, axis=-1, keepdims=True))
    return dx, jnp.sum(dn * x * r, axis=0)


def exact_nt(a, b):
    return lax.dot_general(a, b, (((1,), (1,)), ((), ())), precision=lax.Precision.HIGHEST)


def project(x, w):
    r = lax.rsqrt(jnp.mean(x * x, axis=-1, keepdims=True) + 1e-6)
    n = (x * r * w["ag"]).astype(BF)
    pre = mm(n, w["WA"]).astype(BF)
    low = mm(n, w["rd"])
    logits = exact_nt(low, w["ru"]) + w["rb"]
    return dict(x=x, r=r, n=n, pre=pre, low=low, logits=logits)


def mix(m, w, rows):
    gated = mixer_fwd(m["pre"], m["logits"], w["gg"], rows, w["WO"].shape[0])
    return m["x"] + core_sum(mm(gated, w["WO"])), dict(m, gated=gated)


def expand(hidden, w):
    r = lax.rsqrt(jnp.mean(hidden * hidden, axis=-1, keepdims=True) + 1e-6)
    second = (hidden * r * w["mg"]).astype(BF)
    gu = mm(second, w["WF"]).astype(BF)
    return dict(hidden=hidden, r=r, second=second, gu=gu)


def contract(f, w, mask):
    gu = f["gu"]
    F = gu.shape[1] // 2
    gate, up = gu[:, :F].astype(F32), gu[:, F:].astype(F32)
    act = (gate * jax.nn.sigmoid(gate) * up).astype(BF)
    return (f["hidden"] + core_sum(mm(act, w["WD"]))) * mask, dict(f, act=act)


def column_halves(v, s):
    h = v.shape[1] // 2
    return lax.dynamic_slice_in_dim(v, s * h, h, 1), lax.dynamic_slice_in_dim(v, (1 - s) * h, h, 1)


def row_grads(rows_, cols, s):
    keep, give = column_halves(cols, s)
    got = over_core(mm_tn(rows_, give).astype(BF))
    return mm_tn(rows_, keep).astype(BF), got


def contract_back(dy, f, w):
    gu = f["gu"]
    F = gu.shape[1] // 2
    da = mm_nt(dy, w["WD"]).astype(BF).astype(F32)
    gate, up = gu[:, :F].astype(F32), gu[:, F:].astype(F32)
    sig = jax.nn.sigmoid(gate)
    return jnp.concatenate([da * up * (sig * (1.0 + gate * (1.0 - sig))), da * (gate * sig)], 1).astype(BF)


def expand_back(dy, dgu, f, w):
    dsec = core_sum(mm_nt(dgu, w["WF"])).astype(BF).astype(F32)
    back, d_mg = norm_back(dsec, f["hidden"], f["r"], w["mg"])
    return dy.astype(F32) + back, d_mg


def project_back(dhid, dpre, dlogits, d_gg, d_mg, m, w):
    dlow = jnp.matmul(dlogits, w["ru"], precision=lax.Precision.HIGHEST)
    dn = mm_nt(dpre, w["WA"]) + mm_nt(dlow, w["rd"])
    dn = core_sum(dn).astype(BF).astype(F32)
    dlow = core_sum(dlow)
    back, d_ag = norm_back(dn, m["x"], m["r"], w["ag"])
    small = dict(
        rd=mm_tn(m["n"], dlow),
        ru=mm_tn(dlogits, m["low"]),
        rb=jnp.sum(dlogits, axis=0),
        gg=d_gg[0],
        ag=d_ag,
        mg=d_mg,
    )
    return dhid + back, small


def body(
    inputs,
    lengths,
    out_grad,
    attn_gain,
    q_weight,
    k_weight,
    v_weight,
    rank_down,
    rank_up,
    rank_bias,
    gate_weight,
    group_gain,
    out_weight,
    mlp_gain,
    ffn_gate,
    ffn_up,
    ffn_down,
):
    size = lax.axis_size("dp")
    meshed = size == 16
    s = lax.axis_index("section")
    me = lax.axis_index("dp")
    at = jnp.stack([me // 4 % 4, (me // 2) % 2, me % 2, s]).astype(jnp.int32)
    first = s == 0
    shape = inputs.shape
    rows = shape[0] * shape[1]
    length, width = shape[2], shape[3]
    tokens = rows * length
    R = q_weight.shape[1]
    K, V, F, W = q_weight.shape[2] // 2, v_weight.shape[2] // 2, ffn_gate.shape[2] // 2, width // 2
    A = 2 * K + 2 * V
    half = (A + W) // 2
    rank = rank_down.shape[2]
    kc, gc = rank_bias.shape[1], group_gain.shape[1]
    ru_at = rank + 4
    links = [Link((0, 0, 1)), Link((0, 1, 0)), Link((1, 0, 0))]

    def paced(*values):
        if meshed:
            tokens = [link.sent[-1] for link in links]
            values = lax.optimization_barrier((values, tokens))[0]
        return values if len(values) > 1 else values[0]

    cuts = cut_columns(
        [
            (q_weight, k_weight, v_weight, gate_weight, out_weight),
            (ffn_gate, ffn_up),
            (ffn_down,),
        ],
        (rank_down, attn_gain, mlp_gain, rank_bias, group_gain, rank_up),
        at,
    )

    def by_layer(pair):
        keep, give = pair
        got = over_core(give)
        return jnp.where(first, keep, got), jnp.where(first, got, keep)

    (keep, give), ff, down = cuts[0], by_layer(cuts[1]), by_layer(cuts[2])
    got = over_core(give)
    table = keep[:, A + W :] + got[:, A + W :]
    keep, got = keep[:, : A + W], got[:, : A + W]
    ao = (jnp.concatenate([jnp.where(first, keep, got), table], 1), jnp.where(first, got, keep))

    def whole(v):
        return lax.all_gather(v, "dp", axis=0, tiled=True)

    def own_rows(v):
        h = v.shape[0] // 2
        keep = lax.dynamic_slice_in_dim(v, s * h, h, 0)
        got = over_core(lax.dynamic_slice_in_dim(v, (1 - s) * h, h, 0))
        return jnp.where(first, jnp.concatenate([keep, got], 1), jnp.concatenate([got, keep], 1))

    if meshed:
        gA = [GatherWide(links, v, half) for v in ao]
        gF = [GatherWide(links, v, F) for v in ff]
        gD = [GatherDown(links, v, at) for v in down]
    else:
        gA = gF = gD = [Idle(), Idle()]

    def place_ao(layer):
        if not meshed:
            v = whole(ao[layer])
            return v[:, :A], own_rows(v[:, A : A + W]), v[:, A + W :]
        columns = [
            [(0, half, 0, 0)],
            [(0, A - half, 0, half), (A - half, A - half + W, 1, 0)],
        ]
        C = ao[layer].shape[1]
        if C > A + W:
            columns[1].append((A - half + W, C - half, 3, 0))
        out = place_blocks(gA[layer].parts(), columns, at, split=1)
        keep, give = out[1].reshape(width // 2, W), out[2].reshape(width // 2, W)
        WO = join_columns(keep, over_core(give), at)
        return out[0].reshape(width, A), WO, (out[3].reshape(width, -1) if len(out) > 3 else None)

    def place_ff(layer):
        if not meshed:
            return whole(ff[layer])
        return place_blocks(gF[layer].parts(), [[(0, F, 0, 0)], [(0, F, 0, F)]], at)[0].reshape(width, 2 * F)

    def place_down(layer):
        if not meshed:
            return own_rows(whole(down[layer]))
        keep, give = split_planes(gD[layer].slabs, at)
        return join_columns(keep, over_core(give), at)

    def unpack(table, layer):
        t = table[:, 64 * layer : 64 * layer + ru_at + rank]
        flat = t[:, rank:ru_at].astype(F32).T
        ru = t.reshape(size, R, -1)[:, :kc, ru_at:].reshape(size * kc, rank).astype(F32)
        rb = flat[2].reshape(size, R)[:, :kc].reshape(1, size * kc)
        return dict(
            rd=t[:, :rank],
            ag=flat[0:1],
            mg=flat[1:2],
            ru=lax.dynamic_slice_in_dim(ru, s * K, K, 0),
            rb=lax.dynamic_slice_in_dim(rb, s * K, K, 1),
            gg=flat[3].reshape(size, R)[:, :gc].reshape(1, size * gc),
        )

    spots = jnp.arange(length)
    mask = (spots[None, :] < lengths.reshape(rows, 1)).astype(F32).reshape(tokens, 1)
    low_mask = mask.astype(BF)
    x0 = inputs.reshape(tokens, width).astype(F32)

    gD[0].sides(), gD[1].sides()
    gA[0].ring(), gA[0].ring(), gA[0].ring()
    gD[0].diag(), gD[1].diag()
    gA[0].first(), gA[0].second(), gA[0].third()
    gF[0].ring(), gF[0].ring(), gF[0].ring(), gD[0].ring()
    WA0, WO0, table = place_ao(0)
    p0, p1 = unpack(table, 0), unpack(table, 1)
    w0 = dict(p0, WA=WA0, WO=WO0)
    gF[0].first(), gD[0].ring()
    x0, w0 = paced(x0, w0)
    m0 = project(x0, w0)
    m0, p1 = paced(m0, p1)
    gF[0].second(), gD[0].ring(), gA[1].ring()
    h0, m0 = paced(*mix(m0, w0, rows))
    gF[0].third(), gA[1].ring(), gA[1].ring()
    w0["WF"] = place_ff(0)
    w0["WD"] = place_down(0)
    gA[1].first(), gF[1].ring()
    f0 = paced(expand(h0, w0))
    gA[1].second(), gF[1].ring()
    y0, f0 = paced(*contract(f0, w0, mask))
    x1 = y0.astype(BF)
    gA[1].third(), gF[1].ring()
    WA1, WO1, _ = place_ao(1)
    w1 = dict(p1, WA=WA1, WO=WO1)
    gF[1].first(), gD[1].ring()
    m1 = paced(project(x1.astype(F32), w1))
    gF[1].second(), gD[1].ring()
    h1, m1 = paced(*mix(m1, w1, rows))
    gF[1].third(), gD[1].ring()
    w1["WF"] = place_ff(1)
    w1["WD"] = place_down(1)
    f1 = expand(h1, w1)
    y1, f1 = contract(f1, w1, mask)
    layer_out = jnp.where(first, x1, y1.astype(BF)).reshape((1,) + shape)

    def all_rows(keep, got):
        return jnp.where(first, jnp.concatenate([keep, got], 0), jnp.concatenate([got, keep], 0))

    def scatter(v):
        return lax.psum_scatter(v, "dp", scatter_dimension=0, tiled=True)

    class Sum:
        def __init__(self, v):
            self.sum = scatter(v)

        def ring(self):
            pass

        along = diag = sides = rest = ring

    def sum_down(g):
        return ReduceDown(links, *g, at) if meshed else Sum(all_rows(*g))

    def sum_ff(second, dgu):
        if meshed:
            return ReduceWide(links, grad_blocks(second, dgu, F, at))
        return Sum(mm_tn(second, dgu).astype(BF))

    def sum_ao(n, dpre, gO, packed=()):
        extras = gO + packed
        if meshed:
            return ReduceWide(links, grad_blocks(n, dpre, half, at, extras))
        return Sum(jnp.concatenate((mm_tn(n, dpre).astype(BF), all_rows(*gO)) + packed, 1))

    dy1 = out_grad.reshape(tokens, width) * low_mask
    gD1 = row_grads(f1["act"], dy1, s)
    rD1 = sum_down(gD1)
    dgu = contract_back(dy1, f1, w1)
    rF1 = sum_ff(after(f1["second"], *gD1), dgu)
    rF1.diag(), rD1.ring()
    dh1, d_mg1 = expand_back(dy1, dgu, f1, w1)
    low = dh1.astype(BF)
    dgated = mm_nt(low, w1["WO"]).astype(BF)
    gO1 = row_grads(m1["gated"], low, s)
    dh1, d_mg1, dgated, gO1 = paced(dh1, d_mg1, dgated, gO1)
    rF1.sides(), rD1.ring()
    back = paced(mixer_bwd(m1["pre"], m1["logits"], w1["gg"], dgated, rows))
    rF1.rest(), rD1.ring()
    rA1 = sum_ao(m1["n"], back[0], gO1)
    dx1, small1 = paced(*project_back(dh1, *back, d_mg1, m1, w1))
    rA1.diag(), rF1.ring()
    dy0 = dx1.astype(BF) * low_mask
    gD0 = row_grads(f0["act"], dy0, s)
    dgu, gD0, dy0 = paced(contract_back(dy0, f0, w0), gD0, dy0)
    rD0 = sum_down(gD0)
    rA1.sides(), rF1.ring()
    rF0 = sum_ff(f0["second"], dgu)
    dh0, d_mg0 = paced(*expand_back(dy0, dgu, f0, w0))
    rA1.rest(), rF1.ring()
    low = dh0.astype(BF)
    dgated = mm_nt(low, w0["WO"]).astype(BF)
    dgated, gO0 = paced(dgated, row_grads(m0["gated"], low, s))
    rF0.diag(), rA1.ring()
    back = paced(mixer_bwd(m0["pre"], m0["logits"], w0["gg"], dgated, rows))
    rF0.sides(), rA1.ring()
    dx0, small0 = project_back(dh0, *back, d_mg0, m0, w0)
    dpre = back[0]
    input_out = jnp.where(first, dx0, dx1).reshape((1,) + shape)

    mine = {k: jnp.where(first, small0[k], small1[k]) for k in small0}
    other = {k: over_core(jnp.where(first, small1[k], small0[k])) for k in ("ru", "rb", "gg")}
    ru = all_rows(mine["ru"], other["ru"])
    rb = all_rows(mine["rb"], other["rb"])

    def tall_blocks(v):
        v = v.reshape(size, v.shape[0] // size, -1)
        return jnp.pad(v, ((0, 0), (0, R - v.shape[1]), (0, 0))).reshape(size * R, -1)

    def long_blocks(v):
        v = v.reshape(size, -1)
        return jnp.pad(v, ((0, 0), (0, R - v.shape[1]))).reshape(size * R)

    flat = jnp.stack([mine["ag"], mine["mg"], long_blocks(rb), long_blocks(mine["gg"] + other["gg"])]).T
    packed = jnp.concatenate([mine["rd"], flat, tall_blocks(ru)], 1)
    packed = jnp.pad(packed, ((0, 0), (0, 128 - packed.shape[1]))).astype(BF)

    rA0 = sum_ao(m0["n"], dpre, gO0, (packed,))
    rF0.rest(), rA1.ring(), rD0.ring(), rD0.ring(), rD0.ring()
    rA0.diag()
    rF0.along()
    rA0.sides()
    rA0.rest()
    rA0.along()
    for r in (rD1, rD0):
        r.diag()
    for r in (rD1, rD0):
        r.sides()
    for r in (rD1, rD0):
        r.rest()

    def join(a, b, widths):
        keep = jnp.where(first, a, b)
        got = over_core(jnp.where(first, b, a))
        return finish(keep, got, widths, at)

    dD = join(rD0.sum, rD1.sum, (W,))[0]
    dFg, dFu = join(rF0.sum, rF1.sum, (F, F))
    dq, dk, dv, dg, dO = join(rA0.sum[:, : A + W], rA1.sum, (K, K, V, V, W))
    t = rA0.sum[:, A + W :].astype(F32)
    return (
        layer_out,
        input_out,
        t[:, rank][None],
        dq,
        dk,
        dv,
        t[:, :rank][None],
        t[:kc, ru_at : ru_at + rank].T[None],
        t[:kc, rank + 2][None],
        dg,
        t[:gc, rank + 3][None],
        dO,
        t[:, rank + 1][None],
        dFg,
        dFu,
        dD,
    )


def solution(mesh):
    rows3 = P("section", "dp", None)
    one = P("section", "dp")
    return jax.shard_map(
        body,
        mesh=mesh,
        in_specs=(
            P(None, "dp", None, None),
            P(None, "dp"),
            P(None, "dp", None, None),
            one,
            rows3,
            rows3,
            rows3,
            rows3,
            P("section", None, "dp"),
            one,
            rows3,
            one,
            rows3,
            one,
            rows3,
            rows3,
            rows3,
        ),
        out_specs=(
            P("section", None, "dp", None, None),
            P("section", None, "dp", None, None),
            one,
            rows3,
            rows3,
            rows3,
            rows3,
            P("section", None, "dp"),
            one,
            rows3,
            one,
            rows3,
            one,
            rows3,
            rows3,
            rows3,
        ),
        check_vma=False,
    )
```

```python
from functools import partial

import jax
import jax.numpy as jnp
from jax import lax
from jax.experimental import pallas as pl
from jax.experimental.pallas import tpu as pltpu
from jax.sharding import PartitionSpec as P

SPAN = 64
BF = jnp.bfloat16
F32 = jnp.float32
PARAMS = pltpu.CompilerParams(vmem_limit_bytes=20 << 20)
FULL = pltpu.CompilerParams(vmem_limit_bytes=60 << 20)
COST = pl.CostEstimate(flops=0, bytes_accessed=0, transcendentals=0)


def mm(a, b):
    return lax.dot_general(
        a.astype(BF), b.astype(BF), (((1,), (0,)), ((), ())), preferred_element_type=F32
    )


def mm_nt(a, b):
    return lax.dot_general(
        a.astype(BF), b.astype(BF), (((1,), (1,)), ((), ())), preferred_element_type=F32
    )


def mm_tn(a, b):
    return lax.dot_general(
        a.astype(BF), b.astype(BF), (((0,), (0,)), ((), ())), preferred_element_type=F32
    )


def after(value, *tokens):
    return lax.optimization_barrier((value,) + tokens)[0]


def copy_call(kernel, at, ins, in_specs, outs, out_specs, grid, params=None):
    return pl.pallas_call(
        kernel,
        grid_spec=pltpu.PrefetchScalarGridSpec(
            num_scalar_prefetch=1, grid=grid, in_specs=in_specs, out_specs=out_specs
        ),
        out_shape=[jax.ShapeDtypeStruct(o, BF) for o in outs],
        compiler_params=params or PARAMS,
        cost_estimate=COST,
    )(at, *ins)


def table_block(s, rd, ag, mg, rb, gg, ru):
    R, rank = rd.shape

    def one_hot(n, at):
        i = lax.broadcasted_iota(jnp.int32, (n, 128), 0)
        return jnp.where(i + at + 64 * s == lax.broadcasted_iota(jnp.int32, (n, 128), 1), 1.0, 0.0)

    def upright(row):
        n = row.shape[1]
        i = lax.broadcasted_iota(jnp.int32, (R, n), 0)
        return mm_nt(jnp.where(i == lax.broadcasted_iota(jnp.int32, (R, n), 1), 1.0, 0.0), row)

    out = mm(rd, one_hot(rank, 0)) + mm(upright(ru), one_hot(rank, rank + 4))
    for k, row in enumerate((ag, mg, rb, gg)):
        out = out + mm(upright(jnp.broadcast_to(row, (8, row.shape[1]))), one_hot(8, rank + k)[0:1] * (
            lax.broadcasted_iota(jnp.int32, (8, 1), 0) == 0
        ).astype(F32))
    return out.astype(BF)


def cut_kernel(groups, at_ref, *refs):
    n = sum(len(g) for g in groups)
    ins, smalls, outs = refs[:n], refs[n : n + 6], refs[n + 6 :]
    s = at_ref[3]
    k = 0
    for g, _ in enumerate(groups):
        to = 0
        for _ in groups[g]:
            h = ins[k].shape[2] // 2
            for o, half in ((2 * g, s), (2 * g + 1, 1 - s)):
                outs[o][:, to : to + h] = ins[k][0, :, pl.ds(pl.multiple_of(half * h, h), h)]
            to += h
            k += 1
        if g == 0:
            rd, ag, mg, rb, gg, ru = smalls
            table = table_block(s, rd[0], ag[...], mg[...], rb[...], gg[...], ru[0])
            outs[0][:, to:] = table
            outs[1][:, to:] = table


def cut_columns(groups, smalls, at):
    ins = [v for g in groups for v in g] + list(smalls)
    in_specs = [pl.BlockSpec(v.shape, lambda i, a, d=v.ndim: (0,) * d) for v in ins]
    outs = []
    for g, arrays in enumerate(groups):
        C = sum(v.shape[2] for v in arrays) // 2 + (128 if g == 0 else 0)
        outs += [(arrays[0].shape[1], C)] * 2
    out_specs = [pl.BlockSpec(o, lambda i, a: (0, 0)) for o in outs]
    out = copy_call(partial(cut_kernel, groups), at, ins, in_specs, outs, out_specs, (1,), FULL)
    return [(out[2 * g], out[2 * g + 1]) for g in range(len(groups))]


def join_kernel(at_ref, keep_ref, got_ref, out_ref):
    W = keep_ref.shape[1]
    s = at_ref[3]
    out_ref[:, pl.ds(pl.multiple_of(s * W, W), W)] = keep_ref[...]
    out_ref[:, pl.ds(pl.multiple_of((1 - s) * W, W), W)] = got_ref[...]


def join_columns(keep, got, at):
    H, W = keep.shape
    n = H // 4
    spec = pl.BlockSpec((n, W), lambda i, a: (i, 0))
    out = pl.BlockSpec((n, 2 * W), lambda i, a: (i, 0))
    return copy_call(join_kernel, at, [keep, got], [spec, spec], [(H, 2 * W)], [out], (4,))[0]


def pairs(dz, dy, dx):
    return [
        (z * 4 + y * 2 + x, ((z + dz) % 4) * 4 + (y ^ dy) * 2 + (x ^ dx))
        for z in range(4)
        for y in range(2)
        for x in range(2)
    ]


LINES = [[z * 4 + y * 2 + x for z in range(4)] for y in range(2) for x in range(2)]


class Links:
    def __init__(self):
        self.sent = {"x": [], "y": []}
        self.open, self.before = [], []

    def hop(self, name, v, step):
        sent = self.sent[name]
        if sent:
            v = after(v, sent[-1], *self.before)
        sent.append(lax.ppermute(v, "dp", pairs(*step)))
        return sent[-1]

    def x(self, v):
        return self.hop("x", v, (0, 0, 1))

    def y(self, v):
        return self.hop("y", v, (0, 1, 0))

    def gather(self, v, due):
        v = lax.all_gather(v, "dp", axis=0, tiled=True, axis_index_groups=LINES)
        self.open.append([due, v])
        return v

    def scatter(self, v, due):
        self.before.append(v)
        v = lax.psum_scatter(v, "dp", scatter_dimension=0, tiled=True, axis_index_groups=LINES)
        self.open.append([due, v])
        return v

    def meeting(self):
        tokens = self.sent["x"][-1:] + self.sent["y"][-1:]
        for entry in self.open:
            entry[0] -= 1
            if entry[0] == 0:
                tokens.append(entry[1])
        return tokens


def over_core(v):
    return lax.ppermute(v, "section", [(0, 1), (1, 0)])


def core_sum(v):
    v = v.astype(BF)
    return v.astype(F32) + over_core(v).astype(F32)


def add(a, b):
    return (a.astype(F32) + b.astype(F32)).astype(BF)


def ring(pz, v):
    slabs = [v]
    for _ in range(3):
        slabs.append(pz(slabs[-1]))
    return slabs


BLOCKS = ((0, 0), (0, 1), (1, 0), (1, 1))


class Idle:
    def __getattr__(self, name):
        return lambda *a: None


class GatherWide:
    def __init__(self, links, shard):
        self.links, self.shard = links, shard

    def along(self, due, *tokens):
        v = after(self.shard, *tokens) if tokens else self.shard
        self.line = self.links.gather(v, due).reshape((4,) + self.shard.shape)

    def along_with(self, other, due, *tokens):
        R, C = self.shard.shape
        v = after(jnp.concatenate([self.shard, other.shard.reshape(R, -1)], 1), *tokens)
        v = self.links.gather(v, due)
        v = v.reshape(4, R, -1)
        self.line = v[:, :, :C]
        other.line = v[:, :, C:].reshape((4,) + other.shard.shape)

    def sides(self):
        self.X, self.Y = self.links.x(self.line), self.links.y(self.line)

    def diag(self):
        self.hi, self.lo = self.links.x(self.Y[2:]), self.links.y(self.X[:2])

    def parts(self):
        return [self.line, self.X, self.Y, self.lo, self.hi]


def plane_of(j, a):
    return (2 * a[3] + j) % 4


def place_kernel(columns, split, n_out, at_ref, *refs):
    ins, outs = refs[:-n_out], refs[-n_out:]
    j = pl.program_id(0)
    y, x = at_ref[1], at_ref[2]

    def write(lo, hi, o, to):
        for (yy, xx), v in zip(BLOCKS, ins[:3]):
            outs[o][0, y ^ yy, x ^ xx, :, to : to + hi - lo] = v[0, :, lo:hi]

        @pl.when(plane_of(j, at_ref) < 2)
        def _():
            outs[o][0, 1 - y, 1 - x, :, to : to + hi - lo] = ins[3][0, :, lo:hi]

        @pl.when(plane_of(j, at_ref) >= 2)
        def _():
            outs[o][0, 1 - y, 1 - x, :, to : to + hi - lo] = ins[4][0, :, lo:hi]

    for lo, hi, o, to in columns:
        if o == split:
            pl.when(j < 2)(partial(write, lo, hi, o, to))
            pl.when(j >= 2)(partial(write, lo, hi, o + 1, to))
        else:
            write(lo, hi, o, to)


def place_blocks(ins, columns, at, split=None):
    _, R, _ = ins[0].shape
    width = {}
    for lo, hi, o, to in columns:
        width[o] = max(width.get(o, 0), to + hi - lo)
    if split is not None:
        width[split + 1] = width[split]
    shapes, specs = [], []
    for o in sorted(width):
        block = (1, 2, 2, R, width[o])
        if split is not None and o == split:
            shapes.append((2,) + block[1:])
            specs.append(pl.BlockSpec(block, lambda j, a: (jnp.minimum(j, 1), 0, 0, 0, 0)))
        elif split is not None and o == split + 1:
            shapes.append((2,) + block[1:])
            specs.append(pl.BlockSpec(block, lambda j, a: (jnp.maximum(j, 2) - 2, 0, 0, 0, 0)))
        else:
            shapes.append((4,) + block[1:])
            specs.append(pl.BlockSpec(block, lambda j, a: (plane_of(j, a), 0, 0, 0, 0)))
    in_specs = [pl.BlockSpec((1,) + v.shape[1:], lambda j, a: (plane_of(j, a), 0, 0)) for v in ins[:3]]
    in_specs += [pl.BlockSpec((1,) + v.shape[1:], lambda j, a: (plane_of(j, a) % 2, 0, 0)) for v in ins[3:]]
    return copy_call(
        partial(place_kernel, columns, split, len(shapes)), at, ins, in_specs, shapes, specs, (4,)
    )


class GatherDown:
    def __init__(self, links, shard, at):
        self.links, self.shard, self.at = links, shard, at

    def around(self):
        v, links = self.shard, self.links
        R, C = v.shape
        h = C // 2
        y, x = self.at[1], self.at[2]
        X, Y = links.x(v), links.y(v)
        D2, D1 = links.x(Y[:, h:]), links.y(X[:, :h])
        out = jnp.zeros((2, 2, R, C), BF)
        for b, p, c in ((0, v, 0), (1, X, 0), (2, Y, 0), (3, D1, 0), (3, D2, h)):
            yy, xx = BLOCKS[b]
            out = lax.dynamic_update_slice(out, p[None, None], (y ^ yy, x ^ xx, 0, c))
        self.block = out.reshape(4 * R, C)

    def along(self, due, *tokens):
        self.all = self.links.gather(after(self.block, *tokens), due)


def grad_kernel(R, at_ref, lhs_ref, rhs_ref, *refs):
    acc = refs[-1]
    extras, (own, Sx, Sy, Rx, Ry) = refs[:-6], refs[-6:-1]
    C = rhs_ref.shape[1]
    acc[:, :C] = mm_tn(lhs_ref[...], rhs_ref[...])
    i = pl.program_id(0)
    y, x, s = at_ref[1], at_ref[2], at_ref[3]
    if extras:
        keep, got = extras[0][...].astype(F32), extras[1][...].astype(F32)
        W = keep.shape[1]
        acc[:, C : C + W] = jnp.where((i // 2) == s, keep, got)
        if len(extras) > 2:
            acc[:, C + W :] = extras[2][...].astype(F32)

    def block(b):
        yy, xx = BLOCKS[b]
        return acc[pl.ds(pl.multiple_of(((y ^ yy) * 2 + (x ^ xx)) * R, R), R), :].astype(BF)

    own[0] = block(0)

    @pl.when(i < 2)
    def _():
        Sx[0, 0] = block(3)
        Sx[1, 0] = block(1)
        Ry[0] = block(2)

    @pl.when(i >= 2)
    def _():
        Sy[0, 0] = block(3)
        Sy[1, 0] = block(2)
        Rx[0] = block(1)


def grad_blocks(lhs, rhs, at, extras=()):
    tokens, D = lhs.shape
    C = rhs.shape[1] + sum(e.shape[1] for e in extras[:1] + extras[2:])
    n = D // 4
    R = n // 4
    in_specs = [
        pl.BlockSpec((tokens, n), lambda i, a: (0, i)),
        pl.BlockSpec(rhs.shape, lambda i, a: (0, 0)),
    ]
    for k, e in enumerate(extras):
        if k < 2:
            in_specs.append(pl.BlockSpec((n, e.shape[1]), lambda i, a: (i % 2, 0)))
        else:
            in_specs.append(pl.BlockSpec((n, e.shape[1]), lambda i, a: (i, 0)))
    pair = (2, 1, R, C)
    return pl.pallas_call(
        partial(grad_kernel, R),
        grid_spec=pltpu.PrefetchScalarGridSpec(
            num_scalar_prefetch=1,
            grid=(4,),
            in_specs=in_specs,
            out_specs=[
                pl.BlockSpec((1, R, C), lambda i, a: (i, 0, 0)),
                pl.BlockSpec(pair, lambda i, a: (0, jnp.minimum(i, 1), 0, 0)),
                pl.BlockSpec(pair, lambda i, a: (0, jnp.maximum(i, 2) - 2, 0, 0)),
                pl.BlockSpec((1, R, C), lambda i, a: (jnp.maximum(i, 2) - 2, 0, 0)),
                pl.BlockSpec((1, R, C), lambda i, a: (jnp.minimum(i, 1), 0, 0)),
            ],
            scratch_shapes=[pltpu.VMEM((n, C), F32)],
        ),
        out_shape=[
            jax.ShapeDtypeStruct(v, BF)
            for v in ((4, R, C), (2, 2, R, C), (2, 2, R, C), (2, R, C), (2, R, C))
        ],
        compiler_params=PARAMS,
    )(at, lhs, rhs, *extras)


def slab_kernel(own, gx, gy, tx, ty, out):
    i = pl.program_id(0)

    @pl.when(i < 2)
    def _():
        out[...] = (own[0].astype(F32) + gx[0, 0].astype(F32) + ty[0].astype(F32)).astype(BF)

    @pl.when(i >= 2)
    def _():
        out[...] = (own[0].astype(F32) + gy[0, 0].astype(F32) + tx[0].astype(F32)).astype(BF)


def sum_slabs(own, gx, gy, tx, ty):
    _, R, C = own.shape
    low = lambda i: jnp.minimum(i, 1)
    high = lambda i: jnp.maximum(i, 2) - 2
    return pl.pallas_call(
        slab_kernel,
        grid=(4,),
        in_specs=[
            pl.BlockSpec((1, R, C), lambda i: (i, 0, 0)),
            pl.BlockSpec((1, 1, R, C), lambda i: (1, low(i), 0, 0)),
            pl.BlockSpec((1, 1, R, C), lambda i: (1, high(i), 0, 0)),
            pl.BlockSpec((1, R, C), lambda i: (high(i), 0, 0)),
            pl.BlockSpec((1, R, C), lambda i: (low(i), 0, 0)),
        ],
        out_specs=pl.BlockSpec((R, C), lambda i: (i, 0)),
        out_shape=jax.ShapeDtypeStruct((4 * R, C), BF),
        compiler_params=PARAMS,
    )(own, gx, gy, tx, ty)


def total(*parts):
    t = parts[0].astype(F32)
    for v in parts[1:]:
        t = t + v.astype(F32)
    return t.astype(BF)


class ReduceWide:
    def __init__(self, links, blocks):
        self.links = links
        self.own, self.Sx, self.Sy, self.Rx, self.Ry = blocks

    def sides(self):
        self.gx, self.gy = self.links.x(self.Sx), self.links.y(self.Sy)

    def rest(self):
        self.tx = self.links.x(add(self.Rx, self.gy[0]))
        self.ty = self.links.y(add(self.Ry, self.gx[0]))

    def along(self, due):
        self.sum = self.links.scatter(sum_slabs(self.own, self.gx, self.gy, self.tx, self.ty), due)


class ReduceDown:
    def __init__(self, links, v, at):
        self.links, self.v, self.at = links, v, at

    def along(self, due):
        self.sum = self.links.scatter(self.v, due)

    def pick(self, b, lo, hi):
        yy, xx = BLOCKS[b]
        R = self.sum.shape[0] // 4
        v = self.sum.reshape(2, 2, R, -1)
        y, x = self.at[1], self.at[2]
        return lax.dynamic_slice(v, (y ^ yy, x ^ xx, 0, lo), (1, 1, R, hi - lo)).reshape(R, hi - lo)


def around(links, parts):
    C = parts[0].sum.shape[1]
    h = C // 2

    def pick(b, lo, hi):
        return jnp.concatenate([p.pick(b, lo, hi) for p in parts], 0)

    r1, r2 = links.x(pick(3, 0, h)), links.y(pick(3, h, C))
    a1, b2 = links.x(pick(1, 0, h)), links.y(pick(2, h, C))
    a2 = links.x(add(pick(1, h, C), r2))
    b1 = links.y(add(pick(2, 0, h), r1))
    v = jnp.concatenate([total(pick(0, 0, h), a1, b1), total(pick(0, h, C), a2, b2)], 1)
    R = v.shape[0] // len(parts)
    for n, p in enumerate(parts):
        p.sum = v[n * R : (n + 1) * R]


def finish_kernel(widths, at_ref, keep_ref, got_ref, *outs):
    s = at_ref[3]
    to = 0
    for w, out in zip(widths, outs):
        out[0, :, pl.ds(pl.multiple_of(s * w, w), w)] = keep_ref[:, to : to + w].astype(F32)
        out[0, :, pl.ds(pl.multiple_of((1 - s) * w, w), w)] = got_ref[:, to : to + w].astype(F32)
        to += w


def finish(keep, got, widths, at):
    R = keep.shape[0]
    return pl.pallas_call(
        partial(finish_kernel, widths),
        grid_spec=pltpu.PrefetchScalarGridSpec(
            num_scalar_prefetch=1,
            grid=(1,),
            in_specs=[pl.BlockSpec(keep.shape, lambda i, a: (0, 0))] * 2,
            out_specs=[pl.BlockSpec((1, R, 2 * w), lambda i, a: (0, 0, 0)) for w in widths],
        ),
        out_shape=[jax.ShapeDtypeStruct((1, R, 2 * w), F32) for w in widths],
        compiler_params=PARAMS,
    )(at, keep, got)


def causal(length):
    i = lax.broadcasted_iota(jnp.int32, (length, length), 0)
    j = lax.broadcasted_iota(jnp.int32, (length, length), 1)
    return (i >= j) & (i // SPAN == j // SPAN)

def head_state(pre, logits, h, K, V, heads, keep):
    kh, vh = K // heads, V // heads
    length = pre.shape[0]
    q = pre[:, h * kh : (h + 1) * kh].astype(F32)
    k = pre[:, K + h * kh : K + (h + 1) * kh].astype(F32)
    v = pre[:, 2 * K + h * vh : 2 * K + (h + 1) * vh]
    x = logits[:, h * kh : (h + 1) * kh]
    a = (jnp.minimum(x, 0.0) - jnp.log1p(jnp.exp(-jnp.abs(x)))) * (1.0 / 16.0)
    tri = jnp.where(keep, 1.0, 0.0)
    b = lax.dot_general(tri, a, (((1,), (0,)), ((), ())), precision=lax.Precision.HIGHEST, preferred_element_type=F32)
    n = length // SPAN
    lasts = [b[(i + 1) * SPAN - 1 : (i + 1) * SPAN] for i in range(n)]
    last = jnp.concatenate([jnp.broadcast_to(t, (SPAN, kh)) for t in lasts], 0)
    eb = jnp.exp(b)
    enb = jnp.exp(-b)
    elb = jnp.exp(last - b)
    qs = q * (kh ** -0.5) * eb
    ks = k * enb
    kc = k * elb
    qs_l, ks_l, kc_l = qs.astype(BF), ks.astype(BF), kc.astype(BF)
    sc = jnp.where(keep, mm_nt(qs_l, ks_l), 0.0).astype(BF)
    local = mm(sc, v)
    states, decs, outs = [], [], []
    S = jnp.zeros((vh, kh), F32)
    for i in range(n):
        at = slice(i * SPAN, (i + 1) * SPAN)
        states.append(S)
        decs.append(jnp.exp(lasts[i]))
        o = local[at]
        if i:
            o = o + mm_nt(qs_l[at], S)
        outs.append(o)
        if i < n - 1:
            S = S * decs[i] + mm_tn(v[at], kc_l[at])
    return dict(q=q, k=k, v=v, x=x, eb=eb, enb=enb, elb=elb, qs=qs, ks=ks, kc=kc, qs_l=qs_l, ks_l=ks_l,
                kc_l=kc_l, sc=sc, states=states, decs=decs, out=jnp.concatenate(outs, 0))

def mixer_fwd_kernel(K, V, heads, pre_ref, logits_ref, gain_ref, out_ref):
    pre, logits, gain = pre_ref[...], logits_ref[...], gain_ref[...]
    keep = causal(pre.shape[0])
    vh = V // heads
    for h in range(heads):
        o = head_state(pre, logits, h, K, V, heads, keep)["out"]
        g = pre[:, 2 * K + V + h * vh : 2 * K + V + (h + 1) * vh].astype(F32)
        o = o * lax.rsqrt(jnp.mean(o * o, axis=-1, keepdims=True) + 1e-5) * gain
        out_ref[:, h * vh : (h + 1) * vh] = (o * (g * jax.nn.sigmoid(g))).astype(BF)

def mixer_bwd_kernel(K, V, heads, pre_ref, logits_ref, gain_ref, dg_ref, dpre_ref, dlog_ref, dgain_ref):
    pre, logits, gain = pre_ref[...], logits_ref[...], gain_ref[...]
    keep = causal(pre.shape[0])
    length = pre.shape[0]
    kh, vh = K // heads, V // heads
    n = length // SPAN
    dgain = jnp.zeros((1, vh), F32)
    for h in range(heads):
        st = head_state(pre, logits, h, K, V, heads, keep)
        out, v = st["out"], st["v"]
        g = pre[:, 2 * K + V + h * vh : 2 * K + V + (h + 1) * vh].astype(F32)
        dgated = dg_ref[:, h * vh : (h + 1) * vh].astype(F32)
        r = lax.rsqrt(jnp.mean(out * out, axis=-1, keepdims=True) + 1e-5)
        sg = jax.nn.sigmoid(g)
        on = out * r
        dgate = dgated * (on * gain) * (sg * (1.0 + g * (1.0 - sg)))
        dm = dgated * (g * sg)
        dgain = dgain + jnp.sum(dm * on, axis=0, keepdims=True)
        t = dm * gain
        dO = (t * r - on * (r * r * jnp.mean(t * out, axis=-1, keepdims=True))).astype(BF)
        dsc = jnp.where(keep, mm_nt(dO, v), 0.0).astype(BF)
        dv = mm_tn(st["sc"], dO)
        dqs = mm(dsc, st["ks_l"])
        dks = mm_tn(dsc, st["qs_l"])
        dqs_c, dkc, dv_c, dlast = [None] * n, [None] * n, [None] * n, [None] * n
        T = None
        for i in range(n - 1, -1, -1):
            at = slice(i * SPAN, (i + 1) * SPAN)
            if i:
                dqs_c[i] = mm(dO[at], st["states"][i])
            else:
                dqs_c[i] = jnp.zeros((SPAN, kh), F32)
            if T is None:
                dkc[i] = jnp.zeros((SPAN, kh), F32)
                dv_c[i] = jnp.zeros((SPAN, vh), F32)
                dlast[i] = jnp.zeros((SPAN, kh), F32)
            else:
                T_l = T.astype(BF)
                dkc[i] = mm(v[at], T_l)
                dv_c[i] = mm_nt(st["kc_l"][at], T_l)
                dl = jnp.sum(dkc[i] * st["kc"][at], axis=0, keepdims=True)
                if i:
                    dl = dl + jnp.sum(T * st["states"][i], axis=0, keepdims=True) * st["decs"][i]
                dlast[i] = jnp.broadcast_to(dl, (SPAN, kh))
            if i:
                new = mm_tn(dO[at], st["qs_l"][at])
                T = new if T is None else T * st["decs"][i] + new
        dqs = dqs + jnp.concatenate(dqs_c, 0)
        dkc = jnp.concatenate(dkc, 0)
        dv = dv + jnp.concatenate(dv_c, 0)
        db = dqs * st["qs"] - dks * st["ks"] - dkc * st["kc"]
        tri = jnp.where(keep, 1.0, 0.0)
        da = lax.dot_general(tri, db, (((0,), (0,)), ((), ())), precision=lax.Precision.HIGHEST, preferred_element_type=F32)
        da = da + jnp.concatenate(dlast, 0)
        x = st["x"]
        dlog_ref[:, h * kh : (h + 1) * kh] = da * (1.0 / 16.0) * (1.0 - jax.nn.sigmoid(x))
        dpre_ref[:, h * kh : (h + 1) * kh] = (dqs * (kh ** -0.5) * st["eb"]).astype(BF)
        dpre_ref[:, K + h * kh : K + (h + 1) * kh] = (dks * st["enb"] + dkc * st["elb"]).astype(BF)
        dpre_ref[:, 2 * K + h * vh : 2 * K + (h + 1) * vh] = dv.astype(BF)
        dpre_ref[:, 2 * K + V + h * vh : 2 * K + V + (h + 1) * vh] = dgate.astype(BF)
    @pl.when(pl.program_id(0) == 0)
    def _():
        dgain_ref[...] = jnp.zeros_like(dgain_ref)
    dgain_ref[...] += dgain

def row_spec(length, cols):
    return pl.BlockSpec((length, cols), lambda r: (r, 0))
def mixer_fwd(pre, logits, gain, rows, V):
    tokens, K = logits.shape
    length = tokens // rows
    heads = V // gain.shape[1]
    return pl.pallas_call(
        partial(mixer_fwd_kernel, K, V, heads),
        grid=(rows,),
        in_specs=[row_spec(length, pre.shape[1]), row_spec(length, K), pl.BlockSpec(gain.shape, lambda r: (0, 0))],
        out_specs=row_spec(length, V),
        out_shape=jax.ShapeDtypeStruct((tokens, V), BF),
        compiler_params=PARAMS,
        cost_estimate=COST,
    )(pre, logits, gain)
def mixer_bwd(pre, logits, gain, dgated, rows):
    tokens, K = logits.shape
    V = dgated.shape[1]
    length = tokens // rows
    heads = V // gain.shape[1]
    return pl.pallas_call(
        partial(mixer_bwd_kernel, K, V, heads),
        grid=(rows,),
        in_specs=[row_spec(length, pre.shape[1]), row_spec(length, K), pl.BlockSpec(gain.shape, lambda r: (0, 0)), row_spec(length, V)],
        out_specs=[row_spec(length, pre.shape[1]), row_spec(length, K), pl.BlockSpec(gain.shape, lambda r: (0, 0))],
        out_shape=[jax.ShapeDtypeStruct(pre.shape, BF), jax.ShapeDtypeStruct(logits.shape, F32), jax.ShapeDtypeStruct(gain.shape, F32)],
        compiler_params=PARAMS,
        cost_estimate=COST,
    )(pre, logits, gain, dgated)


def norm_back(dn, x, r, gain):
    t = dn * gain
    dx = t * r - x * (r * r * r * jnp.mean(t * x, axis=-1, keepdims=True))
    return dx, jnp.sum(dn * x * r, axis=0)


def exact_nt(a, b):
    return lax.dot_general(a, b, (((1,), (1,)), ((), ())), precision=lax.Precision.HIGHEST)


def project(x, w):
    r = lax.rsqrt(jnp.mean(x * x, axis=-1, keepdims=True) + 1e-6)
    n = (x * r * w["ag"]).astype(BF)
    pre = mm(n, w["WA"]).astype(BF)
    low = mm(n, w["rd"])
    logits = exact_nt(low, w["ru"]) + w["rb"]
    return dict(x=x, r=r, n=n, pre=pre, low=low, logits=logits)


def mix(m, w, rows):
    gated = mixer_fwd(m["pre"], m["logits"], w["gg"], rows, w["WO"].shape[0])
    return m["x"] + core_sum(mm(gated, w["WO"])), dict(m, gated=gated)


def expand(hidden, w):
    r = lax.rsqrt(jnp.mean(hidden * hidden, axis=-1, keepdims=True) + 1e-6)
    second = (hidden * r * w["mg"]).astype(BF)
    gu = mm(second, w["WF"]).astype(BF)
    return dict(hidden=hidden, r=r, second=second, gu=gu)


def contract(f, w, mask):
    gu = f["gu"]
    F = gu.shape[1] // 2
    gate, up = gu[:, :F].astype(F32), gu[:, F:].astype(F32)
    act = (gate * jax.nn.sigmoid(gate) * up).astype(BF)
    return (f["hidden"] + core_sum(mm(act, w["WD"]))) * mask, dict(f, act=act)


def column_halves(v, s):
    h = v.shape[1] // 2
    return lax.dynamic_slice_in_dim(v, s * h, h, 1), lax.dynamic_slice_in_dim(v, (1 - s) * h, h, 1)


def row_grads(rows_, cols, s):
    keep, give = column_halves(cols, s)
    got = over_core(mm_tn(rows_, give).astype(BF))
    return mm_tn(rows_, keep).astype(BF), got


def contract_back(dy, f, w):
    gu = f["gu"]
    F = gu.shape[1] // 2
    da = mm_nt(dy, w["WD"]).astype(BF).astype(F32)
    gate, up = gu[:, :F].astype(F32), gu[:, F:].astype(F32)
    sig = jax.nn.sigmoid(gate)
    return jnp.concatenate([da * up * (sig * (1.0 + gate * (1.0 - sig))), da * (gate * sig)], 1).astype(BF)


def expand_back(dy, dgu, f, w):
    dsec = core_sum(mm_nt(dgu, w["WF"])).astype(BF).astype(F32)
    back, d_mg = norm_back(dsec, f["hidden"], f["r"], w["mg"])
    return dy.astype(F32) + back, d_mg


def project_back(dhid, dpre, dlogits, d_gg, d_mg, m, w):
    dlow = jnp.matmul(dlogits, w["ru"], precision=lax.Precision.HIGHEST)
    dn = mm_nt(dpre, w["WA"]) + mm_nt(dlow, w["rd"])
    dn = core_sum(dn).astype(BF).astype(F32)
    dlow = core_sum(dlow)
    back, d_ag = norm_back(dn, m["x"], m["r"], w["ag"])
    small = dict(
        rd=mm_tn(m["n"], dlow),
        ru=mm_tn(dlogits, m["low"]),
        rb=jnp.sum(dlogits, axis=0),
        gg=d_gg[0],
        ag=d_ag,
        mg=d_mg,
    )
    return dhid + back, small


def body(
    inputs,
    lengths,
    out_grad,
    attn_gain,
    q_weight,
    k_weight,
    v_weight,
    rank_down,
    rank_up,
    rank_bias,
    gate_weight,
    group_gain,
    out_weight,
    mlp_gain,
    ffn_gate,
    ffn_up,
    ffn_down,
):
    size = lax.axis_size("dp")
    meshed = size == 16
    s = lax.axis_index("section")
    me = lax.axis_index("dp")
    at = jnp.stack([me // 4 % 4, (me // 2) % 2, me % 2, s]).astype(jnp.int32)
    first = s == 0
    shape = inputs.shape
    rows = shape[0] * shape[1]
    length, width = shape[2], shape[3]
    tokens = rows * length
    R = q_weight.shape[1]
    K, V, F, W = q_weight.shape[2] // 2, v_weight.shape[2] // 2, ffn_gate.shape[2] // 2, width // 2
    A = 2 * K + 2 * V
    rank = rank_down.shape[2]
    kc, gc = rank_bias.shape[1], group_gain.shape[1]
    ru_at = rank + 4
    links = Links()

    def paced(*values):
        if meshed:
            values = lax.optimization_barrier((values, links.meeting()))[0]
        return values if len(values) > 1 else values[0]

    cuts = cut_columns(
        [
            (q_weight, k_weight, v_weight, gate_weight, out_weight),
            (ffn_gate, ffn_up),
            (ffn_down,),
        ],
        (rank_down, attn_gain, mlp_gain, rank_bias, group_gain, rank_up),
        at,
    )

    def by_layer(pair):
        keep, give = pair
        got = over_core(give)
        return jnp.where(first, keep, got), jnp.where(first, got, keep)

    (keep, give), ff, down = cuts[0], by_layer(cuts[1]), by_layer(cuts[2])
    got = over_core(give)
    table = keep[:, A + W :] + got[:, A + W :]
    keep, got = keep[:, : A + W], got[:, : A + W]
    ao = (jnp.concatenate([jnp.where(first, keep, got), table], 1), jnp.where(first, got, keep))

    def whole(v):
        return lax.all_gather(v, "dp", axis=0, tiled=True)

    def own_rows(v):
        h = v.shape[0] // 2
        keep = lax.dynamic_slice_in_dim(v, s * h, h, 0)
        got = over_core(lax.dynamic_slice_in_dim(v, (1 - s) * h, h, 0))
        return jnp.where(first, jnp.concatenate([keep, got], 1), jnp.concatenate([got, keep], 1))

    if meshed:
        gA = [GatherWide(links, v) for v in ao]
        gF = [GatherWide(links, v) for v in ff]
        gD = [GatherWide(links, down[0]), GatherDown(links, down[1], at)]
    else:
        gA = gF = gD = [Idle(), Idle()]

    def place_ao(layer):
        if not meshed:
            v = whole(ao[layer])
            return v[:, :A], own_rows(v[:, A : A + W]), v[:, A + W :]
        columns = [(0, A, 0, 0), (A, A + W, 1, 0)]
        if ao[layer].shape[1] > A + W:
            columns.append((A + W, ao[layer].shape[1], 3, 0))
        out = place_blocks(gA[layer].parts(), columns, at, split=1)
        keep, give = out[1].reshape(width // 2, W), out[2].reshape(width // 2, W)
        WO = join_columns(keep, over_core(give), at)
        return out[0].reshape(width, A), WO, (out[3].reshape(width, -1) if len(out) > 3 else None)

    def place_ff(layer):
        if not meshed:
            return whole(ff[layer])
        return place_blocks(gF[layer].parts(), [(0, 2 * F, 0, 0)], at)[0].reshape(width, 2 * F)

    def place_down(layer):
        if not meshed:
            return own_rows(whole(down[layer]))
        if layer == 0:
            keep, give = place_blocks(gD[0].parts(), [(0, W, 0, 0)], at, split=0)
            keep, give = keep.reshape(-1, W), give.reshape(-1, W)
        else:
            v = gD[1].all
            h = v.shape[0] // 2
            keep = lax.dynamic_slice_in_dim(v, s * h, h, 0)
            give = lax.dynamic_slice_in_dim(v, (1 - s) * h, h, 0)
        return join_columns(keep, over_core(give), at)

    def unpack(table, layer):
        t = table[:, 64 * layer : 64 * layer + ru_at + rank]
        flat = t[:, rank:ru_at].astype(F32).T
        ru = t.reshape(size, R, -1)[:, :kc, ru_at:].reshape(size * kc, rank).astype(F32)
        rb = flat[2].reshape(size, R)[:, :kc].reshape(1, size * kc)
        return dict(
            rd=t[:, :rank],
            ag=flat[0:1],
            mg=flat[1:2],
            ru=lax.dynamic_slice_in_dim(ru, s * K, K, 0),
            rb=lax.dynamic_slice_in_dim(rb, s * K, K, 1),
            gg=flat[3].reshape(size, R)[:, :gc].reshape(1, size * gc),
        )

    spots = jnp.arange(length)
    mask = (spots[None, :] < lengths.reshape(rows, 1)).astype(F32).reshape(tokens, 1)
    low_mask = mask.astype(BF)
    x0 = inputs.reshape(tokens, width).astype(F32)

    gA[0].along(9), gD[1].around(), gF[0].along(9)
    if meshed:
        gA[1].along_with(gD[0], 3, gA[0].line)
    gA[0].sides(), gA[0].diag()
    WA0, WO0, table = place_ao(0)
    p0, p1 = unpack(table, 0), unpack(table, 1)
    w0 = dict(p0, WA=WA0, WO=WO0)
    gF[0].sides()
    if meshed:
        gF[1].along(2, gA[1].line)
    h0, m0 = mix(project(x0, w0), w0, rows)
    h0, m0, p1 = paced(h0, m0, p1)
    gF[0].diag()
    w0["WF"] = place_ff(0)
    gD[0].sides()
    f0 = paced(expand(h0, w0))
    gD[0].diag()
    if meshed:
        gD[1].along(3, gF[1].line)
    w0["WD"] = place_down(0)
    gA[1].sides()
    y0, f0 = paced(*contract(f0, w0, mask))
    x1 = y0.astype(BF)
    gA[1].diag()
    WA1, WO1, _ = place_ao(1)
    w1 = dict(p1, WA=WA1, WO=WO1)
    gF[1].sides()
    h1, m1 = mix(project(x1.astype(F32), w1), w1, rows)
    h1, m1 = paced(h1, m1)
    gF[1].diag()
    w1["WD"] = place_down(1)
    w1["WF"] = place_ff(1)
    f1 = expand(h1, w1)
    y1, f1 = contract(f1, w1, mask)
    layer_out = jnp.where(first, x1, y1.astype(BF)).reshape((1,) + shape)

    def all_rows(keep, got):
        return jnp.where(first, jnp.concatenate([keep, got], 0), jnp.concatenate([got, keep], 0))

    def scatter(v):
        return lax.psum_scatter(v, "dp", scatter_dimension=0, tiled=True)

    class Sum:
        def __init__(self, v):
            self.sum = scatter(v)

        def along(self, *a):
            pass

        sides = rest = along

    def sum_down(g):
        return ReduceDown(links, all_rows(*g), at) if meshed else Sum(all_rows(*g))

    def sum_ff(second, dgu):
        if meshed:
            return ReduceWide(links, grad_blocks(second, dgu, at))
        return Sum(mm_tn(second, dgu).astype(BF))

    def sum_ao(n, dpre, gO, packed=()):
        extras = gO + packed
        if meshed:
            return ReduceWide(links, grad_blocks(n, dpre, at, extras))
        return Sum(jnp.concatenate((mm_tn(n, dpre).astype(BF), all_rows(*gO)) + packed, 1))

    dy1 = out_grad.reshape(tokens, width) * low_mask
    gD1 = row_grads(f1["act"], dy1, s)
    rD1 = sum_down(gD1)
    dgu = contract_back(dy1, f1, w1)
    rF1 = sum_ff(f1["second"], dgu)
    rF1.sides(), rD1.along(3)
    if meshed:
        dgu = after(dgu, rF1.own)
    dh1, d_mg1 = expand_back(dy1, dgu, f1, w1)
    low = dh1.astype(BF)
    gO1 = row_grads(m1["gated"], low, s)
    back = mixer_bwd(m1["pre"], m1["logits"], w1["gg"], mm_nt(low, w1["WO"]).astype(BF), rows)
    dh1, d_mg1, gO1, back = paced(dh1, d_mg1, gO1, back)
    rF1.rest()
    rA1 = sum_ao(m1["n"], back[0], gO1)
    dx1, small1 = paced(*project_back(dh1, *back, d_mg1, m1, w1))
    rA1.sides(), rF1.along(3)
    dy0 = dx1.astype(BF) * low_mask
    gD0 = row_grads(f0["act"], dy0, s)
    dgu = contract_back(dy0, f0, w0)
    rF0 = sum_ff(f0["second"], dgu)
    rD0 = sum_down(gD0)
    rD0.along(9)
    dh0, d_mg0 = expand_back(dy0, dgu, f0, w0)
    if meshed:
        (rF0.own, rF0.Sx, rF0.Sy, rF0.Rx, rF0.Ry), dh0, d_mg0 = paced(
            (rF0.own, rF0.Sx, rF0.Sy, rF0.Rx, rF0.Ry), dh0, d_mg0
        )
    rA1.rest()
    low = dh0.astype(BF)
    gO0 = row_grads(m0["gated"], low, s)
    dgated, gO0, dh0 = paced(mm_nt(low, w0["WO"]).astype(BF), gO0, dh0)
    rF0.sides(), rA1.along(9)
    back = paced(mixer_bwd(m0["pre"], m0["logits"], w0["gg"], dgated, rows))
    rF0.rest()
    dx0, small0 = project_back(dh0, *back, d_mg0, m0, w0)
    dpre = back[0]
    mine = {k: jnp.where(first, small0[k], small1[k]) for k in small0}
    other = {k: over_core(jnp.where(first, small1[k], small0[k])) for k in ("ru", "rb", "gg")}
    ru = all_rows(mine["ru"], other["ru"])
    rb = all_rows(mine["rb"], other["rb"])

    def tall_blocks(v):
        v = v.reshape(size, v.shape[0] // size, -1)
        return jnp.pad(v, ((0, 0), (0, R - v.shape[1]), (0, 0))).reshape(size * R, -1)

    def long_blocks(v):
        v = v.reshape(size, -1)
        return jnp.pad(v, ((0, 0), (0, R - v.shape[1]))).reshape(size * R)

    flat = jnp.stack([mine["ag"], mine["mg"], long_blocks(rb), long_blocks(mine["gg"] + other["gg"])]).T
    packed = jnp.concatenate([mine["rd"], flat, tall_blocks(ru)], 1)
    packed = jnp.pad(packed, ((0, 0), (0, 128 - packed.shape[1]))).astype(BF)

    rA0 = sum_ao(m0["n"], dpre, gO0, (packed,))
    rA0.sides(), rF0.along(9)
    if meshed:
        links.before += [rA1.sum]
    rA0.rest()
    rA0.along(9)
    if meshed:
        links.before += [rF0.sum]
        around(links, (rD1, rD0))

    input_out = jnp.where(first, dx0, dx1).reshape((1,) + shape)

    def join(a, b, widths):
        keep = jnp.where(first, a, b)
        got = over_core(jnp.where(first, b, a))
        return finish(keep, got, widths, at)

    dD = join(rD0.sum, rD1.sum, (W,))[0]
    dFg, dFu = join(rF0.sum, rF1.sum, (F, F))
    dq, dk, dv, dg, dO = join(rA0.sum[:, : A + W], rA1.sum, (K, K, V, V, W))
    t = rA0.sum[:, A + W :].astype(F32)
    return (
        layer_out,
        input_out,
        t[:, rank][None],
        dq,
        dk,
        dv,
        t[:, :rank][None],
        t[:kc, ru_at : ru_at + rank].T[None],
        t[:kc, rank + 2][None],
        dg,
        t[:gc, rank + 3][None],
        dO,
        t[:, rank + 1][None],
        dFg,
        dFu,
        dD,
    )


def solution(mesh):
    rows3 = P("section", "dp", None)
    one = P("section", "dp")
    return jax.shard_map(
        body,
        mesh=mesh,
        in_specs=(
            P(None, "dp", None, None),
            P(None, "dp"),
            P(None, "dp", None, None),
            one,
            rows3,
            rows3,
            rows3,
            rows3,
            P("section", None, "dp"),
            one,
            rows3,
            one,
            rows3,
            one,
            rows3,
            rows3,
            rows3,
        ),
        out_specs=(
            P("section", None, "dp", None, None),
            P("section", None, "dp", None, None),
            one,
            rows3,
            rows3,
            rows3,
            rows3,
            P("section", None, "dp"),
            one,
            rows3,
            one,
            rows3,
            one,
            rows3,
            rows3,
            rows3,
        ),
        check_vma=False,
    )
```

```python
from functools import partial

import jax
import jax.numpy as jnp
from jax import lax
from jax.experimental import pallas as pl
from jax.experimental.pallas import tpu as pltpu
from jax.sharding import PartitionSpec as P

SPAN = 64
BF = jnp.bfloat16
F32 = jnp.float32
PARAMS = pltpu.CompilerParams(vmem_limit_bytes=20 << 20)
FULL = pltpu.CompilerParams(vmem_limit_bytes=60 << 20)
COST = pl.CostEstimate(flops=0, bytes_accessed=0, transcendentals=0)


def mm(a, b):
    return lax.dot_general(
        a.astype(BF), b.astype(BF), (((1,), (0,)), ((), ())), preferred_element_type=F32
    )


def mm_nt(a, b):
    return lax.dot_general(
        a.astype(BF), b.astype(BF), (((1,), (1,)), ((), ())), preferred_element_type=F32
    )


def mm_tn(a, b):
    return lax.dot_general(
        a.astype(BF), b.astype(BF), (((0,), (0,)), ((), ())), preferred_element_type=F32
    )


def after(value, *tokens):
    return lax.optimization_barrier((value,) + tokens)[0]


def copy_call(kernel, at, ins, in_specs, outs, out_specs, grid, params=None):
    return pl.pallas_call(
        kernel,
        grid_spec=pltpu.PrefetchScalarGridSpec(
            num_scalar_prefetch=1, grid=grid, in_specs=in_specs, out_specs=out_specs
        ),
        out_shape=[jax.ShapeDtypeStruct(o, BF) for o in outs],
        compiler_params=params or PARAMS,
        cost_estimate=COST,
    )(at, *ins)


def table_block(s, rd, ag, mg, rb, gg, ru):
    R, rank = rd.shape

    def one_hot(n, at):
        i = lax.broadcasted_iota(jnp.int32, (n, 128), 0)
        return jnp.where(i + at + 64 * s == lax.broadcasted_iota(jnp.int32, (n, 128), 1), 1.0, 0.0)

    def upright(row):
        n = row.shape[1]
        i = lax.broadcasted_iota(jnp.int32, (R, n), 0)
        return mm_nt(jnp.where(i == lax.broadcasted_iota(jnp.int32, (R, n), 1), 1.0, 0.0), row)

    out = mm(rd, one_hot(rank, 0)) + mm(upright(ru), one_hot(rank, rank + 4))
    for k, row in enumerate((ag, mg, rb, gg)):
        out = out + mm(upright(jnp.broadcast_to(row, (8, row.shape[1]))), one_hot(8, rank + k)[0:1] * (
            lax.broadcasted_iota(jnp.int32, (8, 1), 0) == 0
        ).astype(F32))
    return out.astype(BF)


def cut_kernel(groups, at_ref, *refs):
    n = sum(len(g) for g in groups)
    ins, smalls, outs = refs[:n], refs[n : n + 6], refs[n + 6 :]
    s = at_ref[3]
    k = 0
    for g, _ in enumerate(groups):
        to = 0
        for _ in groups[g]:
            h = ins[k].shape[2] // 2
            for o, half in ((2 * g, s), (2 * g + 1, 1 - s)):
                outs[o][:, to : to + h] = ins[k][0, :, pl.ds(pl.multiple_of(half * h, h), h)]
            to += h
            k += 1
        if g == 0:
            rd, ag, mg, rb, gg, ru = smalls
            table = table_block(s, rd[0], ag[...], mg[...], rb[...], gg[...], ru[0])
            outs[0][:, to:] = table
            outs[1][:, to:] = table


def cut_columns(groups, smalls, at):
    ins = [v for g in groups for v in g] + list(smalls)
    in_specs = [pl.BlockSpec(v.shape, lambda i, a, d=v.ndim: (0,) * d) for v in ins]
    outs = []
    for g, arrays in enumerate(groups):
        C = sum(v.shape[2] for v in arrays) // 2 + (128 if g == 0 else 0)
        outs += [(arrays[0].shape[1], C)] * 2
    out_specs = [pl.BlockSpec(o, lambda i, a: (0, 0)) for o in outs]
    out = copy_call(partial(cut_kernel, groups), at, ins, in_specs, outs, out_specs, (1,), FULL)
    return [(out[2 * g], out[2 * g + 1]) for g in range(len(groups))]


def join_kernel(at_ref, keep_ref, got_ref, out_ref):
    W = keep_ref.shape[1]
    s = at_ref[3]
    out_ref[:, pl.ds(pl.multiple_of(s * W, W), W)] = keep_ref[...]
    out_ref[:, pl.ds(pl.multiple_of((1 - s) * W, W), W)] = got_ref[...]


def join_columns(keep, got, at):
    H, W = keep.shape
    n = H // 4
    spec = pl.BlockSpec((n, W), lambda i, a: (i, 0))
    out = pl.BlockSpec((n, 2 * W), lambda i, a: (i, 0))
    return copy_call(join_kernel, at, [keep, got], [spec, spec], [(H, 2 * W)], [out], (4,))[0]


def pairs(dz, dy, dx):
    return [
        (z * 4 + y * 2 + x, ((z + dz) % 4) * 4 + (y ^ dy) * 2 + (x ^ dx))
        for z in range(4)
        for y in range(2)
        for x in range(2)
    ]


LINES = [[z * 4 + y * 2 + x for z in range(4)] for y in range(2) for x in range(2)]


class Links:
    def __init__(self):
        self.sent = {"x": [], "y": []}
        self.open, self.before = [], []

    def hop(self, name, v, step):
        sent = self.sent[name]
        if sent:
            v = after(v, sent[-1], *self.before)
        sent.append(lax.ppermute(v, "dp", pairs(*step)))
        return sent[-1]

    def x(self, v):
        return self.hop("x", v, (0, 0, 1))

    def y(self, v):
        return self.hop("y", v, (0, 1, 0))

    def gather(self, v, due):
        v = lax.all_gather(v, "dp", axis=0, tiled=True, axis_index_groups=LINES)
        self.open.append([due, v])
        return v

    def scatter(self, v, due):
        self.before.append(v)
        v = lax.psum_scatter(v, "dp", scatter_dimension=0, tiled=True, axis_index_groups=LINES)
        self.open.append([due, v])
        return v

    def meeting(self):
        tokens = self.sent["x"][-1:] + self.sent["y"][-1:]
        for entry in self.open:
            entry[0] -= 1
            if entry[0] == 0:
                tokens.append(entry[1])
        return tokens


def over_core(v):
    return lax.ppermute(v, "section", [(0, 1), (1, 0)])


def core_sum(v):
    v = v.astype(BF)
    return v.astype(F32) + over_core(v).astype(F32)


def add(a, b):
    return (a.astype(F32) + b.astype(F32)).astype(BF)


def ring(pz, v):
    slabs = [v]
    for _ in range(3):
        slabs.append(pz(slabs[-1]))
    return slabs


BLOCKS = ((0, 0), (0, 1), (1, 0), (1, 1))


class Idle:
    def __getattr__(self, name):
        return lambda *a: None


class GatherWide:
    def __init__(self, links, shard):
        self.links, self.shard = links, shard

    def along(self, due, *tokens):
        v = after(self.shard, *tokens) if tokens else self.shard
        self.line = self.links.gather(v, due).reshape((4,) + self.shard.shape)

    def along_with(self, other, due, *tokens):
        R, C = self.shard.shape
        v = after(jnp.concatenate([self.shard, other.shard.reshape(R, -1)], 1), *tokens)
        v = self.links.gather(v, due)
        v = v.reshape(4, R, -1)
        self.line = v[:, :, :C]
        other.line = v[:, :, C:].reshape((4,) + other.shard.shape)

    def sides(self):
        self.X, self.Y = self.links.x(self.line), self.links.y(self.line)

    def diag(self):
        self.hi, self.lo = self.links.x(self.Y[2:]), self.links.y(self.X[:2])

    def parts(self):
        return [self.line, self.X, self.Y, self.lo, self.hi]


def plane_of(j, a):
    return (2 * a[3] + j) % 4


def place_kernel(columns, split, n_out, at_ref, *refs):
    ins, outs = refs[:-n_out], refs[-n_out:]
    j = pl.program_id(0)
    y, x = at_ref[1], at_ref[2]

    def write(lo, hi, o, to):
        for (yy, xx), v in zip(BLOCKS, ins[:3]):
            outs[o][0, y ^ yy, x ^ xx, :, to : to + hi - lo] = v[0, :, lo:hi]

        @pl.when(plane_of(j, at_ref) < 2)
        def _():
            outs[o][0, 1 - y, 1 - x, :, to : to + hi - lo] = ins[3][0, :, lo:hi]

        @pl.when(plane_of(j, at_ref) >= 2)
        def _():
            outs[o][0, 1 - y, 1 - x, :, to : to + hi - lo] = ins[4][0, :, lo:hi]

    for lo, hi, o, to in columns:
        if o == split:
            pl.when(j < 2)(partial(write, lo, hi, o, to))
            pl.when(j >= 2)(partial(write, lo, hi, o + 1, to))
        else:
            write(lo, hi, o, to)


def place_blocks(ins, columns, at, split=None):
    _, R, _ = ins[0].shape
    width = {}
    for lo, hi, o, to in columns:
        width[o] = max(width.get(o, 0), to + hi - lo)
    if split is not None:
        width[split + 1] = width[split]
    shapes, specs = [], []
    for o in sorted(width):
        block = (1, 2, 2, R, width[o])
        if split is not None and o == split:
            shapes.append((2,) + block[1:])
            specs.append(pl.BlockSpec(block, lambda j, a: (jnp.minimum(j, 1), 0, 0, 0, 0)))
        elif split is not None and o == split + 1:
            shapes.append((2,) + block[1:])
            specs.append(pl.BlockSpec(block, lambda j, a: (jnp.maximum(j, 2) - 2, 0, 0, 0, 0)))
        else:
            shapes.append((4,) + block[1:])
            specs.append(pl.BlockSpec(block, lambda j, a: (plane_of(j, a), 0, 0, 0, 0)))
    in_specs = [pl.BlockSpec((1,) + v.shape[1:], lambda j, a: (plane_of(j, a), 0, 0)) for v in ins[:3]]
    in_specs += [pl.BlockSpec((1,) + v.shape[1:], lambda j, a: (plane_of(j, a) % 2, 0, 0)) for v in ins[3:]]
    return copy_call(
        partial(place_kernel, columns, split, len(shapes)), at, ins, in_specs, shapes, specs, (4,)
    )


class GatherDown:
    def __init__(self, links, shard, at):
        self.links, self.shard, self.at = links, shard, at

    def around(self):
        v, links = self.shard, self.links
        R, C = v.shape
        h = C // 2
        y, x = self.at[1], self.at[2]
        X, Y = links.x(v), links.y(v)
        D2, D1 = links.x(Y[:, h:]), links.y(X[:, :h])
        out = jnp.zeros((2, 2, R, C), BF)
        for b, p, c in ((0, v, 0), (1, X, 0), (2, Y, 0), (3, D1, 0), (3, D2, h)):
            yy, xx = BLOCKS[b]
            out = lax.dynamic_update_slice(out, p[None, None], (y ^ yy, x ^ xx, 0, c))
        self.block = out.reshape(4 * R, C)

    def along(self, due, *tokens):
        self.all = self.links.gather(after(self.block, *tokens), due)


def grad_kernel(R, at_ref, lhs_ref, rhs_ref, *refs):
    acc = refs[-1]
    extras, (own, Sx, Sy, Rx, Ry) = refs[:-6], refs[-6:-1]
    C = rhs_ref.shape[1]
    acc[:, :C] = mm_tn(lhs_ref[...], rhs_ref[...])
    i = pl.program_id(0)
    y, x, s = at_ref[1], at_ref[2], at_ref[3]
    if extras:
        keep, got = extras[0][...].astype(F32), extras[1][...].astype(F32)
        W = keep.shape[1]
        acc[:, C : C + W] = jnp.where((i // 2) == s, keep, got)
        if len(extras) > 2:
            acc[:, C + W :] = extras[2][...].astype(F32)

    def block(b):
        yy, xx = BLOCKS[b]
        return acc[pl.ds(pl.multiple_of(((y ^ yy) * 2 + (x ^ xx)) * R, R), R), :].astype(BF)

    own[0] = block(0)

    @pl.when(i < 2)
    def _():
        Sx[0, 0] = block(3)
        Sx[1, 0] = block(1)
        Ry[0] = block(2)

    @pl.when(i >= 2)
    def _():
        Sy[0, 0] = block(3)
        Sy[1, 0] = block(2)
        Rx[0] = block(1)


def grad_blocks(lhs, rhs, at, extras=()):
    tokens, D = lhs.shape
    C = rhs.shape[1] + sum(e.shape[1] for e in extras[:1] + extras[2:])
    n = D // 4
    R = n // 4
    in_specs = [
        pl.BlockSpec((tokens, n), lambda i, a: (0, i)),
        pl.BlockSpec(rhs.shape, lambda i, a: (0, 0)),
    ]
    for k, e in enumerate(extras):
        if k < 2:
            in_specs.append(pl.BlockSpec((n, e.shape[1]), lambda i, a: (i % 2, 0)))
        else:
            in_specs.append(pl.BlockSpec((n, e.shape[1]), lambda i, a: (i, 0)))
    pair = (2, 1, R, C)
    return pl.pallas_call(
        partial(grad_kernel, R),
        grid_spec=pltpu.PrefetchScalarGridSpec(
            num_scalar_prefetch=1,
            grid=(4,),
            in_specs=in_specs,
            out_specs=[
                pl.BlockSpec((1, R, C), lambda i, a: (i, 0, 0)),
                pl.BlockSpec(pair, lambda i, a: (0, jnp.minimum(i, 1), 0, 0)),
                pl.BlockSpec(pair, lambda i, a: (0, jnp.maximum(i, 2) - 2, 0, 0)),
                pl.BlockSpec((1, R, C), lambda i, a: (jnp.maximum(i, 2) - 2, 0, 0)),
                pl.BlockSpec((1, R, C), lambda i, a: (jnp.minimum(i, 1), 0, 0)),
            ],
            scratch_shapes=[pltpu.VMEM((n, C), F32)],
        ),
        out_shape=[
            jax.ShapeDtypeStruct(v, BF)
            for v in ((4, R, C), (2, 2, R, C), (2, 2, R, C), (2, R, C), (2, R, C))
        ],
        compiler_params=PARAMS,
    )(at, lhs, rhs, *extras)


def slab_kernel(own, gx, gy, tx, ty, out):
    i = pl.program_id(0)

    @pl.when(i < 2)
    def _():
        out[...] = (own[0].astype(F32) + gx[0, 0].astype(F32) + ty[0].astype(F32)).astype(BF)

    @pl.when(i >= 2)
    def _():
        out[...] = (own[0].astype(F32) + gy[0, 0].astype(F32) + tx[0].astype(F32)).astype(BF)


def sum_slabs(own, gx, gy, tx, ty):
    _, R, C = own.shape
    low = lambda i: jnp.minimum(i, 1)
    high = lambda i: jnp.maximum(i, 2) - 2
    return pl.pallas_call(
        slab_kernel,
        grid=(4,),
        in_specs=[
            pl.BlockSpec((1, R, C), lambda i: (i, 0, 0)),
            pl.BlockSpec((1, 1, R, C), lambda i: (1, low(i), 0, 0)),
            pl.BlockSpec((1, 1, R, C), lambda i: (1, high(i), 0, 0)),
            pl.BlockSpec((1, R, C), lambda i: (high(i), 0, 0)),
            pl.BlockSpec((1, R, C), lambda i: (low(i), 0, 0)),
        ],
        out_specs=pl.BlockSpec((R, C), lambda i: (i, 0)),
        out_shape=jax.ShapeDtypeStruct((4 * R, C), BF),
        compiler_params=PARAMS,
    )(own, gx, gy, tx, ty)


def total(*parts):
    t = parts[0].astype(F32)
    for v in parts[1:]:
        t = t + v.astype(F32)
    return t.astype(BF)


class ReduceWide:
    def __init__(self, links, blocks):
        self.links = links
        self.own, self.Sx, self.Sy, self.Rx, self.Ry = blocks

    def sides(self):
        self.gx, self.gy = self.links.x(self.Sx), self.links.y(self.Sy)

    def rest(self):
        self.last = add(self.Rx, self.gy[0]), add(self.Ry, self.gx[0])
        self.tx, self.ty = self.links.x(self.last[0]), self.links.y(self.last[1])

    def along(self, due):
        self.sum = self.links.scatter(sum_slabs(self.own, self.gx, self.gy, self.tx, self.ty), due)


class ReduceDown:
    def __init__(self, links, v, at):
        self.links, self.v, self.at = links, v, at

    def along(self, due):
        self.sum = self.links.scatter(self.v, due)

    def pick(self, b, lo, hi):
        yy, xx = BLOCKS[b]
        R = self.sum.shape[0] // 4
        v = self.sum.reshape(2, 2, R, -1)
        y, x = self.at[1], self.at[2]
        return lax.dynamic_slice(v, (y ^ yy, x ^ xx, 0, lo), (1, 1, R, hi - lo)).reshape(R, hi - lo)


def around(links, parts):
    C = parts[0].sum.shape[1]
    h = C // 2

    def pick(b, lo, hi):
        return jnp.concatenate([p.pick(b, lo, hi) for p in parts], 0)

    r1, r2 = links.x(pick(3, 0, h)), links.y(pick(3, h, C))
    a1, b2 = links.x(pick(1, 0, h)), links.y(pick(2, h, C))
    a2 = links.x(add(pick(1, h, C), r2))
    b1 = links.y(add(pick(2, 0, h), r1))
    v = jnp.concatenate([total(pick(0, 0, h), a1, b1), total(pick(0, h, C), a2, b2)], 1)
    R = v.shape[0] // len(parts)
    for n, p in enumerate(parts):
        p.sum = v[n * R : (n + 1) * R]


def finish_kernel(widths, at_ref, keep_ref, got_ref, *outs):
    s = at_ref[3]
    to = 0
    for w, out in zip(widths, outs):
        out[0, :, pl.ds(pl.multiple_of(s * w, w), w)] = keep_ref[:, to : to + w].astype(F32)
        out[0, :, pl.ds(pl.multiple_of((1 - s) * w, w), w)] = got_ref[:, to : to + w].astype(F32)
        to += w


def finish(keep, got, widths, at):
    R = keep.shape[0]
    return pl.pallas_call(
        partial(finish_kernel, widths),
        grid_spec=pltpu.PrefetchScalarGridSpec(
            num_scalar_prefetch=1,
            grid=(1,),
            in_specs=[pl.BlockSpec(keep.shape, lambda i, a: (0, 0))] * 2,
            out_specs=[pl.BlockSpec((1, R, 2 * w), lambda i, a: (0, 0, 0)) for w in widths],
        ),
        out_shape=[jax.ShapeDtypeStruct((1, R, 2 * w), F32) for w in widths],
        compiler_params=PARAMS,
    )(at, keep, got)


def causal(length):
    i = lax.broadcasted_iota(jnp.int32, (length, length), 0)
    j = lax.broadcasted_iota(jnp.int32, (length, length), 1)
    return (i >= j) & (i // SPAN == j // SPAN)

def sum_parts(ones, v, axis):
    high = v.astype(BF)
    rest = v - high.astype(F32)
    middle = rest.astype(BF)
    low = (rest - middle.astype(F32)).astype(BF)
    dims = (((axis,), (0,)), ((), ()))
    dot = partial(lax.dot_general, dimension_numbers=dims, preferred_element_type=F32)
    return dot(ones, high) + (dot(ones, middle) + dot(ones, low))


def head_state(pre, logits, h, K, V, heads, keep):
    kh, vh = K // heads, V // heads
    length = pre.shape[0]
    q = pre[:, h * kh : (h + 1) * kh].astype(F32)
    k = pre[:, K + h * kh : K + (h + 1) * kh].astype(F32)
    v = pre[:, 2 * K + h * vh : 2 * K + (h + 1) * vh]
    x = logits[:, h * kh : (h + 1) * kh]
    a = (jnp.minimum(x, 0.0) - jnp.log1p(jnp.exp(-jnp.abs(x)))) * (1.0 / 16.0)
    tri = jnp.where(keep, 1.0, 0.0).astype(BF)
    b = sum_parts(tri, a, 1)
    n = length // SPAN
    lasts = [b[(i + 1) * SPAN - 1 : (i + 1) * SPAN] for i in range(n)]
    last = jnp.concatenate([jnp.broadcast_to(t, (SPAN, kh)) for t in lasts], 0)
    eb = jnp.exp(b)
    enb = jnp.exp(-b)
    elb = jnp.exp(last - b)
    qs = q * (kh ** -0.5) * eb
    ks = k * enb
    kc = k * elb
    qs_l, ks_l, kc_l = qs.astype(BF), ks.astype(BF), kc.astype(BF)
    sc = jnp.where(keep, mm_nt(qs_l, ks_l), 0.0).astype(BF)
    local = mm(sc, v)
    states, decs, outs = [], [], []
    S = jnp.zeros((vh, kh), F32)
    for i in range(n):
        at = slice(i * SPAN, (i + 1) * SPAN)
        states.append(S)
        decs.append(jnp.exp(lasts[i]))
        o = local[at]
        if i:
            o = o + mm_nt(qs_l[at], S)
        outs.append(o)
        if i < n - 1:
            S = S * decs[i] + mm_tn(v[at], kc_l[at])
    return dict(q=q, k=k, v=v, x=x, eb=eb, enb=enb, elb=elb, qs=qs, ks=ks, kc=kc, qs_l=qs_l, ks_l=ks_l,
                kc_l=kc_l, sc=sc, states=states, decs=decs, out=jnp.concatenate(outs, 0))

def mixer_fwd_kernel(K, V, heads, pre_ref, logits_ref, gain_ref, out_ref):
    pre, logits, gain = pre_ref[...], logits_ref[...], gain_ref[...]
    keep = causal(pre.shape[0])
    vh = V // heads
    for h in range(heads):
        o = head_state(pre, logits, h, K, V, heads, keep)["out"]
        g = pre[:, 2 * K + V + h * vh : 2 * K + V + (h + 1) * vh].astype(F32)
        o = o * lax.rsqrt(jnp.mean(o * o, axis=-1, keepdims=True) + 1e-5) * gain
        out_ref[:, h * vh : (h + 1) * vh] = (o * (g * jax.nn.sigmoid(g))).astype(BF)

def mixer_bwd_kernel(K, V, heads, pre_ref, logits_ref, gain_ref, dg_ref, dpre_ref, dlog_ref, dgain_ref):
    pre, logits, gain = pre_ref[...], logits_ref[...], gain_ref[...]
    keep = causal(pre.shape[0])
    length = pre.shape[0]
    kh, vh = K // heads, V // heads
    n = length // SPAN
    dgain = jnp.zeros((1, vh), F32)
    for h in range(heads):
        st = head_state(pre, logits, h, K, V, heads, keep)
        out, v = st["out"], st["v"]
        g = pre[:, 2 * K + V + h * vh : 2 * K + V + (h + 1) * vh].astype(F32)
        dgated = dg_ref[:, h * vh : (h + 1) * vh].astype(F32)
        r = lax.rsqrt(jnp.mean(out * out, axis=-1, keepdims=True) + 1e-5)
        sg = jax.nn.sigmoid(g)
        on = out * r
        dgate = dgated * (on * gain) * (sg * (1.0 + g * (1.0 - sg)))
        dm = dgated * (g * sg)
        dgain = dgain + jnp.sum(dm * on, axis=0, keepdims=True)
        t = dm * gain
        dO = (t * r - on * (r * r * jnp.mean(t * out, axis=-1, keepdims=True))).astype(BF)
        dsc = jnp.where(keep, mm_nt(dO, v), 0.0).astype(BF)
        dv = mm_tn(st["sc"], dO)
        dqs = mm(dsc, st["ks_l"])
        dks = mm_tn(dsc, st["qs_l"])
        dqs_c, dkc, dv_c, dlast = [None] * n, [None] * n, [None] * n, [None] * n
        T = None
        for i in range(n - 1, -1, -1):
            at = slice(i * SPAN, (i + 1) * SPAN)
            if i:
                dqs_c[i] = mm(dO[at], st["states"][i])
            else:
                dqs_c[i] = jnp.zeros((SPAN, kh), F32)
            if T is None:
                dkc[i] = jnp.zeros((SPAN, kh), F32)
                dv_c[i] = jnp.zeros((SPAN, vh), F32)
                dlast[i] = jnp.zeros((SPAN, kh), F32)
            else:
                T_l = T.astype(BF)
                dkc[i] = mm(v[at], T_l)
                dv_c[i] = mm_nt(st["kc_l"][at], T_l)
                dl = jnp.sum(dkc[i] * st["kc"][at], axis=0, keepdims=True)
                if i:
                    dl = dl + jnp.sum(T * st["states"][i], axis=0, keepdims=True) * st["decs"][i]
                dlast[i] = jnp.broadcast_to(dl, (SPAN, kh))
            if i:
                new = mm_tn(dO[at], st["qs_l"][at])
                T = new if T is None else T * st["decs"][i] + new
        dqs = dqs + jnp.concatenate(dqs_c, 0)
        dkc = jnp.concatenate(dkc, 0)
        dv = dv + jnp.concatenate(dv_c, 0)
        db = dqs * st["qs"] - dks * st["ks"] - dkc * st["kc"]
        tri = jnp.where(keep, 1.0, 0.0).astype(BF)
        da = sum_parts(tri, db, 0)
        da = da + jnp.concatenate(dlast, 0)
        x = st["x"]
        dlog_ref[:, h * kh : (h + 1) * kh] = da * (1.0 / 16.0) * (1.0 - jax.nn.sigmoid(x))
        dpre_ref[:, h * kh : (h + 1) * kh] = (dqs * (kh ** -0.5) * st["eb"]).astype(BF)
        dpre_ref[:, K + h * kh : K + (h + 1) * kh] = (dks * st["enb"] + dkc * st["elb"]).astype(BF)
        dpre_ref[:, 2 * K + h * vh : 2 * K + (h + 1) * vh] = dv.astype(BF)
        dpre_ref[:, 2 * K + V + h * vh : 2 * K + V + (h + 1) * vh] = dgate.astype(BF)
    @pl.when(pl.program_id(0) == 0)
    def _():
        dgain_ref[...] = jnp.zeros_like(dgain_ref)
    dgain_ref[...] += dgain

def row_spec(length, cols):
    return pl.BlockSpec((length, cols), lambda r: (r, 0))
def mixer_fwd(pre, logits, gain, rows, V):
    tokens, K = logits.shape
    length = tokens // rows
    heads = V // gain.shape[1]
    return pl.pallas_call(
        partial(mixer_fwd_kernel, K, V, heads),
        grid=(rows,),
        in_specs=[row_spec(length, pre.shape[1]), row_spec(length, K), pl.BlockSpec(gain.shape, lambda r: (0, 0))],
        out_specs=row_spec(length, V),
        out_shape=jax.ShapeDtypeStruct((tokens, V), BF),
        compiler_params=PARAMS,
        cost_estimate=COST,
    )(pre, logits, gain)
def mixer_bwd(pre, logits, gain, dgated, rows):
    tokens, K = logits.shape
    V = dgated.shape[1]
    length = tokens // rows
    heads = V // gain.shape[1]
    return pl.pallas_call(
        partial(mixer_bwd_kernel, K, V, heads),
        grid=(rows,),
        in_specs=[row_spec(length, pre.shape[1]), row_spec(length, K), pl.BlockSpec(gain.shape, lambda r: (0, 0)), row_spec(length, V)],
        out_specs=[row_spec(length, pre.shape[1]), row_spec(length, K), pl.BlockSpec(gain.shape, lambda r: (0, 0))],
        out_shape=[jax.ShapeDtypeStruct(pre.shape, BF), jax.ShapeDtypeStruct(logits.shape, F32), jax.ShapeDtypeStruct(gain.shape, F32)],
        compiler_params=PARAMS,
        cost_estimate=COST,
    )(pre, logits, gain, dgated)


def norm_back(dn, x, r, gain):
    t = dn * gain
    dx = t * r - x * (r * r * r * jnp.mean(t * x, axis=-1, keepdims=True))
    return dx, jnp.sum(dn * x * r, axis=0)


def exact_nt(a, b):
    return lax.dot_general(a, b, (((1,), (1,)), ((), ())), precision=lax.Precision.HIGHEST)


def project(x, w):
    r = lax.rsqrt(jnp.mean(x * x, axis=-1, keepdims=True) + 1e-6)
    n = (x * r * w["ag"]).astype(BF)
    pre = mm(n, w["WA"]).astype(BF)
    low = mm(n, w["rd"])
    logits = exact_nt(low, w["ru"]) + w["rb"]
    return dict(x=x, r=r, n=n, pre=pre, low=low, logits=logits)


def mix(m, w, rows):
    gated = mixer_fwd(m["pre"], m["logits"], w["gg"], rows, w["WO"].shape[0])
    return m["x"] + core_sum(mm(gated, w["WO"])), dict(m, gated=gated)


def expand(hidden, w):
    r = lax.rsqrt(jnp.mean(hidden * hidden, axis=-1, keepdims=True) + 1e-6)
    second = (hidden * r * w["mg"]).astype(BF)
    gu = mm(second, w["WF"]).astype(BF)
    return dict(hidden=hidden, r=r, second=second, gu=gu)


def activate(f):
    gu = f["gu"]
    F = gu.shape[1] // 2
    gate, up = gu[:, :F].astype(F32), gu[:, F:].astype(F32)
    return dict(f, act=(gate * jax.nn.sigmoid(gate) * up).astype(BF))


def contract(f, w, mask):
    f = activate(f)
    return (f["hidden"] + core_sum(mm(f["act"], w["WD"]))) * mask, f


def column_halves(v, s):
    h = v.shape[1] // 2
    return lax.dynamic_slice_in_dim(v, s * h, h, 1), lax.dynamic_slice_in_dim(v, (1 - s) * h, h, 1)


def row_grads(rows_, cols, s):
    keep, give = column_halves(cols, s)
    got = over_core(mm_tn(rows_, give).astype(BF))
    return mm_tn(rows_, keep).astype(BF), got


def contract_back(dy, f, w):
    gu = f["gu"]
    F = gu.shape[1] // 2
    da = mm_nt(dy, w["WD"]).astype(BF).astype(F32)
    gate, up = gu[:, :F].astype(F32), gu[:, F:].astype(F32)
    sig = jax.nn.sigmoid(gate)
    return jnp.concatenate([da * up * (sig * (1.0 + gate * (1.0 - sig))), da * (gate * sig)], 1).astype(BF)


def expand_back(dy, dgu, f, w):
    dsec = core_sum(mm_nt(dgu, w["WF"])).astype(BF).astype(F32)
    back, d_mg = norm_back(dsec, f["hidden"], f["r"], w["mg"])
    return dy.astype(F32) + back, d_mg


def project_back(dhid, dpre, dlogits, d_gg, d_mg, m, w):
    dlow = jnp.matmul(dlogits, w["ru"], precision=lax.Precision.HIGHEST)
    dn = mm_nt(dpre, w["WA"]) + mm_nt(dlow, w["rd"])
    dn = core_sum(dn).astype(BF).astype(F32)
    dlow = core_sum(dlow)
    back, d_ag = norm_back(dn, m["x"], m["r"], w["ag"])
    small = dict(
        rd=mm_tn(m["n"], dlow),
        ru=mm_tn(dlogits, m["low"]),
        rb=jnp.sum(dlogits, axis=0),
        gg=d_gg[0],
        ag=d_ag,
        mg=d_mg,
    )
    return dhid + back, small


def body(
    inputs,
    lengths,
    out_grad,
    attn_gain,
    q_weight,
    k_weight,
    v_weight,
    rank_down,
    rank_up,
    rank_bias,
    gate_weight,
    group_gain,
    out_weight,
    mlp_gain,
    ffn_gate,
    ffn_up,
    ffn_down,
):
    size = lax.axis_size("dp")
    meshed = size == 16
    s = lax.axis_index("section")
    me = lax.axis_index("dp")
    at = jnp.stack([me // 4 % 4, (me // 2) % 2, me % 2, s]).astype(jnp.int32)
    first = s == 0
    shape = inputs.shape
    rows = shape[0] * shape[1]
    length, width = shape[2], shape[3]
    tokens = rows * length
    R = q_weight.shape[1]
    K, V, F, W = q_weight.shape[2] // 2, v_weight.shape[2] // 2, ffn_gate.shape[2] // 2, width // 2
    A = 2 * K + 2 * V
    rank = rank_down.shape[2]
    kc, gc = rank_bias.shape[1], group_gain.shape[1]
    ru_at = rank + 4
    links = Links()

    def paced(*values):
        if meshed:
            values = lax.optimization_barrier((values, links.meeting()))[0]
        return values if len(values) > 1 else values[0]

    cuts = cut_columns(
        [
            (q_weight, k_weight, v_weight, gate_weight, out_weight),
            (ffn_gate, ffn_up),
            (ffn_down,),
        ],
        (rank_down, attn_gain, mlp_gain, rank_bias, group_gain, rank_up),
        at,
    )

    def by_layer(pair):
        keep, give = pair
        got = over_core(give)
        return jnp.where(first, keep, got), jnp.where(first, got, keep)

    (keep, give), ff, down = cuts[0], by_layer(cuts[1]), by_layer(cuts[2])
    got = over_core(give)
    table = keep[:, A + W :] + got[:, A + W :]
    keep, got = keep[:, : A + W], got[:, : A + W]
    ao = (jnp.concatenate([jnp.where(first, keep, got), table], 1), jnp.where(first, got, keep))

    def whole(v):
        return lax.all_gather(v, "dp", axis=0, tiled=True)

    def own_rows(v):
        h = v.shape[0] // 2
        keep = lax.dynamic_slice_in_dim(v, s * h, h, 0)
        got = over_core(lax.dynamic_slice_in_dim(v, (1 - s) * h, h, 0))
        return jnp.where(first, jnp.concatenate([keep, got], 1), jnp.concatenate([got, keep], 1))

    if meshed:
        gA = [GatherWide(links, v) for v in ao]
        gF = [GatherWide(links, v) for v in ff]
        gD = [GatherWide(links, down[0]), GatherDown(links, down[1], at)]
    else:
        gA = gF = gD = [Idle(), Idle()]

    def place_ao(layer):
        if not meshed:
            v = whole(ao[layer])
            return v[:, :A], own_rows(v[:, A : A + W]), v[:, A + W :]
        columns = [(0, A, 0, 0), (A, A + W, 1, 0)]
        if ao[layer].shape[1] > A + W:
            columns.append((A + W, ao[layer].shape[1], 3, 0))
        out = place_blocks(gA[layer].parts(), columns, at, split=1)
        keep, give = out[1].reshape(width // 2, W), out[2].reshape(width // 2, W)
        WO = join_columns(keep, over_core(give), at)
        return out[0].reshape(width, A), WO, (out[3].reshape(width, -1) if len(out) > 3 else None)

    def place_ff(layer):
        if not meshed:
            return whole(ff[layer])
        return place_blocks(gF[layer].parts(), [(0, 2 * F, 0, 0)], at)[0].reshape(width, 2 * F)

    def place_down(layer):
        if not meshed:
            return own_rows(whole(down[layer]))
        if layer == 0:
            keep, give = place_blocks(gD[0].parts(), [(0, W, 0, 0)], at, split=0)
            keep, give = keep.reshape(-1, W), give.reshape(-1, W)
        else:
            v = gD[1].all
            h = v.shape[0] // 2
            keep = lax.dynamic_slice_in_dim(v, s * h, h, 0)
            give = lax.dynamic_slice_in_dim(v, (1 - s) * h, h, 0)
        return join_columns(keep, over_core(give), at)

    def unpack(table, layer):
        t = table[:, 64 * layer : 64 * layer + ru_at + rank]
        flat = t[:, rank:ru_at].astype(F32).T
        ru = t.reshape(size, R, -1)[:, :kc, ru_at:].reshape(size * kc, rank).astype(F32)
        rb = flat[2].reshape(size, R)[:, :kc].reshape(1, size * kc)
        return dict(
            rd=t[:, :rank],
            ag=flat[0:1],
            mg=flat[1:2],
            ru=lax.dynamic_slice_in_dim(ru, s * K, K, 0),
            rb=lax.dynamic_slice_in_dim(rb, s * K, K, 1),
            gg=flat[3].reshape(size, R)[:, :gc].reshape(1, size * gc),
        )

    spots = jnp.arange(length)
    mask = (spots[None, :] < lengths.reshape(rows, 1)).astype(F32).reshape(tokens, 1)
    low_mask = mask.astype(BF)
    x0 = inputs.reshape(tokens, width).astype(F32)

    gA[0].along(9), gD[1].around(), gF[0].along(9)
    if meshed:
        gA[1].along_with(gD[0], 3, gA[0].line)
    gA[0].sides(), gA[0].diag()
    WA0, WO0, table = place_ao(0)
    p0, p1 = unpack(table, 0), unpack(table, 1)
    w0 = dict(p0, WA=WA0, WO=WO0)
    gF[0].sides()
    if meshed:
        gF[1].along(2, gA[1].line)
    h0, m0 = mix(project(x0, w0), w0, rows)
    h0, m0, p1 = paced(h0, m0, p1)
    gF[0].diag()
    w0["WF"] = place_ff(0)
    gD[0].sides()
    f0 = paced(expand(h0, w0))
    gD[0].diag()
    if meshed:
        gD[1].along(3, gF[1].line)
    w0["WD"] = place_down(0)
    gA[1].sides()
    y0, f0 = paced(*contract(f0, w0, mask))
    x1 = y0.astype(BF)
    gA[1].diag()
    WA1, WO1, _ = place_ao(1)
    w1 = dict(p1, WA=WA1, WO=WO1)
    gF[1].sides()
    h1, m1 = mix(project(x1.astype(F32), w1), w1, rows)
    h1, m1 = paced(h1, m1)
    gF[1].diag()
    w1["WD"] = place_down(1)
    w1["WF"] = place_ff(1)
    f1 = expand(h1, w1)
    f1 = activate(f1)

    def all_rows(keep, got):
        return jnp.where(first, jnp.concatenate([keep, got], 0), jnp.concatenate([got, keep], 0))

    def scatter(v):
        return lax.psum_scatter(v, "dp", scatter_dimension=0, tiled=True)

    class Sum:
        def __init__(self, v):
            self.sum = scatter(v)

        def along(self, *a):
            pass

        sides = rest = along

    def sum_down(g):
        return ReduceDown(links, all_rows(*g), at) if meshed else Sum(all_rows(*g))

    def sum_ff(second, dgu):
        if meshed:
            return ReduceWide(links, grad_blocks(second, dgu, at))
        return Sum(mm_tn(second, dgu).astype(BF))

    def sum_ao(n, dpre, gO, packed=()):
        extras = gO + packed
        if meshed:
            return ReduceWide(links, grad_blocks(n, dpre, at, extras))
        return Sum(jnp.concatenate((mm_tn(n, dpre).astype(BF), all_rows(*gO)) + packed, 1))

    dy1 = out_grad.reshape(tokens, width) * low_mask
    gD1 = row_grads(f1["act"], dy1, s)
    rD1 = sum_down(gD1)
    dgu = contract_back(dy1, f1, w1)
    rF1 = sum_ff(f1["second"], dgu)
    rF1.sides(), rD1.along(3)
    if meshed:
        dgu = after(dgu, rF1.own)
    dh1, d_mg1 = expand_back(dy1, dgu, f1, w1)
    low = dh1.astype(BF)
    gO1 = row_grads(m1["gated"], low, s)
    back = mixer_bwd(m1["pre"], m1["logits"], w1["gg"], mm_nt(low, w1["WO"]).astype(BF), rows)
    act = after(f1["act"], dh1) if meshed else f1["act"]
    y1 = (f1["hidden"] + core_sum(mm(act, w1["WD"]))) * mask
    y1, dh1, d_mg1, gO1, back = paced(y1, dh1, d_mg1, gO1, back)
    if meshed:
        links.before += [y1]
    rF1.rest()
    rA1 = sum_ao(m1["n"], back[0], gO1)
    dx1, small1 = paced(*project_back(dh1, *back, d_mg1, m1, w1))
    rA1.sides(), rF1.along(3)
    dy0 = dx1.astype(BF) * low_mask
    gD0 = row_grads(f0["act"], dy0, s)
    dgu = contract_back(dy0, f0, w0)
    rF0 = sum_ff(f0["second"], dgu)
    rD0 = sum_down(gD0)
    rD0.along(9)
    dh0, d_mg0 = expand_back(dy0, dgu, f0, w0)
    if meshed:
        (rF0.own, rF0.Sx, rF0.Sy, rF0.Rx, rF0.Ry), dh0, d_mg0 = paced(
            (rF0.own, rF0.Sx, rF0.Sy, rF0.Rx, rF0.Ry), dh0, d_mg0
        )
    rA1.rest()
    low = dh0.astype(BF)
    gO0 = row_grads(m0["gated"], low, s)
    dgated, gO0, dh0 = paced(mm_nt(low, w0["WO"]).astype(BF), gO0, dh0)
    if meshed:
        rA1.own = after(rA1.own, rF0.own)
    rF0.sides(), rA1.along(9)
    back = paced(mixer_bwd(m0["pre"], m0["logits"], w0["gg"], dgated, rows))
    rF0.rest()
    dx0, small0 = project_back(dh0, *back, d_mg0, m0, w0)
    dpre = back[0]
    mine = {k: jnp.where(first, small0[k], small1[k]) for k in small0}
    other = {k: over_core(jnp.where(first, small1[k], small0[k])) for k in ("ru", "rb", "gg")}
    ru = all_rows(mine["ru"], other["ru"])
    rb = all_rows(mine["rb"], other["rb"])

    def tall_blocks(v):
        v = v.reshape(size, v.shape[0] // size, -1)
        return jnp.pad(v, ((0, 0), (0, R - v.shape[1]), (0, 0))).reshape(size * R, -1)

    def long_blocks(v):
        v = v.reshape(size, -1)
        return jnp.pad(v, ((0, 0), (0, R - v.shape[1]))).reshape(size * R)

    flat = jnp.stack([mine["ag"], mine["mg"], long_blocks(rb), long_blocks(mine["gg"] + other["gg"])]).T
    packed = jnp.concatenate([mine["rd"], flat, tall_blocks(ru)], 1)
    packed = jnp.pad(packed, ((0, 0), (0, 128 - packed.shape[1]))).astype(BF)

    rA0 = sum_ao(m0["n"], dpre, gO0, (packed,))
    rA0.sides(), rF0.along(9)
    if meshed:
        links.before += [rA1.sum]
    rA0.rest()
    rA0.along(9)
    if meshed:
        links.before += [rF0.sum]
        around(links, (rD1, rD0))

    input_out = jnp.where(first, dx0, dx1).reshape((1,) + shape)
    layer_out = jnp.where(first, x1, y1.astype(BF)).reshape((1,) + shape)

    def join(a, b, widths):
        keep = jnp.where(first, a, b)
        got = over_core(jnp.where(first, b, a))
        return finish(keep, got, widths, at)

    dD = join(rD0.sum, rD1.sum, (W,))[0]
    dFg, dFu = join(rF0.sum, rF1.sum, (F, F))
    dq, dk, dv, dg, dO = join(rA0.sum[:, : A + W], rA1.sum, (K, K, V, V, W))
    t = rA0.sum[:, A + W :].astype(F32)
    return (
        layer_out,
        input_out,
        t[:, rank][None],
        dq,
        dk,
        dv,
        t[:, :rank][None],
        t[:kc, ru_at : ru_at + rank].T[None],
        t[:kc, rank + 2][None],
        dg,
        t[:gc, rank + 3][None],
        dO,
        t[:, rank + 1][None],
        dFg,
        dFu,
        dD,
    )


def solution(mesh):
    rows3 = P("section", "dp", None)
    one = P("section", "dp")
    return jax.shard_map(
        body,
        mesh=mesh,
        in_specs=(
            P(None, "dp", None, None),
            P(None, "dp"),
            P(None, "dp", None, None),
            one,
            rows3,
            rows3,
            rows3,
            rows3,
            P("section", None, "dp"),
            one,
            rows3,
            one,
            rows3,
            one,
            rows3,
            rows3,
            rows3,
        ),
        out_specs=(
            P("section", None, "dp", None, None),
            P("section", None, "dp", None, None),
            one,
            rows3,
            rows3,
            rows3,
            rows3,
            P("section", None, "dp"),
            one,
            rows3,
            one,
            rows3,
            one,
            rows3,
            rows3,
            rows3,
        ),
        check_vma=False,
    )
```

```python
from functools import partial

import jax
import jax.numpy as jnp
from jax import lax
from jax.experimental import pallas as pl
from jax.experimental.pallas import tpu as pltpu
from jax.sharding import PartitionSpec as P

SPAN = 64
BF = jnp.bfloat16
F32 = jnp.float32
PARAMS = pltpu.CompilerParams(vmem_limit_bytes=20 << 20)
FULL = pltpu.CompilerParams(vmem_limit_bytes=60 << 20)
COST = pl.CostEstimate(flops=0, bytes_accessed=0, transcendentals=0)


def mm(a, b):
    return lax.dot_general(
        a.astype(BF), b.astype(BF), (((1,), (0,)), ((), ())), preferred_element_type=F32
    )


def mm_nt(a, b):
    return lax.dot_general(
        a.astype(BF), b.astype(BF), (((1,), (1,)), ((), ())), preferred_element_type=F32
    )


def mm_tn(a, b):
    return lax.dot_general(
        a.astype(BF), b.astype(BF), (((0,), (0,)), ((), ())), preferred_element_type=F32
    )


def after(value, *tokens):
    return lax.optimization_barrier((value,) + tokens)[0]


def copy_call(kernel, at, ins, in_specs, outs, out_specs, grid, params=None):
    return pl.pallas_call(
        kernel,
        grid_spec=pltpu.PrefetchScalarGridSpec(
            num_scalar_prefetch=1, grid=grid, in_specs=in_specs, out_specs=out_specs
        ),
        out_shape=[jax.ShapeDtypeStruct(o, BF) for o in outs],
        compiler_params=params or PARAMS,
        cost_estimate=COST,
    )(at, *ins)


def table_block(s, rd, ag, mg, rb, gg, ru):
    R, rank = rd.shape

    def one_hot(n, at):
        i = lax.broadcasted_iota(jnp.int32, (n, 128), 0)
        return jnp.where(i + at + 64 * s == lax.broadcasted_iota(jnp.int32, (n, 128), 1), 1.0, 0.0)

    def upright(row):
        n = row.shape[1]
        i = lax.broadcasted_iota(jnp.int32, (R, n), 0)
        return mm_nt(jnp.where(i == lax.broadcasted_iota(jnp.int32, (R, n), 1), 1.0, 0.0), row)

    out = mm(rd, one_hot(rank, 0)) + mm(upright(ru), one_hot(rank, rank + 4))
    for k, row in enumerate((ag, mg, rb, gg)):
        out = out + mm(upright(jnp.broadcast_to(row, (8, row.shape[1]))), one_hot(8, rank + k)[0:1] * (
            lax.broadcasted_iota(jnp.int32, (8, 1), 0) == 0
        ).astype(F32))
    return out.astype(BF)


def cut_kernel(groups, at_ref, *refs):
    n = sum(len(g) for g in groups)
    ins, smalls, outs = refs[:n], refs[n : n + 6], refs[n + 6 :]
    s = at_ref[3]
    k = 0
    for g, _ in enumerate(groups):
        to = 0
        for _ in groups[g]:
            h = ins[k].shape[2] // 2
            for o, half in ((2 * g, s), (2 * g + 1, 1 - s)):
                outs[o][:, to : to + h] = ins[k][0, :, pl.ds(pl.multiple_of(half * h, h), h)]
            to += h
            k += 1
        if g == 0:
            rd, ag, mg, rb, gg, ru = smalls
            table = table_block(s, rd[0], ag[...], mg[...], rb[...], gg[...], ru[0])
            outs[0][:, to:] = table
            outs[1][:, to:] = table


def cut_columns(groups, smalls, at):
    ins = [v for g in groups for v in g] + list(smalls)
    in_specs = [pl.BlockSpec(v.shape, lambda i, a, d=v.ndim: (0,) * d) for v in ins]
    outs = []
    for g, arrays in enumerate(groups):
        C = sum(v.shape[2] for v in arrays) // 2 + (128 if g == 0 else 0)
        outs += [(arrays[0].shape[1], C)] * 2
    out_specs = [pl.BlockSpec(o, lambda i, a: (0, 0)) for o in outs]
    out = copy_call(partial(cut_kernel, groups), at, ins, in_specs, outs, out_specs, (1,), FULL)
    return [(out[2 * g], out[2 * g + 1]) for g in range(len(groups))]


def join_kernel(at_ref, keep_ref, got_ref, out_ref):
    W = keep_ref.shape[1]
    s = at_ref[3]
    out_ref[:, pl.ds(pl.multiple_of(s * W, W), W)] = keep_ref[...]
    out_ref[:, pl.ds(pl.multiple_of((1 - s) * W, W), W)] = got_ref[...]


def join_columns(keep, got, at):
    H, W = keep.shape
    n = H // 4
    spec = pl.BlockSpec((n, W), lambda i, a: (i, 0))
    out = pl.BlockSpec((n, 2 * W), lambda i, a: (i, 0))
    return copy_call(join_kernel, at, [keep, got], [spec, spec], [(H, 2 * W)], [out], (4,))[0]


def pairs(dz, dy, dx):
    return [
        (z * 4 + y * 2 + x, ((z + dz) % 4) * 4 + (y ^ dy) * 2 + (x ^ dx))
        for z in range(4)
        for y in range(2)
        for x in range(2)
    ]


LINES = [[z * 4 + y * 2 + x for z in range(4)] for y in range(2) for x in range(2)]


class Links:
    def __init__(self):
        self.sent = {"x": [], "y": []}
        self.open, self.before = [], []

    def hop(self, name, v, step):
        sent = self.sent[name]
        if sent:
            v = after(v, sent[-1], *self.before)
        sent.append(lax.ppermute(v, "dp", pairs(*step)))
        return sent[-1]

    def x(self, v):
        return self.hop("x", v, (0, 0, 1))

    def y(self, v):
        return self.hop("y", v, (0, 1, 0))

    def gather(self, v, due):
        v = lax.all_gather(v, "dp", axis=0, tiled=True, axis_index_groups=LINES)
        self.open.append([due, v])
        return v

    def scatter(self, v, due):
        self.before.append(v)
        v = lax.psum_scatter(v, "dp", scatter_dimension=0, tiled=True, axis_index_groups=LINES)
        self.open.append([due, v])
        return v

    def meeting(self):
        tokens = self.sent["x"][-1:] + self.sent["y"][-1:]
        for entry in self.open:
            entry[0] -= 1
            if entry[0] == 0:
                tokens.append(entry[1])
        return tokens


def over_core(v):
    return lax.ppermute(v, "section", [(0, 1), (1, 0)])


def core_sum(v):
    v = v.astype(BF)
    return v.astype(F32) + over_core(v).astype(F32)


def add(a, b):
    return (a.astype(F32) + b.astype(F32)).astype(BF)


def ring(pz, v):
    slabs = [v]
    for _ in range(3):
        slabs.append(pz(slabs[-1]))
    return slabs


BLOCKS = ((0, 0), (0, 1), (1, 0), (1, 1))


class Idle:
    def __getattr__(self, name):
        return lambda *a: None


class GatherWide:
    def __init__(self, links, shard):
        self.links, self.shard = links, shard

    def along(self, due, *tokens):
        v = after(self.shard, *tokens) if tokens else self.shard
        self.line = self.links.gather(v, due).reshape((4,) + self.shard.shape)

    def along_with(self, other, due, *tokens):
        R, C = self.shard.shape
        v = after(jnp.concatenate([self.shard, other.shard.reshape(R, -1)], 1), *tokens)
        v = self.links.gather(v, due)
        v = v.reshape(4, R, -1)
        self.line = v[:, :, :C]
        other.line = v[:, :, C:].reshape((4,) + other.shard.shape)

    def sides(self):
        self.X, self.Y = self.links.x(self.line), self.links.y(self.line)

    def diag(self):
        self.hi, self.lo = self.links.x(self.Y[2:]), self.links.y(self.X[:2])

    def parts(self):
        return [self.line, self.X, self.Y, self.lo, self.hi]


def plane_of(j, a):
    return (2 * a[3] + j) % 4


def place_kernel(columns, split, n_out, at_ref, *refs):
    ins, outs = refs[:-n_out], refs[-n_out:]
    j = pl.program_id(0)
    y, x = at_ref[1], at_ref[2]

    def write(lo, hi, o, to):
        for (yy, xx), v in zip(BLOCKS, ins[:3]):
            outs[o][0, y ^ yy, x ^ xx, :, to : to + hi - lo] = v[0, :, lo:hi]

        @pl.when(plane_of(j, at_ref) < 2)
        def _():
            outs[o][0, 1 - y, 1 - x, :, to : to + hi - lo] = ins[3][0, :, lo:hi]

        @pl.when(plane_of(j, at_ref) >= 2)
        def _():
            outs[o][0, 1 - y, 1 - x, :, to : to + hi - lo] = ins[4][0, :, lo:hi]

    for lo, hi, o, to in columns:
        if o == split:
            pl.when(j < 2)(partial(write, lo, hi, o, to))
            pl.when(j >= 2)(partial(write, lo, hi, o + 1, to))
        else:
            write(lo, hi, o, to)


def place_blocks(ins, columns, at, split=None):
    _, R, _ = ins[0].shape
    width = {}
    for lo, hi, o, to in columns:
        width[o] = max(width.get(o, 0), to + hi - lo)
    if split is not None:
        width[split + 1] = width[split]
    shapes, specs = [], []
    for o in sorted(width):
        block = (1, 2, 2, R, width[o])
        if split is not None and o == split:
            shapes.append((2,) + block[1:])
            specs.append(pl.BlockSpec(block, lambda j, a: (jnp.minimum(j, 1), 0, 0, 0, 0)))
        elif split is not None and o == split + 1:
            shapes.append((2,) + block[1:])
            specs.append(pl.BlockSpec(block, lambda j, a: (jnp.maximum(j, 2) - 2, 0, 0, 0, 0)))
        else:
            shapes.append((4,) + block[1:])
            specs.append(pl.BlockSpec(block, lambda j, a: (plane_of(j, a), 0, 0, 0, 0)))
    in_specs = [pl.BlockSpec((1,) + v.shape[1:], lambda j, a: (plane_of(j, a), 0, 0)) for v in ins[:3]]
    in_specs += [pl.BlockSpec((1,) + v.shape[1:], lambda j, a: (plane_of(j, a) % 2, 0, 0)) for v in ins[3:]]
    return copy_call(
        partial(place_kernel, columns, split, len(shapes)), at, ins, in_specs, shapes, specs, (4,)
    )


class GatherDown:
    def __init__(self, links, shard, at):
        self.links, self.shard, self.at = links, shard, at

    def around(self):
        v, links = self.shard, self.links
        R, C = v.shape
        h = C // 2
        y, x = self.at[1], self.at[2]
        X, Y = links.x(v), links.y(v)
        D2, D1 = links.x(Y[:, h:]), links.y(X[:, :h])
        out = jnp.zeros((2, 2, R, C), BF)
        for b, p, c in ((0, v, 0), (1, X, 0), (2, Y, 0), (3, D1, 0), (3, D2, h)):
            yy, xx = BLOCKS[b]
            out = lax.dynamic_update_slice(out, p[None, None], (y ^ yy, x ^ xx, 0, c))
        self.block = out.reshape(4 * R, C)

    def along(self, due, *tokens):
        self.all = self.links.gather(after(self.block, *tokens), due)


def grad_kernel(R, at_ref, lhs_ref, rhs_ref, *refs):
    acc = refs[-1]
    extras, (own, Sx, Sy, Rx, Ry) = refs[:-6], refs[-6:-1]
    C = rhs_ref.shape[1]
    acc[:, :C] = mm_tn(lhs_ref[...], rhs_ref[...])
    i = pl.program_id(0)
    y, x, s = at_ref[1], at_ref[2], at_ref[3]
    if extras:
        keep, got = extras[0][...].astype(F32), extras[1][...].astype(F32)
        W = keep.shape[1]
        acc[:, C : C + W] = jnp.where((i // 2) == s, keep, got)
        if len(extras) > 2:
            acc[:, C + W :] = extras[2][...].astype(F32)

    def block(b):
        yy, xx = BLOCKS[b]
        return acc[pl.ds(pl.multiple_of(((y ^ yy) * 2 + (x ^ xx)) * R, R), R), :].astype(BF)

    own[0] = block(0)

    @pl.when(i < 2)
    def _():
        Sx[0, 0] = block(3)
        Sx[1, 0] = block(1)
        Ry[0] = block(2)

    @pl.when(i >= 2)
    def _():
        Sy[0, 0] = block(3)
        Sy[1, 0] = block(2)
        Rx[0] = block(1)


def grad_blocks(lhs, rhs, at, extras=()):
    tokens, D = lhs.shape
    C = rhs.shape[1] + sum(e.shape[1] for e in extras[:1] + extras[2:])
    n = D // 4
    R = n // 4
    in_specs = [
        pl.BlockSpec((tokens, n), lambda i, a: (0, i)),
        pl.BlockSpec(rhs.shape, lambda i, a: (0, 0)),
    ]
    for k, e in enumerate(extras):
        if k < 2:
            in_specs.append(pl.BlockSpec((n, e.shape[1]), lambda i, a: (i % 2, 0)))
        else:
            in_specs.append(pl.BlockSpec((n, e.shape[1]), lambda i, a: (i, 0)))
    pair = (2, 1, R, C)
    return pl.pallas_call(
        partial(grad_kernel, R),
        grid_spec=pltpu.PrefetchScalarGridSpec(
            num_scalar_prefetch=1,
            grid=(4,),
            in_specs=in_specs,
            out_specs=[
                pl.BlockSpec((1, R, C), lambda i, a: (i, 0, 0)),
                pl.BlockSpec(pair, lambda i, a: (0, jnp.minimum(i, 1), 0, 0)),
                pl.BlockSpec(pair, lambda i, a: (0, jnp.maximum(i, 2) - 2, 0, 0)),
                pl.BlockSpec((1, R, C), lambda i, a: (jnp.maximum(i, 2) - 2, 0, 0)),
                pl.BlockSpec((1, R, C), lambda i, a: (jnp.minimum(i, 1), 0, 0)),
            ],
            scratch_shapes=[pltpu.VMEM((n, C), F32)],
        ),
        out_shape=[
            jax.ShapeDtypeStruct(v, BF)
            for v in ((4, R, C), (2, 2, R, C), (2, 2, R, C), (2, R, C), (2, R, C))
        ],
        compiler_params=PARAMS,
    )(at, lhs, rhs, *extras)


def slab_kernel(own, gx, gy, tx, ty, out):
    i = pl.program_id(0)

    @pl.when(i < 2)
    def _():
        out[...] = (own[0].astype(F32) + gx[0, 0].astype(F32) + ty[0].astype(F32)).astype(BF)

    @pl.when(i >= 2)
    def _():
        out[...] = (own[0].astype(F32) + gy[0, 0].astype(F32) + tx[0].astype(F32)).astype(BF)


def sum_slabs(own, gx, gy, tx, ty):
    _, R, C = own.shape
    low = lambda i: jnp.minimum(i, 1)
    high = lambda i: jnp.maximum(i, 2) - 2
    return pl.pallas_call(
        slab_kernel,
        grid=(4,),
        in_specs=[
            pl.BlockSpec((1, R, C), lambda i: (i, 0, 0)),
            pl.BlockSpec((1, 1, R, C), lambda i: (1, low(i), 0, 0)),
            pl.BlockSpec((1, 1, R, C), lambda i: (1, high(i), 0, 0)),
            pl.BlockSpec((1, R, C), lambda i: (high(i), 0, 0)),
            pl.BlockSpec((1, R, C), lambda i: (low(i), 0, 0)),
        ],
        out_specs=pl.BlockSpec((R, C), lambda i: (i, 0)),
        out_shape=jax.ShapeDtypeStruct((4 * R, C), BF),
        compiler_params=PARAMS,
    )(own, gx, gy, tx, ty)


def total(*parts):
    t = parts[0].astype(F32)
    for v in parts[1:]:
        t = t + v.astype(F32)
    return t.astype(BF)


class ReduceWide:
    def __init__(self, links, blocks):
        self.links = links
        self.own, self.Sx, self.Sy, self.Rx, self.Ry = blocks

    def sides(self):
        self.gx, self.gy = self.links.x(self.Sx), self.links.y(self.Sy)

    def rest(self):
        self.last = add(self.Rx, self.gy[0]), add(self.Ry, self.gx[0])
        self.tx, self.ty = self.links.x(self.last[0]), self.links.y(self.last[1])

    def along(self, due):
        self.sum = self.links.scatter(sum_slabs(self.own, self.gx, self.gy, self.tx, self.ty), due)


class ReduceDown:
    def __init__(self, links, v, at):
        self.links, self.v, self.at = links, v, at

    def along(self, due):
        self.sum = self.links.scatter(self.v, due)

    def pick(self, b, lo, hi):
        yy, xx = BLOCKS[b]
        R = self.sum.shape[0] // 4
        v = self.sum.reshape(2, 2, R, -1)
        y, x = self.at[1], self.at[2]
        return lax.dynamic_slice(v, (y ^ yy, x ^ xx, 0, lo), (1, 1, R, hi - lo)).reshape(R, hi - lo)


def around(links, parts):
    C = parts[0].sum.shape[1]
    h = C // 2

    def pick(b, lo, hi):
        return jnp.concatenate([p.pick(b, lo, hi) for p in parts], 0)

    r1, r2 = links.x(pick(3, 0, h)), links.y(pick(3, h, C))
    a1, b2 = links.x(pick(1, 0, h)), links.y(pick(2, h, C))
    a2 = links.x(add(pick(1, h, C), r2))
    b1 = links.y(add(pick(2, 0, h), r1))
    v = jnp.concatenate([total(pick(0, 0, h), a1, b1), total(pick(0, h, C), a2, b2)], 1)
    R = v.shape[0] // len(parts)
    for n, p in enumerate(parts):
        p.sum = v[n * R : (n + 1) * R]


def finish_kernel(widths, at_ref, first_ref, second_ref, got_ref, *outs):
    s = at_ref[3]
    to = 0
    for w, out in zip(widths, outs):
        keep = jnp.where(s == 0, first_ref[:, to : to + w].astype(F32), second_ref[:, to : to + w].astype(F32))
        out[0, :, pl.ds(pl.multiple_of(s * w, w), w)] = keep
        out[0, :, pl.ds(pl.multiple_of((1 - s) * w, w), w)] = got_ref[:, to : to + w].astype(F32)
        to += w


def finish(a, b, got, widths, at):
    R = got.shape[0]
    return pl.pallas_call(
        partial(finish_kernel, widths),
        grid_spec=pltpu.PrefetchScalarGridSpec(
            num_scalar_prefetch=1,
            grid=(1,),
            in_specs=[pl.BlockSpec(v.shape, lambda i, a: (0, 0)) for v in (a, b, got)],
            out_specs=[pl.BlockSpec((1, R, 2 * w), lambda i, a: (0, 0, 0)) for w in widths],
        ),
        out_shape=[jax.ShapeDtypeStruct((1, R, 2 * w), F32) for w in widths],
        compiler_params=PARAMS,
    )(at, a, b, got)


def causal(length):
    i = lax.broadcasted_iota(jnp.int32, (length, length), 0)
    j = lax.broadcasted_iota(jnp.int32, (length, length), 1)
    return (i >= j) & (i // SPAN == j // SPAN)

def sum_parts(ones, v, axis):
    high = v.astype(BF)
    rest = v - high.astype(F32)
    middle = rest.astype(BF)
    low = (rest - middle.astype(F32)).astype(BF)
    dims = (((axis,), (0,)), ((), ()))
    dot = partial(lax.dot_general, dimension_numbers=dims, preferred_element_type=F32)
    return dot(ones, high) + (dot(ones, middle) + dot(ones, low))


def head_state(pre, logits, h, K, V, heads, keep):
    kh, vh = K // heads, V // heads
    length = pre.shape[0]
    q = pre[:, h * kh : (h + 1) * kh].astype(F32)
    k = pre[:, K + h * kh : K + (h + 1) * kh].astype(F32)
    v = pre[:, 2 * K + h * vh : 2 * K + (h + 1) * vh]
    x = logits[:, h * kh : (h + 1) * kh]
    a = (jnp.minimum(x, 0.0) - jnp.log1p(jnp.exp(-jnp.abs(x)))) * (1.0 / 16.0)
    tri = jnp.where(keep, 1.0, 0.0).astype(BF)
    b = sum_parts(tri, a, 1)
    n = length // SPAN
    lasts = [b[(i + 1) * SPAN - 1 : (i + 1) * SPAN] for i in range(n)]
    last = jnp.concatenate([jnp.broadcast_to(t, (SPAN, kh)) for t in lasts], 0)
    eb = jnp.exp(b)
    enb = jnp.exp(-b)
    elb = jnp.exp(last - b)
    qs = q * (kh ** -0.5) * eb
    ks = k * enb
    kc = k * elb
    qs_l, ks_l, kc_l = qs.astype(BF), ks.astype(BF), kc.astype(BF)
    sc = jnp.where(keep, mm_nt(qs_l, ks_l), 0.0).astype(BF)
    local = mm(sc, v)
    states, decs, outs = [], [], []
    S = jnp.zeros((vh, kh), F32)
    for i in range(n):
        at = slice(i * SPAN, (i + 1) * SPAN)
        states.append(S)
        decs.append(jnp.exp(lasts[i]))
        o = local[at]
        if i:
            o = o + mm_nt(qs_l[at], S)
        outs.append(o)
        if i < n - 1:
            S = S * decs[i] + mm_tn(v[at], kc_l[at])
    return dict(q=q, k=k, v=v, x=x, eb=eb, enb=enb, elb=elb, qs=qs, ks=ks, kc=kc, qs_l=qs_l, ks_l=ks_l,
                kc_l=kc_l, sc=sc, states=states, decs=decs, out=jnp.concatenate(outs, 0))

def mixer_fwd_kernel(K, V, heads, pre_ref, logits_ref, gain_ref, out_ref):
    pre, logits, gain = pre_ref[...], logits_ref[...], gain_ref[...]
    keep = causal(pre.shape[0])
    vh = V // heads
    for h in range(heads):
        o = head_state(pre, logits, h, K, V, heads, keep)["out"]
        g = pre[:, 2 * K + V + h * vh : 2 * K + V + (h + 1) * vh].astype(F32)
        o = o * lax.rsqrt(jnp.mean(o * o, axis=-1, keepdims=True) + 1e-5) * gain
        out_ref[:, h * vh : (h + 1) * vh] = (o * (g * jax.nn.sigmoid(g))).astype(BF)

def mixer_bwd_kernel(K, V, heads, pre_ref, logits_ref, gain_ref, dg_ref, dpre_ref, dlog_ref, dgain_ref):
    pre, logits, gain = pre_ref[...], logits_ref[...], gain_ref[...]
    keep = causal(pre.shape[0])
    length = pre.shape[0]
    kh, vh = K // heads, V // heads
    n = length // SPAN
    dgain = jnp.zeros((1, vh), F32)
    for h in range(heads):
        st = head_state(pre, logits, h, K, V, heads, keep)
        out, v = st["out"], st["v"]
        g = pre[:, 2 * K + V + h * vh : 2 * K + V + (h + 1) * vh].astype(F32)
        dgated = dg_ref[:, h * vh : (h + 1) * vh].astype(F32)
        r = lax.rsqrt(jnp.mean(out * out, axis=-1, keepdims=True) + 1e-5)
        sg = jax.nn.sigmoid(g)
        on = out * r
        dgate = dgated * (on * gain) * (sg * (1.0 + g * (1.0 - sg)))
        dm = dgated * (g * sg)
        dgain = dgain + jnp.sum(dm * on, axis=0, keepdims=True)
        t = dm * gain
        dO = (t * r - on * (r * r * jnp.mean(t * out, axis=-1, keepdims=True))).astype(BF)
        dsc = jnp.where(keep, mm_nt(dO, v), 0.0).astype(BF)
        dv = mm_tn(st["sc"], dO)
        dqs = mm(dsc, st["ks_l"])
        dks = mm_tn(dsc, st["qs_l"])
        dqs_c, dkc, dv_c, dlast = [None] * n, [None] * n, [None] * n, [None] * n
        T = None
        for i in range(n - 1, -1, -1):
            at = slice(i * SPAN, (i + 1) * SPAN)
            if i:
                dqs_c[i] = mm(dO[at], st["states"][i])
            else:
                dqs_c[i] = jnp.zeros((SPAN, kh), F32)
            if T is None:
                dkc[i] = jnp.zeros((SPAN, kh), F32)
                dv_c[i] = jnp.zeros((SPAN, vh), F32)
                dlast[i] = jnp.zeros((SPAN, kh), F32)
            else:
                T_l = T.astype(BF)
                dkc[i] = mm(v[at], T_l)
                dv_c[i] = mm_nt(st["kc_l"][at], T_l)
                dl = jnp.sum(dkc[i] * st["kc"][at], axis=0, keepdims=True)
                if i:
                    dl = dl + jnp.sum(T * st["states"][i], axis=0, keepdims=True) * st["decs"][i]
                dlast[i] = jnp.broadcast_to(dl, (SPAN, kh))
            if i:
                new = mm_tn(dO[at], st["qs_l"][at])
                T = new if T is None else T * st["decs"][i] + new
        dqs = dqs + jnp.concatenate(dqs_c, 0)
        dkc = jnp.concatenate(dkc, 0)
        dv = dv + jnp.concatenate(dv_c, 0)
        db = dqs * st["qs"] - dks * st["ks"] - dkc * st["kc"]
        tri = jnp.where(keep, 1.0, 0.0).astype(BF)
        da = sum_parts(tri, db, 0)
        da = da + jnp.concatenate(dlast, 0)
        x = st["x"]
        dlog_ref[:, h * kh : (h + 1) * kh] = da * (1.0 / 16.0) * (1.0 - jax.nn.sigmoid(x))
        dpre_ref[:, h * kh : (h + 1) * kh] = (dqs * (kh ** -0.5) * st["eb"]).astype(BF)
        dpre_ref[:, K + h * kh : K + (h + 1) * kh] = (dks * st["enb"] + dkc * st["elb"]).astype(BF)
        dpre_ref[:, 2 * K + h * vh : 2 * K + (h + 1) * vh] = dv.astype(BF)
        dpre_ref[:, 2 * K + V + h * vh : 2 * K + V + (h + 1) * vh] = dgate.astype(BF)
    @pl.when(pl.program_id(0) == 0)
    def _():
        dgain_ref[...] = jnp.zeros_like(dgain_ref)
    dgain_ref[...] += dgain

def row_spec(length, cols):
    return pl.BlockSpec((length, cols), lambda r: (r, 0))
def mixer_fwd(pre, logits, gain, rows, V):
    tokens, K = logits.shape
    length = tokens // rows
    heads = V // gain.shape[1]
    return pl.pallas_call(
        partial(mixer_fwd_kernel, K, V, heads),
        grid=(rows,),
        in_specs=[row_spec(length, pre.shape[1]), row_spec(length, K), pl.BlockSpec(gain.shape, lambda r: (0, 0))],
        out_specs=row_spec(length, V),
        out_shape=jax.ShapeDtypeStruct((tokens, V), BF),
        compiler_params=PARAMS,
        cost_estimate=COST,
    )(pre, logits, gain)
def mixer_bwd(pre, logits, gain, dgated, rows):
    tokens, K = logits.shape
    V = dgated.shape[1]
    length = tokens // rows
    heads = V // gain.shape[1]
    return pl.pallas_call(
        partial(mixer_bwd_kernel, K, V, heads),
        grid=(rows,),
        in_specs=[row_spec(length, pre.shape[1]), row_spec(length, K), pl.BlockSpec(gain.shape, lambda r: (0, 0)), row_spec(length, V)],
        out_specs=[row_spec(length, pre.shape[1]), row_spec(length, K), pl.BlockSpec(gain.shape, lambda r: (0, 0))],
        out_shape=[jax.ShapeDtypeStruct(pre.shape, BF), jax.ShapeDtypeStruct(logits.shape, F32), jax.ShapeDtypeStruct(gain.shape, F32)],
        compiler_params=PARAMS,
        cost_estimate=COST,
    )(pre, logits, gain, dgated)


def norm_back(dn, x, r, gain):
    t = dn * gain
    dx = t * r - x * (r * r * r * jnp.mean(t * x, axis=-1, keepdims=True))
    return dx, jnp.sum(dn * x * r, axis=0)


def exact_nt(a, b):
    return lax.dot_general(a, b, (((1,), (1,)), ((), ())), precision=lax.Precision.HIGHEST)


def project(x, w):
    r = lax.rsqrt(jnp.mean(x * x, axis=-1, keepdims=True) + 1e-6)
    n = (x * r * w["ag"]).astype(BF)
    pre = mm(n, w["WA"]).astype(BF)
    low = mm(n, w["rd"])
    logits = exact_nt(low, w["ru"]) + w["rb"]
    return dict(x=x, r=r, n=n, pre=pre, low=low, logits=logits)


def mix(m, w, rows):
    gated = mixer_fwd(m["pre"], m["logits"], w["gg"], rows, w["WO"].shape[0])
    return m["x"] + core_sum(mm(gated, w["WO"])), dict(m, gated=gated)


def expand(hidden, w):
    r = lax.rsqrt(jnp.mean(hidden * hidden, axis=-1, keepdims=True) + 1e-6)
    second = (hidden * r * w["mg"]).astype(BF)
    gu = mm(second, w["WF"]).astype(BF)
    return dict(hidden=hidden, r=r, second=second, gu=gu)


def activate(f):
    gu = f["gu"]
    F = gu.shape[1] // 2
    gate, up = gu[:, :F].astype(F32), gu[:, F:].astype(F32)
    return dict(f, act=(gate * jax.nn.sigmoid(gate) * up).astype(BF))


def contract(f, w, mask):
    f = activate(f)
    return (f["hidden"] + core_sum(mm(f["act"], w["WD"]))) * mask, f


def column_halves(v, s):
    h = v.shape[1] // 2
    return lax.dynamic_slice_in_dim(v, s * h, h, 1), lax.dynamic_slice_in_dim(v, (1 - s) * h, h, 1)


def row_grads(rows_, cols, s):
    keep, give = column_halves(cols, s)
    got = over_core(mm_tn(rows_, give).astype(BF))
    return mm_tn(rows_, keep).astype(BF), got


def contract_back(dy, f, w):
    gu = f["gu"]
    F = gu.shape[1] // 2
    da = mm_nt(dy, w["WD"]).astype(BF).astype(F32)
    gate, up = gu[:, :F].astype(F32), gu[:, F:].astype(F32)
    sig = jax.nn.sigmoid(gate)
    return jnp.concatenate([da * up * (sig * (1.0 + gate * (1.0 - sig))), da * (gate * sig)], 1).astype(BF)


def expand_back(dy, dgu, f, w):
    dsec = core_sum(mm_nt(dgu, w["WF"])).astype(BF).astype(F32)
    back, d_mg = norm_back(dsec, f["hidden"], f["r"], w["mg"])
    return dy.astype(F32) + back, d_mg


def project_back(dhid, dpre, dlogits, d_gg, d_mg, m, w):
    dlow = jnp.matmul(dlogits, w["ru"], precision=lax.Precision.HIGHEST)
    dn = mm_nt(dpre, w["WA"]) + mm_nt(dlow, w["rd"])
    dn = core_sum(dn).astype(BF).astype(F32)
    dlow = core_sum(dlow)
    back, d_ag = norm_back(dn, m["x"], m["r"], w["ag"])
    small = dict(
        rd=mm_tn(m["n"], dlow),
        ru=mm_tn(dlogits, m["low"]),
        rb=jnp.sum(dlogits, axis=0),
        gg=d_gg[0],
        ag=d_ag,
        mg=d_mg,
    )
    return dhid + back, small


def body(
    inputs,
    lengths,
    out_grad,
    attn_gain,
    q_weight,
    k_weight,
    v_weight,
    rank_down,
    rank_up,
    rank_bias,
    gate_weight,
    group_gain,
    out_weight,
    mlp_gain,
    ffn_gate,
    ffn_up,
    ffn_down,
):
    size = lax.axis_size("dp")
    meshed = size == 16
    s = lax.axis_index("section")
    me = lax.axis_index("dp")
    at = jnp.stack([me // 4 % 4, (me // 2) % 2, me % 2, s]).astype(jnp.int32)
    first = s == 0
    shape = inputs.shape
    rows = shape[0] * shape[1]
    length, width = shape[2], shape[3]
    tokens = rows * length
    R = q_weight.shape[1]
    K, V, F, W = q_weight.shape[2] // 2, v_weight.shape[2] // 2, ffn_gate.shape[2] // 2, width // 2
    A = 2 * K + 2 * V
    rank = rank_down.shape[2]
    kc, gc = rank_bias.shape[1], group_gain.shape[1]
    ru_at = rank + 4
    links = Links()

    def paced(*values):
        if meshed:
            values = lax.optimization_barrier((values, links.meeting()))[0]
        return values if len(values) > 1 else values[0]

    cuts = cut_columns(
        [
            (q_weight, k_weight, v_weight, gate_weight, out_weight),
            (ffn_gate, ffn_up),
            (ffn_down,),
        ],
        (rank_down, attn_gain, mlp_gain, rank_bias, group_gain, rank_up),
        at,
    )

    def by_layer(pair):
        keep, give = pair
        got = over_core(give)
        return jnp.where(first, keep, got), jnp.where(first, got, keep)

    (keep, give), ff, down = cuts[0], by_layer(cuts[1]), by_layer(cuts[2])
    got = over_core(give)
    table = keep[:, A + W :] + got[:, A + W :]
    keep, got = keep[:, : A + W], got[:, : A + W]
    ao = (jnp.concatenate([jnp.where(first, keep, got), table], 1), jnp.where(first, got, keep))

    def whole(v):
        return lax.all_gather(v, "dp", axis=0, tiled=True)

    def own_rows(v):
        h = v.shape[0] // 2
        keep = lax.dynamic_slice_in_dim(v, s * h, h, 0)
        got = over_core(lax.dynamic_slice_in_dim(v, (1 - s) * h, h, 0))
        return jnp.where(first, jnp.concatenate([keep, got], 1), jnp.concatenate([got, keep], 1))

    if meshed:
        gA = [GatherWide(links, v) for v in ao]
        gF = [GatherWide(links, v) for v in ff]
        gD = [GatherWide(links, down[0]), GatherDown(links, down[1], at)]
    else:
        gA = gF = gD = [Idle(), Idle()]

    def place_ao(layer):
        if not meshed:
            v = whole(ao[layer])
            return v[:, :A], own_rows(v[:, A : A + W]), v[:, A + W :]
        columns = [(0, A, 0, 0), (A, A + W, 1, 0)]
        if ao[layer].shape[1] > A + W:
            columns.append((A + W, ao[layer].shape[1], 3, 0))
        out = place_blocks(gA[layer].parts(), columns, at, split=1)
        keep, give = out[1].reshape(width // 2, W), out[2].reshape(width // 2, W)
        WO = join_columns(keep, over_core(give), at)
        return out[0].reshape(width, A), WO, (out[3].reshape(width, -1) if len(out) > 3 else None)

    def place_ff(layer):
        if not meshed:
            return whole(ff[layer])
        return place_blocks(gF[layer].parts(), [(0, 2 * F, 0, 0)], at)[0].reshape(width, 2 * F)

    def place_down(layer):
        if not meshed:
            return own_rows(whole(down[layer]))
        if layer == 0:
            keep, give = place_blocks(gD[0].parts(), [(0, W, 0, 0)], at, split=0)
            keep, give = keep.reshape(-1, W), give.reshape(-1, W)
        else:
            v = gD[1].all
            h = v.shape[0] // 2
            keep = lax.dynamic_slice_in_dim(v, s * h, h, 0)
            give = lax.dynamic_slice_in_dim(v, (1 - s) * h, h, 0)
        return join_columns(keep, over_core(give), at)

    def unpack(table, layer):
        t = table[:, 64 * layer : 64 * layer + ru_at + rank]
        flat = t[:, rank:ru_at].astype(F32).T
        ru = t.reshape(size, R, -1)[:, :kc, ru_at:].reshape(size * kc, rank).astype(F32)
        rb = flat[2].reshape(size, R)[:, :kc].reshape(1, size * kc)
        return dict(
            rd=t[:, :rank],
            ag=flat[0:1],
            mg=flat[1:2],
            ru=lax.dynamic_slice_in_dim(ru, s * K, K, 0),
            rb=lax.dynamic_slice_in_dim(rb, s * K, K, 1),
            gg=flat[3].reshape(size, R)[:, :gc].reshape(1, size * gc),
        )

    spots = jnp.arange(length)
    mask = (spots[None, :] < lengths.reshape(rows, 1)).astype(F32).reshape(tokens, 1)
    low_mask = mask.astype(BF)
    x0 = inputs.reshape(tokens, width).astype(F32)

    gA[0].along(9), gD[1].around(), gF[0].along(9)
    if meshed:
        gA[1].along_with(gD[0], 3, gA[0].line)
    gA[0].sides(), gA[0].diag()
    WA0, WO0, table = place_ao(0)
    p0, p1 = unpack(table, 0), unpack(table, 1)
    w0 = dict(p0, WA=WA0, WO=WO0)
    gF[0].sides()
    if meshed:
        gF[1].along(2, gA[1].line)
    h0, m0 = mix(project(x0, w0), w0, rows)
    h0, m0, p1 = paced(h0, m0, p1)
    gF[0].diag()
    w0["WF"] = place_ff(0)
    gD[0].sides()
    f0 = paced(expand(h0, w0))
    gD[0].diag()
    if meshed:
        gD[1].along(3, gF[1].line)
    w0["WD"] = place_down(0)
    gA[1].sides()
    y0, f0 = paced(*contract(f0, w0, mask))
    x1 = y0.astype(BF)
    gA[1].diag()
    WA1, WO1, _ = place_ao(1)
    w1 = dict(p1, WA=WA1, WO=WO1)
    gF[1].sides()
    h1, m1 = mix(project(x1.astype(F32), w1), w1, rows)
    h1, m1 = paced(h1, m1)
    gF[1].diag()
    w1["WD"] = place_down(1)
    w1["WF"] = place_ff(1)
    f1 = expand(h1, w1)
    f1 = activate(f1)

    def all_rows(keep, got):
        return jnp.where(first, jnp.concatenate([keep, got], 0), jnp.concatenate([got, keep], 0))

    def scatter(v):
        return lax.psum_scatter(v, "dp", scatter_dimension=0, tiled=True)

    class Sum:
        def __init__(self, v):
            self.sum = scatter(v)

        def along(self, *a):
            pass

        sides = rest = along

    def sum_down(g):
        return ReduceDown(links, all_rows(*g), at) if meshed else Sum(all_rows(*g))

    def sum_ff(second, dgu):
        if meshed:
            return ReduceWide(links, grad_blocks(second, dgu, at))
        return Sum(mm_tn(second, dgu).astype(BF))

    def sum_ao(n, dpre, gO, packed=()):
        extras = gO + packed
        if meshed:
            return ReduceWide(links, grad_blocks(n, dpre, at, extras))
        return Sum(jnp.concatenate((mm_tn(n, dpre).astype(BF), all_rows(*gO)) + packed, 1))

    dy1 = out_grad.reshape(tokens, width) * low_mask
    gD1 = row_grads(f1["act"], dy1, s)
    rD1 = sum_down(gD1)
    dgu = contract_back(dy1, f1, w1)
    rF1 = sum_ff(f1["second"], dgu)
    rF1.sides(), rD1.along(3)
    if meshed:
        dgu = after(dgu, rF1.own)
    dh1, d_mg1 = expand_back(dy1, dgu, f1, w1)
    low = dh1.astype(BF)
    gO1 = row_grads(m1["gated"], low, s)
    back = mixer_bwd(m1["pre"], m1["logits"], w1["gg"], mm_nt(low, w1["WO"]).astype(BF), rows)
    act = after(f1["act"], dh1) if meshed else f1["act"]
    y1 = (f1["hidden"] + core_sum(mm(act, w1["WD"]))) * mask
    y1, dh1, d_mg1, gO1, back = paced(y1, dh1, d_mg1, gO1, back)
    if meshed:
        links.before += [y1]
    rF1.rest()
    rA1 = sum_ao(m1["n"], back[0], gO1)
    dx1, small1 = paced(*project_back(dh1, *back, d_mg1, m1, w1))
    rA1.sides(), rF1.along(3)
    dy0 = dx1.astype(BF) * low_mask
    gD0 = row_grads(f0["act"], dy0, s)
    dgu = contract_back(dy0, f0, w0)
    rF0 = sum_ff(f0["second"], dgu)
    rD0 = sum_down(gD0)
    rD0.along(9)
    dh0, d_mg0 = expand_back(dy0, dgu, f0, w0)
    if meshed:
        (rF0.own, rF0.Sx, rF0.Sy, rF0.Rx, rF0.Ry), dh0, d_mg0 = paced(
            (rF0.own, rF0.Sx, rF0.Sy, rF0.Rx, rF0.Ry), dh0, d_mg0
        )
    rA1.rest()
    low = dh0.astype(BF)
    gO0 = row_grads(m0["gated"], low, s)
    dgated, gO0, dh0 = paced(mm_nt(low, w0["WO"]).astype(BF), gO0, dh0)
    if meshed:
        rA1.own = after(rA1.own, rF0.own)
    rF0.sides(), rA1.along(9)
    back = paced(mixer_bwd(m0["pre"], m0["logits"], w0["gg"], dgated, rows))
    rF0.rest()
    dx0, small0 = project_back(dh0, *back, d_mg0, m0, w0)
    dpre = back[0]
    mine = {k: jnp.where(first, small0[k], small1[k]) for k in small0}
    other = {k: over_core(jnp.where(first, small1[k], small0[k])) for k in ("ru", "rb", "gg")}
    ru = all_rows(mine["ru"], other["ru"])
    rb = all_rows(mine["rb"], other["rb"])

    def tall_blocks(v):
        v = v.reshape(size, v.shape[0] // size, -1)
        return jnp.pad(v, ((0, 0), (0, R - v.shape[1]), (0, 0))).reshape(size * R, -1)

    def long_blocks(v):
        v = v.reshape(size, -1)
        return jnp.pad(v, ((0, 0), (0, R - v.shape[1]))).reshape(size * R)

    flat = jnp.stack([mine["ag"], mine["mg"], long_blocks(rb), long_blocks(mine["gg"] + other["gg"])]).T
    packed = jnp.concatenate([mine["rd"], flat, tall_blocks(ru)], 1)
    packed = jnp.pad(packed, ((0, 0), (0, 128 - packed.shape[1]))).astype(BF)

    rA0 = sum_ao(m0["n"], dpre, gO0, (packed,))
    rA0.sides(), rF0.along(9)
    if meshed:
        links.before += [rA1.sum]
    rA0.rest()
    rA0.along(9)
    if meshed:
        links.before += [rF0.sum]
        around(links, (rD1, rD0))

    input_out = jnp.where(first, dx0, dx1).reshape((1,) + shape)
    layer_out = jnp.where(first, x1, y1.astype(BF)).reshape((1,) + shape)

    def join(a, b, widths):
        return finish(a, b, over_core(jnp.where(first, b, a[:, : b.shape[1]])), widths, at)

    dD = join(rD0.sum, rD1.sum, (W,))[0]
    dFg, dFu = join(rF0.sum, rF1.sum, (F, F))
    dq, dk, dv, dg, dO = join(rA0.sum, rA1.sum, (K, K, V, V, W))
    t = rA0.sum[:, A + W :].astype(F32)
    return (
        layer_out,
        input_out,
        t[:, rank][None],
        dq,
        dk,
        dv,
        t[:, :rank][None],
        t[:kc, ru_at : ru_at + rank].T[None],
        t[:kc, rank + 2][None],
        dg,
        t[:gc, rank + 3][None],
        dO,
        t[:, rank + 1][None],
        dFg,
        dFu,
        dD,
    )


def solution(mesh):
    rows3 = P("section", "dp", None)
    one = P("section", "dp")
    return jax.shard_map(
        body,
        mesh=mesh,
        in_specs=(
            P(None, "dp", None, None),
            P(None, "dp"),
            P(None, "dp", None, None),
            one,
            rows3,
            rows3,
            rows3,
            rows3,
            P("section", None, "dp"),
            one,
            rows3,
            one,
            rows3,
            one,
            rows3,
            rows3,
            rows3,
        ),
        out_specs=(
            P("section", None, "dp", None, None),
            P("section", None, "dp", None, None),
            one,
            rows3,
            rows3,
            rows3,
            rows3,
            P("section", None, "dp"),
            one,
            rows3,
            one,
            rows3,
            one,
            rows3,
            rows3,
            rows3,
        ),
        check_vma=False,
    )
```
